32 devices in a mesh: depth: 2 (over core), row: 2 (over x), col: 8 (over z, y).
Axes of the slice: x: 2, y: 2, z: 4, core: 2. Of those that a mesh axis runs over, the one named last changes fastest.
Arguments:
- probe: float32 [2, 256, 256], replicated, may hold values from -6 to 6
- object_re: bfloat16 [2, 1024, 8192], P('depth', 'row', 'col'), may hold values from 0.099609375 to 1.8984375
- object_im: bfloat16 [2, 1024, 8192], P('depth', 'row', 'col'), may hold values from -1.796875 to 1.796875
- phases: float32 [256, 256], replicated, may hold values from -3.140625 to 3.140625
- centres: int32 [2, 8, 4, 2, 2], P('row', 'col'), may hold values from 0 to 1023, as said below
- occupied: int32 [2, 8, 4], P('row', 'col'), may hold values from 0 to 2, as said below
- measured: float32 [2, 8, 4, 2, 256, 256], P('row', 'col'), may hold values from 0 to 4
Outputs:
- object_grad: float32 [2, 2, 1024, 8192], P(None, 'depth', 'row', 'col')
- probe_grad: float32 [2, 256, 256], P(None, 'depth')
The draws below stay inside these ranges and needn't reach their ends.
Inputs may be any that keep to these rules, and one draw needn't show every extreme that they name: `centres`: the 256 x 256 window around every centre, starting 256 // 2 pixels before it in both directions, lies inside the field of view. `occupied`: in every draw some tile has all 2 slots used in some micro-batch.
All inputs are finite; a program needn't handle non-finite values.
Results may differ from the reference program's by a relative error of at most 0.006.
Values may be sent and summed in bfloat16 or wider, within the bound.
No kernel may reach another device: no remote copies, remote signals or barrier semaphores. Data moves between devices by JAX's collectives and lax.ppermute only.
A program may use at most 192 MiB of HBM per device.

```python
import jax
import jax.numpy as jnp
from jax import lax

P_SIZE = 256
TR = 512
TC = 1024
MB = 4
CAP = 2
SLICES = 2
GRID_R = 2
GRID_C = 8
NY = 1024
NX = 8192


def draw_centres(key, part):
    half_size = P_SIZE // 2
    grid_shape = (GRID_R, GRID_C, MB, CAP)
    row_ids = jnp.arange(GRID_R, dtype=jnp.int32).reshape(GRID_R, 1, 1, 1)
    col_ids = jnp.arange(GRID_C, dtype=jnp.int32).reshape(1, GRID_C, 1, 1)
    low_rows = jnp.broadcast_to(jnp.where(row_ids == 0, half_size, 0), grid_shape)
    high_rows = jnp.broadcast_to(jnp.where(row_ids == GRID_R - 1, TR - half_size, TR), grid_shape)
    low_cols = jnp.broadcast_to(jnp.where(col_ids == 0, half_size, 0), grid_shape)
    high_cols = jnp.broadcast_to(jnp.where(col_ids == GRID_C - 1, TC - half_size, TC), grid_shape)
    key_rows, key_cols = jax.random.split(jax.random.fold_in(key, 11))
    centre_rows = jax.random.randint(key_rows, grid_shape, low_rows, high_rows, dtype=jnp.int32)
    centre_cols = jax.random.randint(key_cols, grid_shape, low_cols, high_cols, dtype=jnp.int32)
    return jnp.stack([centre_rows, centre_cols], axis=-1)


def draw_occupied(key, part):
    key_counts, key_pick = jax.random.split(jax.random.fold_in(key, 23))
    counts = jax.random.randint(key_counts, (GRID_R, GRID_C, MB), 0, CAP + 1, dtype=jnp.int32)
    chosen = jax.random.randint(key_pick, (), 0, GRID_R * GRID_C * MB, dtype=jnp.int32)
    flattened = counts.reshape(-1)
    positions = jnp.arange(GRID_R * GRID_C * MB, dtype=jnp.int32)
    flattened = jnp.where(positions == chosen, CAP, flattened)
    return flattened.reshape(GRID_R, GRID_C, MB)


def steps_of(own_key, shape, pieces, least, high):
    def one(dim, blocks):
        steps = jax.random.uniform(jax.random.fold_in(jax.random.fold_in(own_key, 6), dim), (blocks,), jnp.float32, least / len(pieces), high / len(pieces))
        return jnp.repeat(jnp.exp(steps), shape[dim] // blocks).reshape((-1,) + (1,) * (len(shape) - dim - 1))

    loudness = one(*pieces[0])
    for cut in pieces[1:]:
        loudness = loudness * one(*cut)
    return loudness


def noise(own_key, shape, scale, reach, pieces=(), kind=jnp.bfloat16):
    level = steps_of(own_key, shape, pieces, -0.22, 0.18) if pieces else 1.0
    result = jax.random.normal(own_key, shape, jnp.float32) * scale * level
    return jnp.minimum(jnp.maximum(result, -reach), reach).astype(kind)


def setup_inputs(seed: int = 0) -> dict:
    streams_of = jax.random.split(jax.random.key(seed), 8)
    return {
        "probe": noise(streams_of[0], (2, P_SIZE, P_SIZE), 1.0, 6.0, (), jnp.float32),
        "object_re": jnp.clip(1.0 + 0.18 * jax.random.normal(streams_of[1], (SLICES, NY, NX), jnp.float32), 0.099609375, 1.8984375).astype(jnp.bfloat16),
        "object_im": noise(streams_of[2], (SLICES, NY, NX), 0.3, 1.796875, ((0, 2), (1, 2), (2, 8))),
        "phases": jnp.clip(jax.random.uniform(streams_of[3], (P_SIZE, P_SIZE), jnp.float32, -3.140625, 3.140625), -3.140625, 3.140625),
        "centres": draw_centres(jax.random.fold_in(streams_of[7], 71), 0),
        "occupied": draw_occupied(jax.random.fold_in(streams_of[7], 71), 0),
        "measured": jnp.clip(4.0 * jax.random.uniform(streams_of[6], (GRID_R, GRID_C, MB, CAP, P_SIZE, P_SIZE), jnp.float32) ** steps_of(streams_of[6], (GRID_R, GRID_C, MB, CAP, P_SIZE, P_SIZE), ((0, 2), (1, 8)), -0.2, 0.2), 0.0, 4.0),
    }


def rounded(value):
    return lax.optimization_barrier(value.astype(jnp.bfloat16)).astype(value.dtype)


def keep_bf16(value):
    return lax.complex(rounded(jnp.real(value)), rounded(jnp.imag(value)))


def forward_ft(value):
    return jnp.fft.fft2(value, norm="ortho")


def inverse_ft(value):
    return jnp.fft.ifft2(value, norm="ortho")


def reference(probe, object_re, object_im, phases, centres, occupied, measured):
    half_size = P_SIZE // 2
    object_c = lax.complex(object_re.astype(jnp.float32), object_im.astype(jnp.float32))
    kernel = lax.complex(jnp.cos(phases), jnp.sin(phases))
    launch = lax.complex(probe[0], probe[1])
    row_base = (jnp.arange(GRID_R, dtype=jnp.int32) * TR)[:, None, None, None]
    col_base = (jnp.arange(GRID_C, dtype=jnp.int32) * TC)[None, :, None, None]
    top_row = (centres[..., 0] + row_base - half_size).astype(jnp.int32).reshape(-1)
    left_col = (centres[..., 1] + col_base - half_size).astype(jnp.int32).reshape(-1)
    slot_ids = jnp.arange(CAP, dtype=jnp.int32)[None, None, None, :]
    live_all = (slot_ids < occupied[..., None]).astype(jnp.float32).reshape(-1)
    frames = measured.reshape(-1, P_SIZE, P_SIZE)

    def visit_one(carry, record):
        gradient, probe_sum = carry
        top_px, left_px, live_w, measure = record
        windows = []
        for slice_no in range(SLICES):
            anchor = (jnp.asarray(slice_no, jnp.int32), top_px, left_px)
            windows.append(lax.dynamic_slice(object_c, anchor, (1, P_SIZE, P_SIZE))[0])
        incident = [launch]
        for slice_no in range(SLICES - 1):
            incident.append(keep_bf16(inverse_ft(kernel * forward_ft(incident[slice_no] * windows[slice_no]))))
        farfield = forward_ft(incident[-1] * windows[-1])
        misfit = jnp.real(farfield) ** 2 + jnp.imag(farfield) ** 2 - measure
        adjoint = inverse_ft(misfit * farfield)
        for slice_no in range(SLICES - 1, -1, -1):
            anchor = (jnp.asarray(slice_no, jnp.int32), top_px, left_px)
            contrib = live_w * jnp.conj(incident[slice_no]) * adjoint
            previous = lax.dynamic_slice(gradient, anchor, (1, P_SIZE, P_SIZE))
            gradient = lax.dynamic_update_slice(gradient, previous + contrib[None], anchor)
            pulled = jnp.conj(windows[slice_no]) * adjoint
            if slice_no > 0:
                adjoint = keep_bf16(inverse_ft(jnp.conj(kernel) * forward_ft(pulled)))
            else:
                probe_sum = probe_sum + live_w * pulled
        return (gradient, probe_sum), None

    start = (jnp.zeros(object_c.shape, object_c.dtype), jnp.zeros(launch.shape, launch.dtype))
    (gradient, probe_sum), _ = lax.scan(visit_one, start, (top_row, left_col, live_all, frames))
    object_grad = jnp.stack([jnp.real(gradient), jnp.imag(gradient)])
    probe_grad = jnp.stack([jnp.real(probe_sum), jnp.imag(probe_sum)])
    return object_grad, probe_grad
```

```python
import functools

import jax
import jax.numpy as jnp
import numpy as np
from jax import lax
from jax.experimental import pallas as pl
from jax.experimental.pallas import tpu as pltpu
from jax.sharding import PartitionSpec as P

f32 = jnp.float32
bf16 = jnp.bfloat16
ROWS = 16
LANES = 128
HBM = pl.BlockSpec(memory_space=pl.ANY)
SMEM = pl.BlockSpec(memory_space=pltpu.SMEM)
LIMIT = 56 * 1024 * 1024


def dft_tables(size):
    half = size // 2
    rows = np.arange(half)[:, None]
    cols = np.arange(half)[None, :]

    def packed(turns):
        angle = -2.0 * np.pi * (turns % size) / size
        re, im = np.cos(angle) / np.sqrt(size), np.sin(angle) / np.sqrt(size)
        return np.block([[re, im], [-im, re]])

    even, odd = packed(rows * 2 * cols), packed(rows * (2 * cols + 1))
    full = np.stack([even, odd, even.T, odd.T]).astype(np.float32)
    high = full.astype(jnp.bfloat16)
    low = (full - high.astype(np.float32)).astype(jnp.bfloat16)
    return np.stack([high, low], axis=1)


def sorting_table(size):
    order = np.concatenate([np.arange(0, size, 2), np.arange(1, size, 2)])
    table = np.zeros((size, size), np.float32)
    table[order, np.arange(size)] = 1.0
    return table.astype(jnp.bfloat16)


def split(x):
    high = x.astype(bf16)
    return high, (x - high.astype(f32)).astype(bf16)


def dot3(left, right):
    lhs = jnp.concatenate([left[0], left[0], left[1]], axis=1)
    rhs = jnp.concatenate([right[0], right[1], right[0]], axis=0)
    return jnp.dot(lhs, rhs, preferred_element_type=f32)


def rows_of(*parts):
    return jnp.concatenate(parts, axis=0)


def cols_of(*parts):
    return jnp.concatenate(parts, axis=1)


def prep_kernel(places, order_t, probe, *refs):
    step = pl.program_id(0)
    size = probe.shape[-1]
    half = size // 2
    blocks = size // LANES
    phases, frames = refs[:blocks], refs[blocks : 2 * blocks]
    kern, sorted_frames, waves = refs[2 * blocks :]

    def halved(parts, at):
        ids = [(at, pl.ds(start, half, stride=2), slice(None)) for start in range(2)]
        return rows_of(*(cols_of(*(part[i] for part in parts)) for i in ids))

    def in_order(rows):
        first, rest = split(rows)
        second, third = split(rows - first.astype(f32))
        table = order_t[...]
        return jnp.dot(
            cols_of(first, second, third), rows_of(table, table, table), preferred_element_type=f32
        )

    @pl.when(step == 0)
    def _():
        angles = in_order(halved(phases, 0))
        kern[0] = jnp.cos(angles)
        kern[1] = jnp.sin(angles)

    sorted_frames[0] = in_order(halved(frames, 0))
    down = places[2 * step] % ROWS
    across = places[2 * step + 1] % LANES
    for plane in range(2):
        moved = pltpu.roll(probe[plane], across, axis=1)
        waves[0, plane] = pltpu.roll(moved, down, axis=0)


def prepare(places, probe, phases, frames):
    count, size = frames.shape[0], phases.shape[-1]
    blocks = size // LANES
    full = lambda *shape: pl.BlockSpec(shape, lambda i: (0,) * len(shape))
    return pl.pallas_call(
        prep_kernel,
        grid=(count,),
        in_specs=[
            SMEM,
            full(size, size),
            full(2, size, size),
            *(pl.BlockSpec((1, size, LANES), lambda i, b=b: (0, 0, b)) for b in range(blocks)),
            *(pl.BlockSpec((1, size, LANES), lambda i, b=b: (i, 0, b)) for b in range(blocks)),
        ],
        out_specs=[
            full(2, size, size),
            pl.BlockSpec((1, size, size), lambda i: (i, 0, 0)),
            pl.BlockSpec((1, 2, size, size), lambda i: (i, 0, 0, 0)),
        ],
        out_shape=[
            jax.ShapeDtypeStruct((2, size, size), f32),
            jax.ShapeDtypeStruct((count, size, size), f32),
            jax.ShapeDtypeStruct((count, 2, size, size), f32),
        ],
        compiler_params=pltpu.CompilerParams(vmem_limit_bytes=LIMIT),
        cost_estimate=pl.CostEstimate(
            flops=2 * (count + 1) * 3 * size**3,
            bytes_accessed=4 * size * size * (4 * count + 6),
            transcendentals=2 * size * size,
        ),
        name="prepare",
    )(
        places,
        jnp.asarray(sorting_table(size)),
        probe,
        *[phases[None]] * blocks,
        *[frames] * blocks,
    )


def spot(places, at, size):
    row, col = places[2 * at], places[2 * at + 1]
    down, across = row % ROWS, col % LANES
    top = pl.multiple_of(row - down, ROWS)
    left = pl.multiple_of(col - across, LANES)
    return down, across, pl.ds(top, size + ROWS), pl.ds(left, size + LANES)


def gather_kernel(
    spots, edges, half, places, offsets, tile_re, tile_im, *rest
):
    strips, (mine, other, padded, sems) = rest[:-4], rest[-4:]
    tile_rows, tile_cols = tile_re.shape[1:]
    size = mine.shape[-1]
    body = (pl.ds(half, tile_rows), pl.ds(half, tile_cols))
    copies = []

    def bring(source, target):
        copies.append(pltpu.make_async_copy(source, target, sems.at[len(copies)]))
        copies[-1].start()

    bring(tile_re.at[0], padded.at[(0,) + body])
    bring(tile_im.at[0], padded.at[(1,) + body])
    columns = {-1: pl.ds(0, half), 0: body[1], 1: pl.ds(half + tile_cols, half)}
    for (side, across), strip in zip(edges, strips):
        if side is None:
            down = body[0]
        else:
            down = pl.ds(pl.multiple_of(offsets[side], half), half)
        bring(strip, padded.at[:, down, columns[across]])
    for copy in copies:
        copy.wait()

    sections = 2
    lane = lax.broadcasted_iota(jnp.int32, (size + ROWS, LANES), 1)
    row = lax.broadcasted_iota(jnp.int32, (ROWS, size), 0)
    here = offsets[len(offsets_names(edges))]

    def cut(at, target, place):
        down, across, tall, wide = spot(places, at, size)
        for plane in range(2):
            block = padded[plane, tall, wide].astype(f32)
            first = jnp.where(lane < across, block[:, size:], block[:, :LANES])
            block = cols_of(first, block[:, LANES:size])
            first = jnp.where(row < down, block[size:], block[:ROWS])
            target[place, plane] = rows_of(first, block[ROWS:size]).astype(bf16)

    def one(place, carry):
        cut(sections * place + here, mine, place)
        cut(sections * place + 1 - here, other, place)
        return carry

    lax.fori_loop(0, spots // sections, one, 0)


def offsets_names(edges):
    return sorted({side for side, _ in edges if side is not None})


def gather(places, offsets, tile_re, tile_im, edges, strips, size):
    half = size // 2
    spots = places.shape[0] // 2
    tile_rows, tile_cols = tile_re.shape[1:]
    shape = jax.ShapeDtypeStruct((spots // 2, 2, size, size), bf16)
    vmem = pl.BlockSpec(memory_space=pltpu.VMEM)
    return pl.pallas_call(
        functools.partial(gather_kernel, spots, edges, half),
        in_specs=[SMEM, SMEM] + [HBM] * (2 + len(strips)),
        out_specs=[vmem, vmem],
        out_shape=[shape, shape],
        scratch_shapes=[
            pltpu.VMEM((2, tile_rows + 2 * half, tile_cols + 2 * half), bf16),
            pltpu.SemaphoreType.DMA((2 + len(strips),)),
        ],
        compiler_params=pltpu.CompilerParams(vmem_limit_bytes=LIMIT),
        name="gather",
    )(places, offsets, tile_re, tile_im, *strips)


def chain_kernel(
    group, places, live, here, tables, kern, mine, theirs, frames, waves,
    keep, send, pulled, windows, middle, terms, sems,
):
    step = pl.program_id(0)
    steps = pl.num_programs(0)
    size = kern.shape[-1]
    half = size // 2
    me = here[0]

    def fetch(at, which):
        source, slot = ((mine, me), (theirs, 1 - me))[which]
        rows = pl.ds(at * group, group)
        return pltpu.make_async_copy(
            source.at[rows], windows.at[at, slot], sems.at[2 * at + which]
        )

    @pl.when(step == 0)
    def _():
        for at in range(windows.shape[0]):
            fetch(at, 0).start()
            fetch(at, 1).start()
        pulled[...] = jnp.zeros_like(pulled)

    fetch(step, 0).wait()
    fetch(step, 1).wait()

    def table(which):
        return tables[which, 0], tables[which, 1]

    def forward(re, im):
        halves = []
        for sign, which in ((1, 2), (-1, 3)):
            if sign > 0:
                part = rows_of(re[:half] + re[half:], im[:half] + im[half:])
            else:
                part = rows_of(re[:half] - re[half:], im[:half] - im[half:])
            halves.append(dot3(table(which), split(part)))
        outs = []
        for sign, which in ((1, 0), (-1, 1)):
            parts = []
            for out in halves:
                re, im = out[:half], out[half:]
                if sign > 0:
                    parts.append(cols_of(re[:, :half] + re[:, half:], im[:, :half] + im[:, half:]))
                else:
                    parts.append(cols_of(re[:, :half] - re[:, half:], im[:, :half] - im[:, half:]))
            outs.append(dot3(split(rows_of(*parts)), table(which)))
        return outs

    def inverse(even, odd):
        first = dot3(split(even), table(2))
        second = dot3(split(odd), table(3))
        plus, minus = first + second, first - second
        re = cols_of(plus[:, :half], minus[:, :half])
        im = cols_of(plus[:, half:], minus[:, half:])
        first = dot3(table(0), split(rows_of(re[:half], im[:half])))
        second = dot3(table(1), split(rows_of(re[half:], im[half:])))
        plus, minus = first + second, first - second
        return rows_of(plus[:half], minus[:half]), rows_of(plus[half:], minus[half:])

    def propagate(re, im, sign):
        outs = []
        for at, part in enumerate(forward(re, im)):
            cols = slice(at * half, (at + 1) * half)
            kre, kim = kern[0, :, cols], kern[1, :, cols] * sign
            re, im = part[:, :half], part[:, half:]
            outs.append(cols_of(re * kre - im * kim, re * kim + im * kre))
        return inverse(*outs)

    def rounded(x):
        return x.astype(bf16).astype(f32)

    def window(slot, at):
        return windows[step, slot, at, 0].astype(f32), windows[step, slot, at, 1].astype(f32)

    for at in range(group):
        wre, wim = window(0, at)
        pre, pim = waves[at, 0], waves[at, 1]
        re, im = propagate(pre * wre - pim * wim, pre * wim + pim * wre, 1.0)
        middle[at, 0] = re.astype(bf16)
        middle[at, 1] = im.astype(bf16)

    for at in range(group):
        wre, wim = window(1, at)
        pre, pim = middle[at, 0].astype(f32), middle[at, 1].astype(f32)
        back = []
        for k, part in enumerate(forward(pre * wre - pim * wim, pre * wim + pim * wre)):
            re, im = part[:, :half], part[:, half:]
            misfit = re * re + im * im - frames[at, :, k * half : (k + 1) * half]
            back.append(cols_of(re * misfit, im * misfit))
        cre, cim = inverse(*back)
        pre, pim = middle[at, 0].astype(f32), middle[at, 1].astype(f32)
        terms[1, at, 0] = pre * cre + pim * cim
        terms[1, at, 1] = pre * cim - pim * cre
        wre, wim = window(1, at)
        re, im = propagate(wre * cre + wim * cim, wre * cim - wim * cre, -1.0)
        cre, cim = rounded(re), rounded(im)
        pre, pim = waves[at, 0], waves[at, 1]
        terms[0, at, 0] = pre * cre + pim * cim
        terms[0, at, 1] = pre * cim - pim * cre
        wre, wim = window(0, at)
        spot_at = step * group + at
        up = (size - places[2 * spot_at] % ROWS) % size
        back_by = (size - places[2 * spot_at + 1] % LANES) % size
        weight = live[spot_at].astype(f32)
        for plane, value in enumerate((wre * cre + wim * cim, wre * cim - wim * cre)):
            value = pltpu.roll(pltpu.roll(value * weight, back_by, axis=1), up, axis=0)
            pulled[plane] += value

    keep[...] = terms[me]
    send[...] = terms[1 - me].astype(bf16)


def chain(places, live, here, kern, mine, theirs, frames, waves, group):
    count, size = frames.shape[0], frames.shape[-1]
    full = lambda *shape: pl.BlockSpec(shape, lambda i: (0,) * len(shape))
    block = pl.BlockSpec((group, 2, size, size), lambda i: (i, 0, 0, 0))
    return pl.pallas_call(
        functools.partial(chain_kernel, group),
        grid=(count // group,),
        in_specs=[
            SMEM,
            SMEM,
            SMEM,
            full(4, 2, size, size),
            full(2, size, size),
            HBM,
            HBM,
            pl.BlockSpec((group, size, size), lambda i: (i, 0, 0)),
            block,
        ],
        out_specs=[block, block, full(2, size, size)],
        out_shape=[
            jax.ShapeDtypeStruct((count, 2, size, size), f32),
            jax.ShapeDtypeStruct((count, 2, size, size), bf16),
            jax.ShapeDtypeStruct((2, size, size), f32),
        ],
        scratch_shapes=[
            pltpu.VMEM((count // group, 2, group, 2, size, size), bf16),
            pltpu.VMEM((group, 2, size, size), bf16),
            pltpu.VMEM((2, group, 2, size, size), f32),
            pltpu.SemaphoreType.DMA((2 * (count // group),)),
        ],
        compiler_params=pltpu.CompilerParams(vmem_limit_bytes=LIMIT),
        name="chain",
    )(places, live, here, jnp.asarray(dft_tables(size)), kern, mine, theirs, frames, waves)


def scatter_kernel(
    spots, edges, half, places, live, offsets, kept, arrived, tile, *rest
):
    strips, (total, sems) = rest[:-2], rest[-2:]
    size = kept.shape[-1]
    tile_rows, tile_cols = tile.shape[1:]
    sections = 2
    here = offsets[len(offsets_names(edges))]
    total[...] = jnp.zeros_like(total)
    lane = lax.broadcasted_iota(jnp.int32, (size, LANES), 1)
    row = lax.broadcasted_iota(jnp.int32, (ROWS, size + LANES), 0)

    def add(at, source, place):
        down, across, tall, wide = spot(places, at, size)

        @pl.when(live[at] > 0)
        def _():
            for plane in range(2):
                value = source[place, plane].astype(f32)
                first = value[:, :LANES]
                inside = lane >= across
                value = cols_of(
                    jnp.where(inside, first, 0.0), value[:, LANES:], jnp.where(inside, 0.0, first)
                )
                first = value[:ROWS]
                inside = row >= down
                value = rows_of(
                    jnp.where(inside, first, 0.0), value[ROWS:], jnp.where(inside, 0.0, first)
                )
                total[plane, tall, wide] += value

    def one(place, carry):
        add(sections * place + here, kept, place)
        add(sections * place + 1 - here, arrived, place)
        return carry

    lax.fori_loop(0, spots // sections, one, 0)
    body = (pl.ds(half, tile_rows), pl.ds(half, tile_cols))
    copy = pltpu.make_async_copy(total.at[(slice(None),) + body], tile, sems.at[0])
    copy.start()
    columns = {-1: pl.ds(0, half), 0: body[1], 1: pl.ds(half + tile_cols, half)}
    for (side, across), strip in zip(edges, strips):
        if side is None:
            rows = body[0]
        else:
            rows = pl.ds(pl.multiple_of(offsets[side], half), half)
        for plane in range(2):
            strip[plane] = total[plane, rows, columns[across]].astype(bf16)
    copy.wait()


def scatter(places, live, offsets, kept, arrived, edges, tile_rows, tile_cols):
    size = kept.shape[-1]
    half = size // 2
    spots = places.shape[0] // 2
    vmem = pl.BlockSpec(memory_space=pltpu.VMEM)
    shapes = [
        jax.ShapeDtypeStruct(
            (2, tile_rows if side is None else half, half if across else tile_cols), bf16
        )
        for side, across in edges
    ]
    return pl.pallas_call(
        functools.partial(scatter_kernel, spots, edges, half),
        in_specs=[SMEM, SMEM, SMEM, vmem, vmem],
        out_specs=[HBM] + [vmem] * len(edges),
        out_shape=[jax.ShapeDtypeStruct((2, tile_rows, tile_cols), f32)] + shapes,
        scratch_shapes=[
            pltpu.VMEM((2, tile_rows + 2 * half, tile_cols + 2 * half), f32),
            pltpu.SemaphoreType.DMA((1,)),
        ],
        compiler_params=pltpu.CompilerParams(vmem_limit_bytes=LIMIT),
        name="scatter",
    )(places, live, offsets, kept, arrived)


def border_kernel(edges, half, sides, offsets, tile_in, *rest):
    strips, (tile, total, in_sem, out_sem) = rest[:-4], rest[-4:]
    tile_rows, tile_cols = tile.shape[1:]
    copy = pltpu.make_async_copy(tile_in, total, in_sem)
    copy.start()
    copy.wait()
    columns = {
        -1: pl.ds(0, half),
        0: pl.ds(0, tile_cols),
        1: pl.ds(tile_cols - half, half),
    }
    for (side, across), strip in zip(edges, strips):
        if side is None:
            rows = pl.ds(0, tile_rows)
        else:
            rows = pl.ds(pl.multiple_of(offsets[side], half), half)
        for plane in range(2):
            total[plane, rows, columns[across]] += strip[plane].astype(f32)
    copy = pltpu.make_async_copy(total, tile, out_sem)
    copy.start()
    copy.wait()


def add_borders(offsets, tile, edges, strips, half):
    vmem = pl.BlockSpec(memory_space=pltpu.VMEM)
    return pl.pallas_call(
        functools.partial(border_kernel, edges, half, None),
        in_specs=[SMEM, HBM] + [vmem] * len(strips),
        out_specs=HBM,
        out_shape=jax.ShapeDtypeStruct(tile.shape, f32),
        scratch_shapes=[
            pltpu.VMEM(tile.shape, f32),
            pltpu.SemaphoreType.DMA,
            pltpu.SemaphoreType.DMA,
        ],
        compiler_params=pltpu.CompilerParams(vmem_limit_bytes=LIMIT),
        name="borders",
    )(offsets, tile, *strips)


def routes(edges, sides, rows, cols):
    result = []
    for side, across in edges:
        pairs = []
        for r in range(rows):
            if side is None:
                to_row = r
            elif rows == 2:
                to_row = 1 - r
            else:
                to_row = r + sides[side]
            for c in range(cols):
                to_col = c + across
                if 0 <= to_row < rows and 0 <= to_col < cols:
                    pairs.append((r * cols + c, to_row * cols + to_col))
        result.append(pairs)
    return result


def summed(block, axis):
    size = lax.axis_size(axis)
    if size & (size - 1):
        return lax.psum(block, axis)
    step = 1
    while step < size:
        block = block + lax.ppermute(block, axis, [(i, i ^ step) for i in range(size)])
        step *= 2
    return block


def shards(probe, object_re, object_im, phases, centres, occupied, measured):
    size = probe.shape[1]
    half = size // 2
    rows, cols = lax.axis_size("row"), lax.axis_size("col")
    sections = lax.axis_size("depth")
    assert sections == 2 and object_re.shape[0] == 1
    here = lax.axis_index("depth").astype(jnp.int32)
    row_at = lax.axis_index("row").astype(jnp.int32)
    tile_rows, tile_cols = object_re.shape[1:]
    batches, slots = centres.shape[2:4]
    spots = batches * slots
    count = spots // sections

    places = centres.reshape(2 * spots)
    slot_ids = jnp.arange(slots, dtype=jnp.int32)
    live = (slot_ids[None, :] < occupied[0, 0][:, None]).astype(jnp.int32)
    my_places = lax.dynamic_index_in_dim(
        centres.reshape(count, sections, 2), here, 1, False
    ).reshape(2 * count)
    my_live = lax.dynamic_index_in_dim(live.reshape(count, sections), here, 1, False)
    live = live.reshape(spots)
    frames = lax.dynamic_index_in_dim(
        measured.reshape(count, sections, size, size), here, 1, False
    )

    if rows == 1:
        sides, from_rows, pad_rows, fold_rows = [], [], [], []
    elif rows == 2:
        sides = [0]
        from_rows = [jnp.where(row_at == 0, tile_rows - half, 0)]
        pad_rows = [jnp.where(row_at == 0, tile_rows + half, 0)]
        fold_rows = from_rows
    else:
        sides = [1, -1]
        from_rows = [jnp.int32(tile_rows - half), jnp.int32(0)]
        pad_rows = [jnp.int32(0), jnp.int32(tile_rows + half)]
        fold_rows = [jnp.int32(0), jnp.int32(tile_rows - half)]
    edges = [(side, 0) for side in range(len(sides))]
    edges += [(None, 1), (None, -1)]
    edges += [(side, across) for side in range(len(sides)) for across in (1, -1)]
    paths = routes(edges, sides, rows, cols)
    both = ("row", "col")

    planes = jnp.stack([object_re[0], object_im[0]])
    strips = []
    for (side, across), path in zip(edges, paths):
        wide = tile_cols if across == 0 else half
        left = tile_cols - half if across == 1 else 0
        tall = tile_rows if side is None else half
        top = 0 if side is None else from_rows[side]
        strip = lax.dynamic_slice(planes, (0, top, left), (2, tall, wide))
        strips.append(lax.ppermute(strip, both, path))
    landed = [(side, -across) for side, across in edges]
    pads = jnp.stack(pad_rows + [here]).astype(jnp.int32)
    kern, sorted_frames, waves = prepare(my_places, probe, phases, frames)
    mine, other = gather(places, pads, object_re, object_im, landed, strips, size)
    across_depth = [(i, 1 - i) for i in range(sections)]
    theirs = lax.ppermute(other, "depth", across_depth)
    keep, send, pulled = chain(
        my_places, my_live, here.reshape(1), kern, mine, theirs, sorted_frames, waves, 2
    )
    arrived = lax.ppermute(send, "depth", across_depth)

    share = size // sections
    kept_rows = lax.dynamic_slice_in_dim(pulled, here * share, share, 1)
    sent_rows = lax.dynamic_slice_in_dim(pulled, (1 - here) * share, share, 1)
    probe_part = kept_rows + lax.ppermute(
        sent_rows.astype(bf16), "depth", across_depth
    ).astype(f32)

    if rows == 2:
        out_rows = pad_rows
    else:
        out_rows = pad_rows[::-1]
    outs = jnp.stack(out_rows + [here]).astype(jnp.int32)
    tile, *own = scatter(places, live, outs, keep, arrived, edges, tile_rows, tile_cols)
    added = [lax.ppermute(strip, both, path) for strip, path in zip(own, paths)]
    folds = jnp.stack(fold_rows + [here]).astype(jnp.int32)
    gradient = add_borders(folds, tile, landed, added, half)
    probe_share = summed(summed(probe_part, "row"), "col")
    return (gradient[:, None], probe_share)


def solution(mesh):
    in_specs = (
        P(),
        P("depth", "row", "col"),
        P("depth", "row", "col"),
        P(),
        P("row", "col", None, None, None),
        P("row", "col", None),
        P("row", "col", None, None, None, None),
    )
    out_specs = (P(None, "depth", "row", "col"), P(None, "depth", None))
    return jax.shard_map(shards, mesh=mesh, in_specs=in_specs, out_specs=out_specs, check_vma=False)
```

```python
import functools

import jax
import jax.numpy as jnp
import numpy as np
from jax import lax
from jax.experimental import pallas as pl
from jax.experimental.pallas import tpu as pltpu
from jax.sharding import PartitionSpec as P

f32 = jnp.float32
bf16 = jnp.bfloat16
ROWS = 16
LANES = 128
HBM = pl.BlockSpec(memory_space=pl.ANY)
SMEM = pl.BlockSpec(memory_space=pltpu.SMEM)
MIB = 1024 * 1024


def dft_tables(size):
    half = size // 2
    rows = np.arange(half)[:, None]
    cols = np.arange(half)[None, :]

    def packed(turns):
        angle = -2.0 * np.pi * (turns % size) / size
        re, im = np.cos(angle) / np.sqrt(size), np.sin(angle) / np.sqrt(size)
        return np.block([[re, im], [-im, re]])

    even, odd = packed(rows * 2 * cols), packed(rows * (2 * cols + 1))
    full = np.stack([even, odd, even.T, odd.T]).astype(np.float32)
    high = full.astype(jnp.bfloat16)
    low = (full - high.astype(np.float32)).astype(jnp.bfloat16)
    return np.stack([high, low], axis=1)


def sorting_table(size):
    order = np.concatenate([np.arange(0, size, 2), np.arange(1, size, 2)])
    table = np.zeros((size, size), np.float32)
    table[order, np.arange(size)] = 1.0
    return table.astype(jnp.bfloat16)


def split(x):
    high = x.astype(bf16)
    return high, (x - high.astype(f32)).astype(bf16)


def dot3(left, right):
    lhs = jnp.concatenate([left[0], left[0], left[1]], axis=1)
    rhs = jnp.concatenate([right[0], right[1], right[0]], axis=0)
    return jnp.dot(lhs, rhs, preferred_element_type=f32)


def rows_of(*parts):
    return jnp.concatenate(parts, axis=0)


def cols_of(*parts):
    return jnp.concatenate(parts, axis=1)


def prep_kernel(places, order_t, probe, *refs):
    step = pl.program_id(0)
    size = probe.shape[-1]
    half = size // 2
    blocks = size // LANES
    phases, frames = refs[:blocks], refs[blocks : 2 * blocks]
    kern, sorted_frames, waves = refs[2 * blocks :]

    def halved(parts, at):
        ids = [(at, pl.ds(start, half, stride=2), slice(None)) for start in range(2)]
        return rows_of(*(cols_of(*(part[i] for part in parts)) for i in ids))

    def in_order(rows):
        first, rest = split(rows)
        second, third = split(rows - first.astype(f32))
        table = order_t[...]
        return jnp.dot(
            cols_of(first, second, third), rows_of(table, table, table), preferred_element_type=f32
        )

    @pl.when(step == 0)
    def _():
        angles = in_order(halved(phases, 0))
        kern[0] = jnp.cos(angles)
        kern[1] = jnp.sin(angles)

    sorted_frames[0] = in_order(halved(frames, 0))
    down = places[2 * step] % ROWS
    across = places[2 * step + 1] % LANES
    for plane in range(2):
        moved = pltpu.roll(probe[plane], across, axis=1)
        waves[0, plane] = pltpu.roll(moved, down, axis=0)


def prepare(places, probe, phases, frames):
    count, size = frames.shape[0], phases.shape[-1]
    blocks = size // LANES
    full = lambda *shape: pl.BlockSpec(shape, lambda i: (0,) * len(shape))
    return pl.pallas_call(
        prep_kernel,
        grid=(count,),
        in_specs=[
            SMEM,
            full(size, size),
            full(2, size, size),
            *(pl.BlockSpec((1, size, LANES), lambda i, b=b: (0, 0, b)) for b in range(blocks)),
            *(pl.BlockSpec((1, size, LANES), lambda i, b=b: (i, 0, b)) for b in range(blocks)),
        ],
        out_specs=[
            full(2, size, size),
            pl.BlockSpec((1, size, size), lambda i: (i, 0, 0)),
            pl.BlockSpec((1, 2, size, size), lambda i: (i, 0, 0, 0)),
        ],
        out_shape=[
            jax.ShapeDtypeStruct((2, size, size), f32),
            jax.ShapeDtypeStruct((count, size, size), f32),
            jax.ShapeDtypeStruct((count, 2, size, size), f32),
        ],
        compiler_params=pltpu.CompilerParams(vmem_limit_bytes=16 * MIB),
        cost_estimate=pl.CostEstimate(
            flops=2 * (count + 1) * 3 * size**3,
            bytes_accessed=4 * size * size * (4 * count + 6),
            transcendentals=2 * size * size,
        ),
        name="prepare",
    )(
        places,
        jnp.asarray(sorting_table(size)),
        probe,
        *[phases[None]] * blocks,
        *[frames] * blocks,
    )


def pack_kernel(edges, half, offsets, tile_re, tile_im, *rest):
    strips, sems = rest[:-1], rest[-1]
    tile_rows, tile_cols = tile_re.shape[1:]
    columns = {-1: pl.ds(0, half), 0: pl.ds(0, tile_cols), 1: pl.ds(tile_cols - half, half)}
    copies = []
    for (side, across), strip in zip(edges, strips):
        if side is None:
            rows = pl.ds(0, tile_rows)
        else:
            rows = pl.ds(pl.multiple_of(offsets[side], half), half)
        for plane, tile in enumerate((tile_re, tile_im)):
            copies.append(
                pltpu.make_async_copy(
                    tile.at[0, rows, columns[across]], strip.at[plane], sems.at[len(copies)]
                )
            )
            copies[-1].start()
    for copy in copies:
        copy.wait()


def strip_shapes(edges, tile_rows, tile_cols, half):
    return [
        jax.ShapeDtypeStruct(
            (2, tile_rows if side is None else half, half if across else tile_cols), bf16
        )
        for side, across in edges
    ]


def pack(offsets, tile_re, tile_im, edges, half):
    return pl.pallas_call(
        functools.partial(pack_kernel, edges, half),
        in_specs=[SMEM, HBM, HBM],
        out_specs=[HBM] * len(edges),
        out_shape=strip_shapes(edges, *tile_re.shape[1:], half),
        scratch_shapes=[pltpu.SemaphoreType.DMA((2 * len(edges),))],
        compiler_params=pltpu.CompilerParams(vmem_limit_bytes=4 * MIB),
        name="pack",
    )(offsets, tile_re, tile_im)


def spot(places, at):
    row, col = places[2 * at], places[2 * at + 1]
    down, across = row % ROWS, col % LANES
    return down, across, pl.multiple_of(row - down, ROWS), pl.multiple_of(col - across, LANES)


def gather_kernel(spots, edges, half, places, offsets, tile_re, tile_im, after, *rest):
    strips, (mine, other, padded, sems) = rest[:-4], rest[-4:]
    tile_rows, tile_cols = tile_re.shape[1:]
    size = mine.shape[-1]
    body = (pl.ds(half, tile_rows), pl.ds(half, tile_cols))
    copies = []

    def bring(source, target):
        copies.append(pltpu.make_async_copy(source, target, sems.at[len(copies)]))
        copies[-1].start()

    bring(tile_re.at[0], padded.at[(0,) + body])
    bring(tile_im.at[0], padded.at[(1,) + body])
    columns = {-1: pl.ds(0, half), 0: body[1], 1: pl.ds(half + tile_cols, half)}
    for (side, across), strip in zip(edges, strips):
        if side is None:
            down = body[0]
        else:
            down = pl.ds(pl.multiple_of(offsets[side], half), half)
        bring(strip, padded.at[:, down, columns[across]])
    for copy in copies:
        copy.wait()

    sections = 2
    lane = lax.broadcasted_iota(jnp.int32, (size, LANES), 1)
    top_lane = lax.broadcasted_iota(jnp.int32, (ROWS, LANES), 1)
    top_row = lax.broadcasted_iota(jnp.int32, (ROWS, size), 0)
    here = offsets[offsets.shape[0] - 1]

    def cut(at, target, place):
        down, across, top, left = spot(places, at)
        inner = size - LANES
        rest = pl.ds(pl.multiple_of(top + ROWS, ROWS), size - ROWS)

        def cols(start, width):
            return pl.ds(pl.multiple_of(left + start, LANES), width)

        for plane in range(2):
            target[place, plane, ROWS:, LANES:] = padded[plane, rest, cols(LANES, inner)]
            near = padded[plane, rest, cols(0, LANES)].astype(f32)
            far = padded[plane, rest, cols(size, LANES)].astype(f32)
            target[place, plane, ROWS:, :LANES] = jnp.where(
                lane[ROWS:] < across, far, near
            ).astype(bf16)
            rows = []
            for start in (0, size):
                block = padded[
                    plane, pl.ds(pl.multiple_of(top + start, ROWS), ROWS), cols(0, size + LANES)
                ].astype(f32)
                first = jnp.where(top_lane < across, block[:, size:], block[:, :LANES])
                rows.append(cols_of(first, block[:, LANES:size]))
            target[place, plane, :ROWS, :] = jnp.where(top_row < down, rows[1], rows[0]).astype(
                bf16
            )

    for place in range(spots // sections):
        cut(sections * place + 1 - here, other, place)
        cut(sections * place + here, mine, place)


def gather(places, offsets, tile_re, tile_im, after, edges, strips, size):
    half = size // 2
    spots = places.shape[0] // 2
    tile_rows, tile_cols = tile_re.shape[1:]
    shape = jax.ShapeDtypeStruct((spots // 2, 2, size, size), bf16)
    vmem = pl.BlockSpec(memory_space=pltpu.VMEM)
    return pl.pallas_call(
        functools.partial(gather_kernel, spots, edges, half),
        in_specs=[SMEM, SMEM] + [HBM] * (3 + len(strips)),
        out_specs=[vmem, vmem],
        out_shape=[shape, shape],
        scratch_shapes=[
            pltpu.VMEM((2, tile_rows + 2 * half, tile_cols + 2 * half), bf16),
            pltpu.SemaphoreType.DMA((2 + len(strips),)),
        ],
        compiler_params=pltpu.CompilerParams(vmem_limit_bytes=16 * MIB),
        name="gather",
    )(places, offsets, tile_re, tile_im, after, *strips)


def chain_kernel(
    group, places, live, here, tables, kern, mine, theirs, frames, waves,
    keep, send, pulled_keep, pulled_send, windows, middle, terms, pulled, sems,
):
    step = pl.program_id(0)
    steps = pl.num_programs(0)
    size = kern.shape[-1]
    half = size // 2
    me = here[0]

    def fetch(at, which):
        source, slot = ((mine, me), (theirs, 1 - me))[which]
        rows = pl.ds(at * group, group)
        return pltpu.make_async_copy(
            source.at[rows], windows.at[at, slot], sems.at[2 * at + which]
        )

    @pl.when(step == 0)
    def _():
        for at in range(windows.shape[0]):
            fetch(at, 0).start()
            fetch(at, 1).start()
        pulled[...] = jnp.zeros_like(pulled)

    fetch(step, 0).wait()
    fetch(step, 1).wait()

    def table(which):
        return tables[which, 0], tables[which, 1]

    def forward(re, im):
        halves = []
        for sign, which in ((1, 2), (-1, 3)):
            if sign > 0:
                part = rows_of(re[:half] + re[half:], im[:half] + im[half:])
            else:
                part = rows_of(re[:half] - re[half:], im[:half] - im[half:])
            halves.append(dot3(table(which), split(part)))
        outs = []
        for sign, which in ((1, 0), (-1, 1)):
            parts = []
            for out in halves:
                re, im = out[:half], out[half:]
                if sign > 0:
                    parts.append(cols_of(re[:, :half] + re[:, half:], im[:, :half] + im[:, half:]))
                else:
                    parts.append(cols_of(re[:, :half] - re[:, half:], im[:, :half] - im[:, half:]))
            outs.append(dot3(split(rows_of(*parts)), table(which)))
        return outs

    def inverse(even, odd):
        first = dot3(split(even), table(2))
        second = dot3(split(odd), table(3))
        plus, minus = first + second, first - second
        re = cols_of(plus[:, :half], minus[:, :half])
        im = cols_of(plus[:, half:], minus[:, half:])
        first = dot3(table(0), split(rows_of(re[:half], im[:half])))
        second = dot3(table(1), split(rows_of(re[half:], im[half:])))
        plus, minus = first + second, first - second
        return rows_of(plus[:half], minus[:half]), rows_of(plus[half:], minus[half:])

    def propagate(re, im, sign):
        outs = []
        for at, part in enumerate(forward(re, im)):
            cols = slice(at * half, (at + 1) * half)
            kre, kim = kern[0, :, cols], kern[1, :, cols] * sign
            re, im = part[:, :half], part[:, half:]
            outs.append(cols_of(re * kre - im * kim, re * kim + im * kre))
        return inverse(*outs)

    def rounded(x):
        return x.astype(bf16).astype(f32)

    def window(slot, at):
        return windows[step, slot, at, 0].astype(f32), windows[step, slot, at, 1].astype(f32)

    for at in range(group):
        wre, wim = window(0, at)
        pre, pim = waves[at, 0], waves[at, 1]
        re, im = propagate(pre * wre - pim * wim, pre * wim + pim * wre, 1.0)
        middle[at, 0] = re.astype(bf16)
        middle[at, 1] = im.astype(bf16)

    for at in range(group):
        wre, wim = window(1, at)
        pre, pim = middle[at, 0].astype(f32), middle[at, 1].astype(f32)
        back = []
        for k, part in enumerate(forward(pre * wre - pim * wim, pre * wim + pim * wre)):
            re, im = part[:, :half], part[:, half:]
            misfit = re * re + im * im - frames[at, :, k * half : (k + 1) * half]
            back.append(cols_of(re * misfit, im * misfit))
        cre, cim = inverse(*back)
        pre, pim = middle[at, 0].astype(f32), middle[at, 1].astype(f32)
        terms[1, at, 0] = pre * cre + pim * cim
        terms[1, at, 1] = pre * cim - pim * cre
        wre, wim = window(1, at)
        re, im = propagate(wre * cre + wim * cim, wre * cim - wim * cre, -1.0)
        cre, cim = rounded(re), rounded(im)
        pre, pim = waves[at, 0], waves[at, 1]
        terms[0, at, 0] = pre * cre + pim * cim
        terms[0, at, 1] = pre * cim - pim * cre
        wre, wim = window(0, at)
        spot_at = step * group + at
        up = (size - places[2 * spot_at] % ROWS) % size
        back_by = (size - places[2 * spot_at + 1] % LANES) % size
        weight = live[spot_at].astype(f32)
        for plane, value in enumerate((wre * cre + wim * cim, wre * cim - wim * cre)):
            value = pltpu.roll(pltpu.roll(value * weight, back_by, axis=1), up, axis=0)
            pulled[plane] += value

    keep[...] = terms[me]
    send[...] = terms[1 - me].astype(bf16)

    @pl.when(step == steps - 1)
    def _():
        share = pulled_keep.shape[1]
        for plane in range(2):
            pulled_keep[plane] = pulled[plane, pl.ds(pl.multiple_of(me * share, share), share), :]
            pulled_send[plane] = pulled[
                plane, pl.ds(pl.multiple_of((1 - me) * share, share), share), :
            ]


def chain(places, live, here, kern, mine, theirs, frames, waves, group):
    count, size = frames.shape[0], frames.shape[-1]
    full = lambda *shape: pl.BlockSpec(shape, lambda i: (0,) * len(shape))
    block = pl.BlockSpec((group, 2, size, size), lambda i: (i, 0, 0, 0))
    return pl.pallas_call(
        functools.partial(chain_kernel, group),
        grid=(count // group,),
        in_specs=[
            SMEM,
            SMEM,
            SMEM,
            full(4, 2, size, size),
            full(2, size, size),
            HBM,
            HBM,
            pl.BlockSpec((group, size, size), lambda i: (i, 0, 0)),
            block,
        ],
        out_specs=[block, block, full(2, size // 2, size), full(2, size // 2, size)],
        out_shape=[
            jax.ShapeDtypeStruct((count, 2, size, size), f32),
            jax.ShapeDtypeStruct((count, 2, size, size), bf16),
            jax.ShapeDtypeStruct((2, size // 2, size), f32),
            jax.ShapeDtypeStruct((2, size // 2, size), f32),
        ],
        scratch_shapes=[
            pltpu.VMEM((count // group, 2, group, 2, size, size), bf16),
            pltpu.VMEM((group, 2, size, size), bf16),
            pltpu.VMEM((2, group, 2, size, size), f32),
            pltpu.VMEM((2, size, size), f32),
            pltpu.SemaphoreType.DMA((2 * (count // group),)),
        ],
        compiler_params=pltpu.CompilerParams(vmem_limit_bytes=40 * MIB),
        name="chain",
    )(places, live, here, jnp.asarray(dft_tables(size)), kern, mine, theirs, frames, waves)


def scatter_kernel(edges, half, places, live, offsets, kept, arrived, tile, *rest):
    strips, (total, near, far, sems) = rest[:-4], rest[-4:]
    count, size = kept.shape[0], kept.shape[-1]
    tile_rows, tile_cols = tile.shape[1:]
    sections = 2
    here = offsets[offsets.shape[0] - 1]

    def fetch(place, which):
        source, target = ((kept, near), (arrived, far))[which]
        return pltpu.make_async_copy(
            source.at[place], target.at[place], sems.at[1 + 2 * place + which]
        )

    for which in range(2):
        for place in range(count):
            fetch(place, which).start()
    total[...] = jnp.zeros_like(total)
    lane = lax.broadcasted_iota(jnp.int32, (size, LANES), 1)
    row = lax.broadcasted_iota(jnp.int32, (ROWS, size + LANES), 0)

    def add(at, source, place):
        down, across, top, left = spot(places, at)
        wide = pl.ds(left, size + LANES)

        @pl.when(live[at] > 0)
        def _():
            for plane in range(2):
                value = source[place, plane].astype(f32)
                first = value[:, :LANES]
                inside = lane >= across
                value = cols_of(
                    jnp.where(inside, first, 0.0), value[:, LANES:], jnp.where(inside, 0.0, first)
                )
                first = value[:ROWS]
                inside = row >= down
                value = rows_of(
                    jnp.where(inside, first, 0.0), value[ROWS:], jnp.where(inside, 0.0, first)
                )
                total[plane, pl.ds(top, size + ROWS), wide] += value

    for which, (source, owner) in enumerate(((near, here), (far, 1 - here))):
        for place in range(count):
            fetch(place, which).wait()
            add(sections * place + owner, source, place)
    body = (pl.ds(half, tile_rows), pl.ds(half, tile_cols))
    copy = pltpu.make_async_copy(total.at[(slice(None),) + body], tile, sems.at[0])
    copy.start()
    columns = {-1: pl.ds(0, half), 0: body[1], 1: pl.ds(half + tile_cols, half)}
    for (side, across), strip in zip(edges, strips):
        if side is None:
            rows = body[0]
        else:
            rows = pl.ds(pl.multiple_of(offsets[side], half), half)
        for plane in range(2):
            strip[plane] = total[plane, rows, columns[across]].astype(bf16)
    copy.wait()


def scatter(places, live, offsets, kept, arrived, edges, tile_rows, tile_cols):
    count, _, size, _ = kept.shape
    half = size // 2
    vmem = pl.BlockSpec(memory_space=pltpu.VMEM)
    return pl.pallas_call(
        functools.partial(scatter_kernel, edges, half),
        in_specs=[SMEM, SMEM, SMEM, HBM, HBM],
        out_specs=[HBM] + [vmem] * len(edges),
        out_shape=[jax.ShapeDtypeStruct((2, tile_rows, tile_cols), f32)]
        + strip_shapes(edges, tile_rows, tile_cols, half),
        scratch_shapes=[
            pltpu.VMEM((2, tile_rows + 2 * half, tile_cols + 2 * half), f32),
            pltpu.VMEM(kept.shape, f32),
            pltpu.VMEM(arrived.shape, bf16),
            pltpu.SemaphoreType.DMA((1 + 2 * count,)),
        ],
        compiler_params=pltpu.CompilerParams(vmem_limit_bytes=20 * MIB),
        name="scatter",
    )(places, live, offsets, kept, arrived)


def border_kernel(edges, half, offsets, tile_in, *rest):
    sides = offsets.shape[0] - 1
    strips, (tile, bands, left, right, in_sems, out_sems) = rest[: len(edges)], rest[len(edges) :]
    tile_rows, tile_cols = tile.shape[1:]
    strips = dict(zip(edges, strips))
    tall = left.shape[1]
    rows = pl.ds(pl.multiple_of(offsets[sides], half), tall)
    regions = []
    for side in range(sides):
        band = pl.ds(pl.multiple_of(offsets[side], half), half)
        regions.append((bands.at[side], band, pl.ds(0, tile_cols)))
    regions.append((left, rows, pl.ds(0, half)))
    regions.append((right, rows, pl.ds(tile_cols - half, half)))

    def copy(k, out):
        block, down, wide = regions[k]
        if out:
            return pltpu.make_async_copy(block, tile.at[:, down, wide], out_sems.at[k])
        return pltpu.make_async_copy(tile_in.at[:, down, wide], block, in_sems.at[k])

    order = [sides, sides + 1, *range(sides)]
    for k in order:
        copy(k, False).start()
    for k in order:
        copy(k, False).wait()
        block, down, wide = regions[k]
        for plane in range(2):
            if k < sides:
                block[plane] += strips[(k, 0)][plane].astype(f32)
                for across, cols in ((-1, slice(0, half)), (1, slice(tile_cols - half, tile_cols))):
                    block[plane, :, cols] += strips[(k, across)][plane].astype(f32) + strips[
                        (None, across)
                    ][plane, down, :].astype(f32)
            else:
                across = -1 if k == sides else 1
                block[plane] += strips[(None, across)][plane, down, :].astype(f32)
        copy(k, True).start()
    for k in order:
        copy(k, True).wait()


def add_borders(offsets, tile, edges, strips, half):
    vmem = pl.BlockSpec(memory_space=pltpu.VMEM)
    sides = offsets.shape[0] - 1
    tile_rows, tile_cols = tile.shape[1:]
    column = (2, tile_rows - sides * half, half)
    return pl.pallas_call(
        functools.partial(border_kernel, edges, half),
        in_specs=[SMEM, HBM] + [vmem] * len(strips),
        out_specs=HBM,
        out_shape=jax.ShapeDtypeStruct(tile.shape, f32),
        scratch_shapes=[
            pltpu.VMEM((max(sides, 1), 2, half, tile_cols), f32),
            pltpu.VMEM(column, f32),
            pltpu.VMEM(column, f32),
            pltpu.SemaphoreType.DMA((sides + 2,)),
            pltpu.SemaphoreType.DMA((sides + 2,)),
        ],
        input_output_aliases={1: 0},
        compiler_params=pltpu.CompilerParams(vmem_limit_bytes=12 * MIB),
        name="borders",
    )(offsets, tile, *strips)


def routes(edges, sides, rows, cols):
    result = []
    for side, across in edges:
        pairs = []
        for r in range(rows):
            if side is None:
                to_row = r
            elif rows == 2:
                to_row = 1 - r
            else:
                to_row = r + sides[side]
            for c in range(cols):
                to_col = c + across
                if 0 <= to_row < rows and 0 <= to_col < cols:
                    pairs.append((r * cols + c, to_row * cols + to_col))
        result.append(pairs)
    return result


def summed(block, axes):
    for axis in axes:
        size = lax.axis_size(axis)
        if size & (size - 1):
            block = lax.psum(block, axis)
            continue
        for step in reversed([1 << k for k in range(size.bit_length() - 1)]):
            own = block.astype(bf16)
            other = lax.ppermute(own, axis, [(i, i ^ step) for i in range(size)])
            block = own.astype(f32) + other.astype(f32)
    return block


def shards(probe, object_re, object_im, phases, centres, occupied, measured):
    size = probe.shape[1]
    half = size // 2
    rows, cols = lax.axis_size("row"), lax.axis_size("col")
    sections = lax.axis_size("depth")
    assert sections == 2 and object_re.shape[0] == 1
    here = lax.axis_index("depth").astype(jnp.int32)
    row_at = lax.axis_index("row").astype(jnp.int32)
    tile_rows, tile_cols = object_re.shape[1:]
    batches, slots = centres.shape[2:4]
    spots = batches * slots
    count = spots // sections

    places = centres.reshape(2 * spots)
    slot_ids = jnp.arange(slots, dtype=jnp.int32)
    live = (slot_ids[None, :] < occupied[0, 0][:, None]).astype(jnp.int32)
    my_places = lax.dynamic_index_in_dim(
        centres.reshape(count, sections, 2), here, 1, False
    ).reshape(2 * count)
    my_live = lax.dynamic_index_in_dim(live.reshape(count, sections), here, 1, False)
    live = live.reshape(spots)
    frames = lax.dynamic_index_in_dim(
        measured.reshape(count, sections, size, size), here, 1, False
    )

    if rows == 1:
        sides, from_rows, pad_rows, fold_rows = [], [], [], []
    elif rows == 2:
        sides = [0]
        from_rows = [jnp.where(row_at == 0, tile_rows - half, 0)]
        pad_rows = [jnp.where(row_at == 0, tile_rows + half, 0)]
        fold_rows = from_rows
    else:
        sides = [1, -1]
        from_rows = [jnp.int32(tile_rows - half), jnp.int32(0)]
        pad_rows = [jnp.int32(0), jnp.int32(tile_rows + half)]
        fold_rows = [jnp.int32(0), jnp.int32(tile_rows - half)]
    edges = [(side, across) for side in range(len(sides)) for across in (1, -1)]
    edges += [(None, 1), (None, -1)]
    edges += [(side, 0) for side in range(len(sides))]
    paths = routes(edges, sides, rows, cols)
    both = ("row", "col")
    landed = [(side, -across) for side, across in edges]

    def numbers(*values):
        return jnp.stack(values).astype(jnp.int32)

    own = pack(numbers(*from_rows, here), object_re, object_im, edges, half)
    strips = [lax.ppermute(strip, both, path) for strip, path in zip(own, paths)]
    kern, sorted_frames, waves = prepare(my_places, probe, phases, frames)
    mine, other = gather(
        places, numbers(*pad_rows, here), object_re, object_im, waves, landed, strips, size
    )
    across_depth = [(i, 1 - i) for i in range(sections)]
    theirs = lax.ppermute(other, "depth", across_depth)
    keep, send, pulled_keep, pulled_send = chain(
        my_places, my_live, here.reshape(1), kern, mine, theirs, sorted_frames, waves, 2
    )
    arrived = lax.ppermute(send, "depth", across_depth)
    pulled = pulled_keep + lax.ppermute(pulled_send, "depth", across_depth)

    out_rows = pad_rows if rows == 2 else pad_rows[::-1]
    tile, *own = scatter(
        places, live, numbers(*out_rows, here), keep, arrived, edges, tile_rows, tile_cols
    )
    *own, pulled = lax.optimization_barrier((*own, pulled))
    added = [lax.ppermute(strip, both, path) for strip, path in zip(own, paths)]
    first_row = jnp.where(row_at == 0, 0, half) if rows == 2 else jnp.int32(half * (rows > 1))
    gradient = add_borders(numbers(*fold_rows, first_row), tile, landed, added, half)
    probe_share = summed(pulled, ("col", "row"))
    return (gradient[:, None], probe_share)


def solution(mesh):
    in_specs = (
        P(),
        P("depth", "row", "col"),
        P("depth", "row", "col"),
        P(),
        P("row", "col", None, None, None),
        P("row", "col", None),
        P("row", "col", None, None, None, None),
    )
    out_specs = (P(None, "depth", "row", "col"), P(None, "depth", None))
    return jax.shard_map(shards, mesh=mesh, in_specs=in_specs, out_specs=out_specs, check_vma=False)
```

```python
import functools

import jax
import jax.numpy as jnp
import numpy as np
from jax import lax
from jax.experimental import pallas as pl
from jax.experimental.pallas import tpu as pltpu
from jax.sharding import PartitionSpec as P

f32 = jnp.float32
bf16 = jnp.bfloat16
ROWS = 16
LANES = 128
ANY = pl.BlockSpec(memory_space=pl.ANY)
HBM = pl.BlockSpec(memory_space=pltpu.HBM)
SMEM = pl.BlockSpec(memory_space=pltpu.SMEM)
MIB = 1024 * 1024


def dft_tables(size):
    half = size // 2
    rows = np.arange(half)[:, None]
    cols = np.arange(half)[None, :]

    def packed(turns):
        angle = -2.0 * np.pi * (turns % size) / size
        re, im = np.cos(angle) / np.sqrt(size), np.sin(angle) / np.sqrt(size)
        return np.block([[re, im], [-im, re]])

    even, odd = packed(rows * 2 * cols), packed(rows * (2 * cols + 1))
    full = np.stack([even, odd, even.T, odd.T]).astype(np.float32)
    high = full.astype(jnp.bfloat16)
    low = (full - high.astype(np.float32)).astype(jnp.bfloat16)
    return np.stack([high, low], axis=1)


def sorting_table(size):
    order = np.concatenate([np.arange(0, size, 2), np.arange(1, size, 2)])
    table = np.zeros((size, size), np.float32)
    table[order, np.arange(size)] = 1.0
    return table.astype(jnp.bfloat16)


def split(x):
    high = x.astype(bf16)
    return high, (x - high.astype(f32)).astype(bf16)


def dot3(left, right):
    lhs = jnp.concatenate([left[0], left[0], left[1]], axis=1)
    rhs = jnp.concatenate([right[0], right[1], right[0]], axis=0)
    return jnp.dot(lhs, rhs, preferred_element_type=f32)


def rows_of(*parts):
    return jnp.concatenate(parts, axis=0)


def cols_of(*parts):
    return jnp.concatenate(parts, axis=1)


def prep_kernel(places, order_t, probe, *refs):
    step = pl.program_id(0)
    size = probe.shape[-1]
    half = size // 2
    blocks = size // LANES
    phases, frames = refs[:blocks], refs[blocks : 2 * blocks]
    kern, sorted_frames, waves = refs[2 * blocks :]

    def halved(parts, at):
        ids = [(at, pl.ds(start, half, stride=2), slice(None)) for start in range(2)]
        return rows_of(*(cols_of(*(part[i] for part in parts)) for i in ids))

    def in_order(rows):
        first, rest = split(rows)
        second, third = split(rows - first.astype(f32))
        table = order_t[...]
        return jnp.dot(
            cols_of(first, second, third), rows_of(table, table, table), preferred_element_type=f32
        )

    @pl.when(step == 0)
    def _():
        angles = in_order(halved(phases, 0))
        kern[0] = jnp.cos(angles)
        kern[1] = jnp.sin(angles)

    sorted_frames[0] = in_order(halved(frames, 0))
    down = places[2 * step] % ROWS
    across = places[2 * step + 1] % LANES
    for plane in range(2):
        moved = pltpu.roll(probe[plane], across, axis=1)
        waves[0, plane] = pltpu.roll(moved, down, axis=0)


def prepare(places, probe, phases, frames):
    count, size = frames.shape[0], phases.shape[-1]
    blocks = size // LANES
    full = lambda *shape: pl.BlockSpec(shape, lambda i: (0,) * len(shape))
    return pl.pallas_call(
        prep_kernel,
        grid=(count,),
        in_specs=[
            SMEM,
            full(size, size),
            full(2, size, size),
            *(pl.BlockSpec((1, size, LANES), lambda i, b=b: (0, 0, b)) for b in range(blocks)),
            *(pl.BlockSpec((1, size, LANES), lambda i, b=b: (i, 0, b)) for b in range(blocks)),
        ],
        out_specs=[
            full(2, size, size),
            pl.BlockSpec((1, size, size), lambda i: (i, 0, 0)),
            pl.BlockSpec((1, 2, size, size), lambda i: (i, 0, 0, 0)),
        ],
        out_shape=[
            jax.ShapeDtypeStruct((2, size, size), f32),
            jax.ShapeDtypeStruct((count, size, size), f32),
            jax.ShapeDtypeStruct((count, 2, size, size), f32),
        ],
        compiler_params=pltpu.CompilerParams(vmem_limit_bytes=16 * MIB),
        cost_estimate=pl.CostEstimate(
            flops=2 * (count + 1) * 3 * size**3,
            bytes_accessed=4 * size * size * (4 * count + 6),
            transcendentals=2 * size * size,
        ),
        name="prepare",
    )(
        places,
        jnp.asarray(sorting_table(size)),
        probe,
        *[phases[None]] * blocks,
        *[frames] * blocks,
    )


def span(key, offsets, names, half, whole):
    if key is None:
        return whole
    return pl.ds(pl.multiple_of(offsets[names.index(key)], half), half)


def pack_kernel(edges, names, half, offsets, tile_re, tile_im, *rest):
    strips, sems = rest[:-1], rest[-1]
    tile_rows, tile_cols = tile_re.shape[1:]
    copies = []
    for (down, across), strip in zip(edges, strips):
        rows = span(down, offsets, names, half, pl.ds(0, tile_rows))
        cols = span(across, offsets, names, half, pl.ds(0, tile_cols))
        for plane, tile in enumerate((tile_re, tile_im)):
            copies.append(
                pltpu.make_async_copy(
                    tile.at[0, rows, cols], strip.at[plane], sems.at[len(copies)]
                )
            )
            copies[-1].start()
    for copy in copies:
        copy.wait()


def strip_shapes(edges, tile_rows, tile_cols, half):
    return [
        jax.ShapeDtypeStruct(
            (2, half if down else tile_rows, half if across else tile_cols), bf16
        )
        for down, across in edges
    ]


def pack(offsets, tile_re, tile_im, edges, names, half):
    return pl.pallas_call(
        functools.partial(pack_kernel, edges, names, half),
        in_specs=[SMEM, HBM, HBM],
        out_specs=[ANY] * len(edges),
        out_shape=strip_shapes(edges, *tile_re.shape[1:], half),
        scratch_shapes=[pltpu.SemaphoreType.DMA((2 * len(edges),))],
        compiler_params=pltpu.CompilerParams(vmem_limit_bytes=4 * MIB),
        name="pack",
    )(offsets, tile_re, tile_im)


def spot(places, at):
    row, col = places[2 * at], places[2 * at + 1]
    down, across = row % ROWS, col % LANES
    return down, across, pl.multiple_of(row - down, ROWS), pl.multiple_of(col - across, LANES)


def gather_kernel(spots, edges, names, half, places, offsets, tile_re, tile_im, after, *rest):
    strips, (mine, other, padded, sems) = rest[:-4], rest[-4:]
    tile_rows, tile_cols = tile_re.shape[1:]
    size = mine.shape[-1]
    body = (pl.ds(half, tile_rows), pl.ds(half, tile_cols))
    copies = []

    def bring(source, target):
        copies.append(pltpu.make_async_copy(source, target, sems.at[len(copies)]))
        copies[-1].start()

    bring(tile_re.at[0], padded.at[(0,) + body])
    bring(tile_im.at[0], padded.at[(1,) + body])
    for (down, across), strip in zip(edges, strips):
        rows = span(down, offsets, names, half, body[0])
        cols = span(across, offsets, names, half, body[1])
        bring(strip, padded.at[:, rows, cols])
    for copy in copies:
        copy.wait()

    sections = 2
    lane = lax.broadcasted_iota(jnp.int32, (size, LANES), 1)
    top_lane = lax.broadcasted_iota(jnp.int32, (ROWS, LANES), 1)
    top_row = lax.broadcasted_iota(jnp.int32, (ROWS, size), 0)
    here = offsets[offsets.shape[0] - 1]

    def cut(at, target, place):
        down, across, top, left = spot(places, at)
        inner = size - LANES
        rest = pl.ds(pl.multiple_of(top + ROWS, ROWS), size - ROWS)

        def cols(start, width):
            return pl.ds(pl.multiple_of(left + start, LANES), width)

        for plane in range(2):
            target[place, plane, ROWS:, LANES:] = padded[plane, rest, cols(LANES, inner)]
            near = padded[plane, rest, cols(0, LANES)].astype(f32)
            far = padded[plane, rest, cols(size, LANES)].astype(f32)
            target[place, plane, ROWS:, :LANES] = jnp.where(
                lane[ROWS:] < across, far, near
            ).astype(bf16)
            rows = []
            for start in (0, size):
                block = padded[
                    plane, pl.ds(pl.multiple_of(top + start, ROWS), ROWS), cols(0, size + LANES)
                ].astype(f32)
                first = jnp.where(top_lane < across, block[:, size:], block[:, :LANES])
                rows.append(cols_of(first, block[:, LANES:size]))
            target[place, plane, :ROWS, :] = jnp.where(top_row < down, rows[1], rows[0]).astype(
                bf16
            )

    for place in range(spots // sections):
        cut(sections * place + 1 - here, other, place)
        cut(sections * place + here, mine, place)


def gather(places, offsets, tile_re, tile_im, after, edges, names, strips, size):
    half = size // 2
    spots = places.shape[0] // 2
    tile_rows, tile_cols = tile_re.shape[1:]
    shape = jax.ShapeDtypeStruct((spots // 2, 2, size, size), bf16)
    vmem = pl.BlockSpec(memory_space=pltpu.VMEM)
    return pl.pallas_call(
        functools.partial(gather_kernel, spots, edges, names, half),
        in_specs=[SMEM, SMEM, HBM, HBM] + [ANY] * (1 + len(strips)),
        out_specs=[vmem, vmem],
        out_shape=[shape, shape],
        scratch_shapes=[
            pltpu.VMEM((2, tile_rows + 2 * half, tile_cols + 2 * half), bf16),
            pltpu.SemaphoreType.DMA((2 + len(strips),)),
        ],
        compiler_params=pltpu.CompilerParams(vmem_limit_bytes=16 * MIB),
        name="gather",
    )(places, offsets, tile_re, tile_im, after, *strips)


def chain_kernel(
    group, places, live, here, tables, kern, mine, theirs, frames, waves,
    keep, send, pulled_keep, pulled_send, windows, middle, terms, pulled, sems, keep_sems,
):
    step = pl.program_id(0)
    steps = pl.num_programs(0)
    size = kern.shape[-1]
    half = size // 2
    me = here[0]

    def fetch(at, which):
        source, slot = ((mine, me), (theirs, 1 - me))[which]
        rows = pl.ds(at * group, group)
        return pltpu.make_async_copy(
            source.at[rows], windows.at[at, slot], sems.at[2 * at + which]
        )

    @pl.when(step == 0)
    def _():
        for at in range(windows.shape[0]):
            fetch(at, 0).start()
            fetch(at, 1).start()
        pulled[...] = jnp.zeros_like(pulled)

    fetch(step, 0).wait()
    fetch(step, 1).wait()

    def table(which):
        return tables[which, 0], tables[which, 1]

    def forward(re, im):
        halves = []
        for sign, which in ((1, 2), (-1, 3)):
            if sign > 0:
                part = rows_of(re[:half] + re[half:], im[:half] + im[half:])
            else:
                part = rows_of(re[:half] - re[half:], im[:half] - im[half:])
            halves.append(dot3(table(which), split(part)))
        outs = []
        for sign, which in ((1, 0), (-1, 1)):
            parts = []
            for out in halves:
                re, im = out[:half], out[half:]
                if sign > 0:
                    parts.append(cols_of(re[:, :half] + re[:, half:], im[:, :half] + im[:, half:]))
                else:
                    parts.append(cols_of(re[:, :half] - re[:, half:], im[:, :half] - im[:, half:]))
            outs.append(dot3(split(rows_of(*parts)), table(which)))
        return outs

    def inverse(even, odd):
        first = dot3(split(even), table(2))
        second = dot3(split(odd), table(3))
        plus, minus = first + second, first - second
        re = cols_of(plus[:, :half], minus[:, :half])
        im = cols_of(plus[:, half:], minus[:, half:])
        first = dot3(table(0), split(rows_of(re[:half], im[:half])))
        second = dot3(table(1), split(rows_of(re[half:], im[half:])))
        plus, minus = first + second, first - second
        return rows_of(plus[:half], minus[:half]), rows_of(plus[half:], minus[half:])

    def propagate(re, im, sign):
        outs = []
        for at, part in enumerate(forward(re, im)):
            cols = slice(at * half, (at + 1) * half)
            kre, kim = kern[0, :, cols], kern[1, :, cols] * sign
            re, im = part[:, :half], part[:, half:]
            outs.append(cols_of(re * kre - im * kim, re * kim + im * kre))
        return inverse(*outs)

    def rounded(x):
        return x.astype(bf16).astype(f32)

    def window(slot, at):
        return windows[step, slot, at, 0].astype(f32), windows[step, slot, at, 1].astype(f32)

    for at in range(group):
        wre, wim = window(0, at)
        pre, pim = waves[at, 0], waves[at, 1]
        re, im = propagate(pre * wre - pim * wim, pre * wim + pim * wre, 1.0)
        middle[at, 0] = re.astype(bf16)
        middle[at, 1] = im.astype(bf16)

    for at in range(group):
        wre, wim = window(1, at)
        pre, pim = middle[at, 0].astype(f32), middle[at, 1].astype(f32)
        back = []
        for k, part in enumerate(forward(pre * wre - pim * wim, pre * wim + pim * wre)):
            re, im = part[:, :half], part[:, half:]
            misfit = re * re + im * im - frames[at, :, k * half : (k + 1) * half]
            back.append(cols_of(re * misfit, im * misfit))
        cre, cim = inverse(*back)
        pre, pim = middle[at, 0].astype(f32), middle[at, 1].astype(f32)
        terms[step, 1, at, 0] = pre * cre + pim * cim
        terms[step, 1, at, 1] = pre * cim - pim * cre
        wre, wim = window(1, at)
        re, im = propagate(wre * cre + wim * cim, wre * cim - wim * cre, -1.0)
        cre, cim = rounded(re), rounded(im)
        pre, pim = waves[at, 0], waves[at, 1]
        terms[step, 0, at, 0] = pre * cre + pim * cim
        terms[step, 0, at, 1] = pre * cim - pim * cre
        wre, wim = window(0, at)
        spot_at = step * group + at
        up = (size - places[2 * spot_at] % ROWS) % size
        back_by = (size - places[2 * spot_at + 1] % LANES) % size
        weight = live[spot_at].astype(f32)
        for plane, value in enumerate((wre * cre + wim * cim, wre * cim - wim * cre)):
            value = pltpu.roll(pltpu.roll(value * weight, back_by, axis=1), up, axis=0)
            pulled[plane] += value

    send[...] = terms[step, 1 - me].astype(bf16)

    def put(at):
        rows = pl.ds(at * group, group)
        return pltpu.make_async_copy(terms.at[at, me], keep.at[rows], keep_sems.at[at])

    put(step).start()

    @pl.when(step == steps - 1)
    def _():
        for at in range(terms.shape[0]):
            put(at).wait()
        share = pulled_keep.shape[1]
        for plane in range(2):
            pulled_keep[plane] = pulled[plane, pl.ds(pl.multiple_of(me * share, share), share), :]
            pulled_send[plane] = pulled[
                plane, pl.ds(pl.multiple_of((1 - me) * share, share), share), :
            ]


def chain(places, live, here, kern, mine, theirs, frames, waves, group):
    count, size = frames.shape[0], frames.shape[-1]
    full = lambda *shape: pl.BlockSpec(shape, lambda i: (0,) * len(shape))
    block = pl.BlockSpec((group, 2, size, size), lambda i: (i, 0, 0, 0))
    return pl.pallas_call(
        functools.partial(chain_kernel, group),
        grid=(count // group,),
        in_specs=[
            SMEM,
            SMEM,
            SMEM,
            full(4, 2, size, size),
            full(2, size, size),
            ANY,
            ANY,
            pl.BlockSpec((group, size, size), lambda i: (i, 0, 0)),
            block,
        ],
        out_specs=[HBM, block, full(2, size // 2, size), full(2, size // 2, size)],
        out_shape=[
            jax.ShapeDtypeStruct((count, 2, size, size), f32),
            jax.ShapeDtypeStruct((count, 2, size, size), bf16),
            jax.ShapeDtypeStruct((2, size // 2, size), f32),
            jax.ShapeDtypeStruct((2, size // 2, size), f32),
        ],
        scratch_shapes=[
            pltpu.VMEM((count // group, 2, group, 2, size, size), bf16),
            pltpu.VMEM((group, 2, size, size), bf16),
            pltpu.VMEM((count // group, 2, group, 2, size, size), f32),
            pltpu.VMEM((2, size, size), f32),
            pltpu.SemaphoreType.DMA((2 * (count // group),)),
            pltpu.SemaphoreType.DMA((count // group,)),
        ],
        compiler_params=pltpu.CompilerParams(vmem_limit_bytes=40 * MIB),
        name="chain",
    )(places, live, here, jnp.asarray(dft_tables(size)), kern, mine, theirs, frames, waves)


def scatter_kernel(edges, names, half, places, live, offsets, kept, arrived, tile, *rest):
    strips, (total, near, far, sems) = rest[:-4], rest[-4:]
    count, size = kept.shape[0], kept.shape[-1]
    tile_rows, tile_cols = tile.shape[1:]
    sections = 2
    here = offsets[offsets.shape[0] - 1]

    def fetch(place, which):
        source, target = ((kept, near), (arrived, far))[which]
        return pltpu.make_async_copy(
            source.at[place], target.at[place], sems.at[1 + 2 * place + which]
        )

    for which in range(2):
        for place in range(count):
            fetch(place, which).start()
    total[...] = jnp.zeros_like(total)
    lane = lax.broadcasted_iota(jnp.int32, (size, LANES), 1)
    row = lax.broadcasted_iota(jnp.int32, (ROWS, size + LANES), 0)

    def add(at, source, place):
        down, across, top, left = spot(places, at)
        wide = pl.ds(left, size + LANES)

        @pl.when(live[at] > 0)
        def _():
            for plane in range(2):
                value = source[place, plane].astype(f32)
                first = value[:, :LANES]
                inside = lane >= across
                value = cols_of(
                    jnp.where(inside, first, 0.0), value[:, LANES:], jnp.where(inside, 0.0, first)
                )
                first = value[:ROWS]
                inside = row >= down
                value = rows_of(
                    jnp.where(inside, first, 0.0), value[ROWS:], jnp.where(inside, 0.0, first)
                )
                total[plane, pl.ds(top, size + ROWS), wide] += value

    for which, (source, owner) in enumerate(((near, here), (far, 1 - here))):
        for place in range(count):
            fetch(place, which).wait()
            add(sections * place + owner, source, place)
    body = (pl.ds(half, tile_rows), pl.ds(half, tile_cols))
    copy = pltpu.make_async_copy(total.at[(slice(None),) + body], tile, sems.at[0])
    copy.start()
    for (down, across), strip in zip(edges, strips):
        rows = span(down, offsets, names, half, body[0])
        cols = span(across, offsets, names, half, body[1])
        for plane in range(2):
            strip[plane] = total[plane, rows, cols].astype(bf16)
    copy.wait()


def scatter(places, live, offsets, kept, arrived, edges, names, tile_rows, tile_cols):
    count, _, size, _ = kept.shape
    half = size // 2
    vmem = pl.BlockSpec(memory_space=pltpu.VMEM)
    return pl.pallas_call(
        functools.partial(scatter_kernel, edges, names, half),
        in_specs=[SMEM, SMEM, SMEM, HBM, ANY],
        out_specs=[HBM] + [vmem] * len(edges),
        out_shape=[jax.ShapeDtypeStruct((2, tile_rows, tile_cols), f32)]
        + strip_shapes(edges, tile_rows, tile_cols, half),
        scratch_shapes=[
            pltpu.VMEM((2, tile_rows + 2 * half, tile_cols + 2 * half), f32),
            pltpu.VMEM(kept.shape, f32),
            pltpu.VMEM(arrived.shape, bf16),
            pltpu.SemaphoreType.DMA((1 + 2 * count,)),
        ],
        compiler_params=pltpu.CompilerParams(vmem_limit_bytes=20 * MIB),
        name="scatter",
    )(places, live, offsets, kept, arrived)


def border_kernel(edges, names, half, offsets, tile_in, *rest):
    strips, (tile, bands, sides, in_sems, out_sems) = rest[: len(edges)], rest[len(edges) :]
    tile_rows, tile_cols = tile.shape[1:]
    strips = dict(zip(edges, strips))
    downs = [key for key in names if key[0] == "row"]
    acrosses = [key for key in names if key[0] == "col"]
    tall = sides.shape[2]
    rest_rows = pl.ds(pl.multiple_of(offsets[len(names)], half), tall)
    spans = {key: span(key, offsets, names, half, None) for key in names}
    regions = []
    for k, key in enumerate(acrosses):
        regions.append((key, sides.at[k], rest_rows, spans[key]))
    for k, key in enumerate(downs):
        regions.append((key, bands.at[k], spans[key], pl.ds(0, tile_cols)))

    def copy(k, out):
        _, block, rows, cols = regions[k]
        if out:
            return pltpu.make_async_copy(block, tile.at[:, rows, cols], out_sems.at[k])
        return pltpu.make_async_copy(tile_in.at[:, rows, cols], block, in_sems.at[k])

    for k in range(len(regions)):
        copy(k, False).start()
    for k, (key, block, rows, cols) in enumerate(regions):
        copy(k, False).wait()
        for plane in range(2):
            if key in downs:
                block[plane] += strips[(key, None)][plane].astype(f32)
                for across in acrosses:
                    block[plane, :, spans[across]] += strips[(key, across)][plane].astype(
                        f32
                    ) + strips[(None, across)][plane, rows, :].astype(f32)
            else:
                block[plane] += strips[(None, key)][plane, rows, :].astype(f32)
        copy(k, True).start()
    for k in range(len(regions)):
        copy(k, True).wait()


def add_borders(offsets, tile, edges, names, strips, half):
    vmem = pl.BlockSpec(memory_space=pltpu.VMEM)
    downs = sum(key[0] == "row" for key in names)
    acrosses = len(names) - downs
    tile_rows, tile_cols = tile.shape[1:]
    return pl.pallas_call(
        functools.partial(border_kernel, edges, names, half),
        in_specs=[SMEM, HBM] + [vmem] * len(strips),
        out_specs=HBM,
        out_shape=jax.ShapeDtypeStruct(tile.shape, f32),
        scratch_shapes=[
            pltpu.VMEM((max(downs, 1), 2, half, tile_cols), f32),
            pltpu.VMEM((max(acrosses, 1), 2, tile_rows - downs * half, half), f32),
            pltpu.SemaphoreType.DMA((max(len(names), 1),)),
            pltpu.SemaphoreType.DMA((max(len(names), 1),)),
        ],
        input_output_aliases={1: 0},
        compiler_params=pltpu.CompilerParams(vmem_limit_bytes=12 * MIB),
        cost_estimate=pl.CostEstimate(
            flops=2 * tile_rows * tile_cols,
            bytes_accessed=16 * tile_rows * tile_cols,
            transcendentals=0,
        ),
        name="borders",
    )(offsets, tile, *strips)


def partner(index, kind):
    return index ^ 1 if kind == 0 else ((index + 1) ^ 1) - 1


def route(edge, rows, cols):
    down, across = edge
    pairs = []
    for r in range(rows):
        to_row = partner(r, down[1]) if down else r
        for c in range(cols):
            to_col = partner(c, across[1]) if across else c
            if 0 <= to_row < rows and 0 <= to_col < cols:
                pairs.append((r * cols + c, to_row * cols + to_col))
    return pairs


def exchanged(block, axes, between=None):
    for axis in axes:
        size = lax.axis_size(axis)
        if size & (size - 1):
            block = lax.psum(block, axis)
            continue
        for step in [1 << k for k in range(size.bit_length() - 1)]:
            own = block.astype(bf16)
            other = lax.ppermute(own, axis, [(i, i ^ step) for i in range(size)])
            if between is not None:
                other, between = between(other), None
            block = own.astype(f32) + other.astype(f32)
    return block


def shards(probe, object_re, object_im, phases, centres, occupied, measured):
    size = probe.shape[1]
    half = size // 2
    rows, cols = lax.axis_size("row"), lax.axis_size("col")
    sections = lax.axis_size("depth")
    assert sections == 2 and object_re.shape[0] == 1
    here = lax.axis_index("depth").astype(jnp.int32)
    row_at = lax.axis_index("row").astype(jnp.int32)
    tile_rows, tile_cols = object_re.shape[1:]
    batches, slots = centres.shape[2:4]
    spots = batches * slots
    count = spots // sections

    places = centres.reshape(2 * spots)
    slot_ids = jnp.arange(slots, dtype=jnp.int32)
    live = (slot_ids[None, :] < occupied[0, 0][:, None]).astype(jnp.int32)
    my_places = lax.dynamic_index_in_dim(
        centres.reshape(count, sections, 2), here, 1, False
    ).reshape(2 * count)
    my_live = lax.dynamic_index_in_dim(live.reshape(count, sections), here, 1, False)
    live = live.reshape(spots)
    frames = lax.dynamic_index_in_dim(
        measured.reshape(count, sections, size, size), here, 1, False
    )

    names, tile_at, padded_at = [], [], []
    for axis, extent, own, length in (
        ("row", rows, row_at, tile_rows),
        ("col", cols, lax.axis_index("col").astype(jnp.int32), tile_cols),
    ):
        for kind in range(min(2, extent - 1)):
            forward = own % 2 == kind
            names.append((axis, kind))
            tile_at.append(jnp.where(forward, length - half, 0))
            padded_at.append(jnp.where(forward, length + half, 0))
    downs = [key for key in names if key[0] == "row"]
    acrosses = [key for key in names if key[0] == "col"]
    edges = [(key, None) for key in downs] + [(None, key) for key in acrosses]
    edges += [(down, across) for down in downs for across in acrosses]
    paths = [route(edge, rows, cols) for edge in edges]
    both = ("row", "col")

    def numbers(*values):
        return jnp.stack(values).astype(jnp.int32)

    padded_at = numbers(*padded_at, here)
    own = pack(numbers(*tile_at, here), object_re, object_im, edges, names, half)
    strips = [lax.ppermute(strip, both, path) for strip, path in zip(own, paths)]
    kern, sorted_frames, waves = prepare(my_places, probe, phases, frames)
    mine, other = gather(
        places, padded_at, object_re, object_im, waves, edges, names, strips, size
    )
    across_depth = [(i, 1 - i) for i in range(sections)]
    theirs = lax.ppermute(other, "depth", across_depth)
    keep, send, pulled_keep, pulled_send = chain(
        my_places, my_live, here.reshape(1), kern, mine, theirs, sorted_frames, waves, 2
    )
    arrived = lax.ppermute(send, "depth", across_depth)
    pulled = pulled_keep + lax.ppermute(pulled_send, "depth", across_depth)

    tile, *own = scatter(
        places, live, padded_at, keep, arrived, edges, names, tile_rows, tile_cols
    )

    def after_scatter(other):
        return lax.optimization_barrier((other, *own))[0]

    probe_share = exchanged(pulled, ("row", "col"), after_scatter)
    added = [lax.ppermute(strip, both, path) for strip, path in zip(own, paths)]
    if rows == 2:
        first_row = jnp.where(row_at == 0, 0, half)
    else:
        first_row = jnp.int32(half if downs else 0)
    gradient = add_borders(numbers(*tile_at, first_row), tile, edges, names, added, half)
    return (gradient[:, None], probe_share)


def solution(mesh):
    in_specs = (
        P(),
        P("depth", "row", "col"),
        P("depth", "row", "col"),
        P(),
        P("row", "col", None, None, None),
        P("row", "col", None),
        P("row", "col", None, None, None, None),
    )
    out_specs = (P(None, "depth", "row", "col"), P(None, "depth", None))
    return jax.shard_map(shards, mesh=mesh, in_specs=in_specs, out_specs=out_specs, check_vma=False)
```

```python
import functools

import jax
import jax.numpy as jnp
import numpy as np
from jax import lax
from jax.experimental import pallas as pl
from jax.experimental.pallas import tpu as pltpu
from jax.sharding import PartitionSpec as P

f32 = jnp.float32
bf16 = jnp.bfloat16
ROWS = 16
LANES = 128
ANY = pl.BlockSpec(memory_space=pl.ANY)
HBM = pl.BlockSpec(memory_space=pltpu.HBM)
SMEM = pl.BlockSpec(memory_space=pltpu.SMEM)
MIB = 1024 * 1024


def dft_tables(size):
    half = size // 2
    rows = np.arange(half)[:, None]
    cols = np.arange(half)[None, :]

    def packed(turns):
        angle = -2.0 * np.pi * (turns % size) / size
        re, im = np.cos(angle) / np.sqrt(size), np.sin(angle) / np.sqrt(size)
        return np.block([[re, im], [-im, re]])

    even, odd = packed(rows * 2 * cols), packed(rows * (2 * cols + 1))
    full = np.stack([even, odd, even.T, odd.T]).astype(np.float32)
    high = full.astype(jnp.bfloat16)
    low = (full - high.astype(np.float32)).astype(jnp.bfloat16)
    return np.stack([high, low], axis=1)


def sorting_table(size):
    order = np.concatenate([np.arange(0, size, 2), np.arange(1, size, 2)])
    table = np.zeros((size, size), np.float32)
    table[order, np.arange(size)] = 1.0
    return table.astype(jnp.bfloat16)


def split(x):
    high = x.astype(bf16)
    return high, (x - high.astype(f32)).astype(bf16)


def dot3(left, right):
    lhs = jnp.concatenate([left[0], left[0], left[1]], axis=1)
    rhs = jnp.concatenate([right[0], right[1], right[0]], axis=0)
    return jnp.dot(lhs, rhs, preferred_element_type=f32)


def rows_of(*parts):
    return jnp.concatenate(parts, axis=0)


def cols_of(*parts):
    return jnp.concatenate(parts, axis=1)


def prep_kernel(places, order_t, probe, *refs):
    step = pl.program_id(0)
    size = probe.shape[-1]
    half = size // 2
    blocks = size // LANES
    phases, frames = refs[:blocks], refs[blocks : 2 * blocks]
    kern, sorted_frames, waves = refs[2 * blocks :]

    def halved(parts, at):
        ids = [(at, pl.ds(start, half, stride=2), slice(None)) for start in range(2)]
        return rows_of(*(cols_of(*(part[i] for part in parts)) for i in ids))

    def in_order(rows):
        first, rest = split(rows)
        second, third = split(rows - first.astype(f32))
        table = order_t[...]
        return jnp.dot(
            cols_of(first, second, third), rows_of(table, table, table), preferred_element_type=f32
        )

    @pl.when(step == 0)
    def _():
        angles = in_order(halved(phases, 0))
        kern[0] = jnp.cos(angles)
        kern[1] = jnp.sin(angles)

    sorted_frames[0] = in_order(halved(frames, 0))
    down = places[2 * step] % ROWS
    across = places[2 * step + 1] % LANES
    for plane in range(2):
        moved = pltpu.roll(probe[plane], across, axis=1)
        waves[0, plane] = pltpu.roll(moved, down, axis=0)


def prepare(places, probe, phases, frames):
    count, size = frames.shape[0], phases.shape[-1]
    blocks = size // LANES
    full = lambda *shape: pl.BlockSpec(shape, lambda i: (0,) * len(shape))
    return pl.pallas_call(
        prep_kernel,
        grid=(count,),
        in_specs=[
            SMEM,
            full(size, size),
            full(2, size, size),
            *(pl.BlockSpec((1, size, LANES), lambda i, b=b: (0, 0, b)) for b in range(blocks)),
            *(pl.BlockSpec((1, size, LANES), lambda i, b=b: (i, 0, b)) for b in range(blocks)),
        ],
        out_specs=[
            full(2, size, size),
            pl.BlockSpec((1, size, size), lambda i: (i, 0, 0)),
            pl.BlockSpec((1, 2, size, size), lambda i: (i, 0, 0, 0)),
        ],
        out_shape=[
            jax.ShapeDtypeStruct((2, size, size), f32),
            jax.ShapeDtypeStruct((count, size, size), f32),
            jax.ShapeDtypeStruct((count, 2, size, size), f32),
        ],
        compiler_params=pltpu.CompilerParams(vmem_limit_bytes=16 * MIB),
        cost_estimate=pl.CostEstimate(flops=0, bytes_accessed=0, transcendentals=0),
        name="prepare",
    )(
        places,
        jnp.asarray(sorting_table(size)),
        probe,
        *[phases[None]] * blocks,
        *[frames] * blocks,
    )


def span(key, offsets, names, half, whole):
    if key is None:
        return whole
    return pl.ds(pl.multiple_of(offsets[names.index(key)], half), half)


def pack_kernel(edges, names, half, offsets, tile_re, tile_im, *rest):
    strips, sems = rest[:-1], rest[-1]
    tile_rows, tile_cols = tile_re.shape[1:]
    copies = []
    for (down, across), strip in zip(edges, strips):
        rows = span(down, offsets, names, half, pl.ds(0, tile_rows))
        cols = span(across, offsets, names, half, pl.ds(0, tile_cols))
        for plane, tile in enumerate((tile_re, tile_im)):
            copies.append(
                pltpu.make_async_copy(
                    tile.at[0, rows, cols], strip.at[plane], sems.at[len(copies)]
                )
            )
            copies[-1].start()
    for copy in copies:
        copy.wait()


def strip_shapes(edges, tile_rows, tile_cols, half):
    return [
        jax.ShapeDtypeStruct(
            (2, half if down else tile_rows, half if across else tile_cols), bf16
        )
        for down, across in edges
    ]


def pack(offsets, tile_re, tile_im, edges, names, half):
    return pl.pallas_call(
        functools.partial(pack_kernel, edges, names, half),
        in_specs=[SMEM, HBM, HBM],
        out_specs=[ANY] * len(edges),
        out_shape=strip_shapes(edges, *tile_re.shape[1:], half),
        scratch_shapes=[pltpu.SemaphoreType.DMA((2 * len(edges),))],
        compiler_params=pltpu.CompilerParams(vmem_limit_bytes=4 * MIB),
        name="pack",
    )(offsets, tile_re, tile_im)


def spot(places, at):
    row, col = places[2 * at], places[2 * at + 1]
    down, across = row % ROWS, col % LANES
    return down, across, pl.multiple_of(row - down, ROWS), pl.multiple_of(col - across, LANES)


def gather_kernel(spots, edges, names, half, places, offsets, tile_re, tile_im, after, *rest):
    strips, (mine, other, padded, sems) = rest[:-4], rest[-4:]
    tile_rows, tile_cols = tile_re.shape[1:]
    size = mine.shape[-1]
    body = (pl.ds(half, tile_rows), pl.ds(half, tile_cols))
    copies = []

    def bring(source, target):
        copies.append(pltpu.make_async_copy(source, target, sems.at[len(copies)]))
        copies[-1].start()

    bring(tile_re.at[0], padded.at[(0,) + body])
    bring(tile_im.at[0], padded.at[(1,) + body])
    for (down, across), strip in zip(edges, strips):
        rows = span(down, offsets, names, half, body[0])
        cols = span(across, offsets, names, half, body[1])
        bring(strip, padded.at[:, rows, cols])
    for copy in copies:
        copy.wait()

    sections = 2
    lane = lax.broadcasted_iota(jnp.int32, (size, LANES), 1)
    top_lane = lax.broadcasted_iota(jnp.int32, (ROWS, LANES), 1)
    top_row = lax.broadcasted_iota(jnp.int32, (ROWS, size), 0)
    here = offsets[offsets.shape[0] - 1]

    def cut(at, target, place):
        down, across, top, left = spot(places, at)
        inner = size - LANES
        rest = pl.ds(pl.multiple_of(top + ROWS, ROWS), size - ROWS)

        def cols(start, width):
            return pl.ds(pl.multiple_of(left + start, LANES), width)

        for plane in range(2):
            target[place, plane, ROWS:, LANES:] = padded[plane, rest, cols(LANES, inner)]
            near = padded[plane, rest, cols(0, LANES)].astype(f32)
            far = padded[plane, rest, cols(size, LANES)].astype(f32)
            target[place, plane, ROWS:, :LANES] = jnp.where(
                lane[ROWS:] < across, far, near
            ).astype(bf16)
            rows = []
            for start in (0, size):
                block = padded[
                    plane, pl.ds(pl.multiple_of(top + start, ROWS), ROWS), cols(0, size + LANES)
                ].astype(f32)
                first = jnp.where(top_lane < across, block[:, size:], block[:, :LANES])
                rows.append(cols_of(first, block[:, LANES:size]))
            target[place, plane, :ROWS, :] = jnp.where(top_row < down, rows[1], rows[0]).astype(
                bf16
            )

    for place in range(spots // sections):
        cut(sections * place + 1 - here, other, place)
        cut(sections * place + here, mine, place)


def gather(places, offsets, tile_re, tile_im, after, edges, names, strips, size):
    half = size // 2
    spots = places.shape[0] // 2
    tile_rows, tile_cols = tile_re.shape[1:]
    shape = jax.ShapeDtypeStruct((spots // 2, 2, size, size), bf16)
    vmem = pl.BlockSpec(memory_space=pltpu.VMEM)
    return pl.pallas_call(
        functools.partial(gather_kernel, spots, edges, names, half),
        in_specs=[SMEM, SMEM, HBM, HBM] + [ANY] * (1 + len(strips)),
        out_specs=[vmem, vmem],
        out_shape=[shape, shape],
        scratch_shapes=[
            pltpu.VMEM((2, tile_rows + 2 * half, tile_cols + 2 * half), bf16),
            pltpu.SemaphoreType.DMA((2 + len(strips),)),
        ],
        compiler_params=pltpu.CompilerParams(vmem_limit_bytes=16 * MIB),
        name="gather",
    )(places, offsets, tile_re, tile_im, after, *strips)


def chain_kernel(
    group, places, live, here, tables, kern, mine, theirs, frames, waves,
    keep, send, pulled_keep, pulled_send, windows, middle, terms, pulled, sems,
):
    step = pl.program_id(0)
    steps = pl.num_programs(0)
    size = kern.shape[-1]
    half = size // 2
    me = here[0]

    def fetch(at, which):
        source, slot = ((mine, me), (theirs, 1 - me))[which]
        rows = pl.ds(at * group, group)
        return pltpu.make_async_copy(
            source.at[rows], windows.at[at, slot], sems.at[2 * at + which]
        )

    @pl.when(step == 0)
    def _():
        for at in range(windows.shape[0]):
            fetch(at, 0).start()
            fetch(at, 1).start()
        pulled[...] = jnp.zeros_like(pulled)

    fetch(step, 0).wait()
    fetch(step, 1).wait()

    def table(which):
        return tables[which, 0], tables[which, 1]

    group_ids = range(group)

    def forward(waves):
        halves = []
        for sign, which in ((1, 2), (-1, 3)):
            parts = []
            for pair in waves:
                if sign > 0:
                    parts.append(rows_of(*(x[:half] + x[half:] for x in pair)))
                else:
                    parts.append(rows_of(*(x[:half] - x[half:] for x in pair)))
            halves.append(dot3(table(which), split(cols_of(*parts))))
        outs = []
        for sign, which in ((1, 0), (-1, 1)):
            parts = []
            for at in group_ids:
                for out in halves:
                    x = out[:, at * size : (at + 1) * size]
                    if sign > 0:
                        x = x[:, :half] + x[:, half:]
                    else:
                        x = x[:, :half] - x[:, half:]
                    parts.append(cols_of(x[:half], x[half:]))
            outs.append(dot3(split(rows_of(*parts)), table(which)))
        return [[out[at * size : (at + 1) * size] for out in outs] for at in group_ids]

    def inverse(parts):
        first = dot3(split(rows_of(*(part[0] for part in parts))), table(2))
        second = dot3(split(rows_of(*(part[1] for part in parts))), table(3))
        evens, odds = [], []
        for at in group_ids:
            rows = slice(at * size, (at + 1) * size)
            plus, minus = first[rows] + second[rows], first[rows] - second[rows]
            re = cols_of(plus[:, :half], minus[:, :half])
            im = cols_of(plus[:, half:], minus[:, half:])
            evens.append(rows_of(re[:half], im[:half]))
            odds.append(rows_of(re[half:], im[half:]))
        first = dot3(table(0), split(cols_of(*evens)))
        second = dot3(table(1), split(cols_of(*odds)))
        outs = []
        for at in group_ids:
            cols = slice(at * size, (at + 1) * size)
            plus, minus = first[:, cols] + second[:, cols], first[:, cols] - second[:, cols]
            outs.append((rows_of(plus[:half], minus[:half]), rows_of(plus[half:], minus[half:])))
        return outs

    def propagate(waves, sign):
        kept = []
        for parts in forward(waves):
            outs = []
            for k, part in enumerate(parts):
                cols = slice(k * half, (k + 1) * half)
                kre, kim = kern[0, :, cols], kern[1, :, cols] * sign
                re, im = part[:, :half], part[:, half:]
                outs.append(cols_of(re * kre - im * kim, re * kim + im * kre))
            kept.append(outs)
        return inverse(kept)

    def product(left, right):
        return left[0] * right[0] - left[1] * right[1], left[0] * right[1] + left[1] * right[0]

    def conj_product(left, right):
        return left[0] * right[0] + left[1] * right[1], left[0] * right[1] - left[1] * right[0]

    def rounded(x):
        return x.astype(bf16).astype(f32)

    def window(slot, at):
        return windows[step, slot, at, 0].astype(f32), windows[step, slot, at, 1].astype(f32)

    def wave(at):
        return waves[at, 0], waves[at, 1]

    def passed(at):
        return middle[at, 0].astype(f32), middle[at, 1].astype(f32)

    outs = propagate([product(wave(at), window(0, at)) for at in group_ids], 1.0)
    for at in group_ids:
        middle[at, 0] = outs[at][0].astype(bf16)
        middle[at, 1] = outs[at][1].astype(bf16)

    far = forward([product(passed(at), window(1, at)) for at in group_ids])
    for at in group_ids:
        for k, part in enumerate(far[at]):
            re, im = part[:, :half], part[:, half:]
            misfit = re * re + im * im - frames[at, :, k * half : (k + 1) * half]
            far[at][k] = cols_of(re * misfit, im * misfit)
    pulls = []
    for at, chi in enumerate(inverse(far)):
        terms[1, at, 0], terms[1, at, 1] = conj_product(passed(at), chi)
        pulls.append(conj_product(window(1, at), chi))

    for at, chi in enumerate(propagate(pulls, -1.0)):
        chi = rounded(chi[0]), rounded(chi[1])
        terms[0, at, 0], terms[0, at, 1] = conj_product(wave(at), chi)
        spot_at = step * group + at
        up = (size - places[2 * spot_at] % ROWS) % size
        back_by = (size - places[2 * spot_at + 1] % LANES) % size
        weight = live[spot_at].astype(f32)
        for plane, value in enumerate(conj_product(window(0, at), chi)):
            value = pltpu.roll(pltpu.roll(value * weight, back_by, axis=1), up, axis=0)
            pulled[plane] += value

    keep[...] = terms[me]
    send[...] = terms[1 - me].astype(bf16)

    @pl.when(step == steps - 1)
    def _():
        share = pulled_keep.shape[1]
        for plane in range(2):
            pulled_keep[plane] = pulled[plane, pl.ds(pl.multiple_of(me * share, share), share), :]
            pulled_send[plane] = pulled[
                plane, pl.ds(pl.multiple_of((1 - me) * share, share), share), :
            ]


def chain(places, live, here, kern, mine, theirs, frames, waves, group):
    count, size = frames.shape[0], frames.shape[-1]
    full = lambda *shape: pl.BlockSpec(shape, lambda i: (0,) * len(shape))
    block = pl.BlockSpec((group, 2, size, size), lambda i: (i, 0, 0, 0))
    return pl.pallas_call(
        functools.partial(chain_kernel, group),
        grid=(count // group,),
        in_specs=[
            SMEM,
            SMEM,
            SMEM,
            full(4, 2, size, size),
            full(2, size, size),
            ANY,
            ANY,
            pl.BlockSpec((group, size, size), lambda i: (i, 0, 0)),
            block,
        ],
        out_specs=[block, block, full(2, size // 2, size), full(2, size // 2, size)],
        out_shape=[
            jax.ShapeDtypeStruct((count, 2, size, size), f32),
            jax.ShapeDtypeStruct((count, 2, size, size), bf16),
            jax.ShapeDtypeStruct((2, size // 2, size), f32),
            jax.ShapeDtypeStruct((2, size // 2, size), f32),
        ],
        scratch_shapes=[
            pltpu.VMEM((count // group, 2, group, 2, size, size), bf16),
            pltpu.VMEM((group, 2, size, size), bf16),
            pltpu.VMEM((2, group, 2, size, size), f32),
            pltpu.VMEM((2, size, size), f32),
            pltpu.SemaphoreType.DMA((2 * (count // group),)),
        ],
        compiler_params=pltpu.CompilerParams(vmem_limit_bytes=40 * MIB),
        name="chain",
    )(places, live, here, jnp.asarray(dft_tables(size)), kern, mine, theirs, frames, waves)


def scatter_kernel(edges, names, half, places, live, offsets, kept, arrived, tile, *rest):
    strips, (total, sems) = rest[:-2], rest[-2:]
    count, size = kept.shape[0], kept.shape[-1]
    tile_rows, tile_cols = tile.shape[1:]
    sections = 2
    here = offsets[offsets.shape[0] - 1]

    total[...] = jnp.zeros_like(total)
    lane = lax.broadcasted_iota(jnp.int32, (size, LANES), 1)
    row = lax.broadcasted_iota(jnp.int32, (ROWS, size + LANES), 0)

    def add(at, source, place):
        down, across, top, left = spot(places, at)
        wide = pl.ds(left, size + LANES)

        @pl.when(live[at] > 0)
        def _():
            for plane in range(2):
                value = source[place, plane].astype(f32)
                first = value[:, :LANES]
                inside = lane >= across
                value = cols_of(
                    jnp.where(inside, first, 0.0), value[:, LANES:], jnp.where(inside, 0.0, first)
                )
                first = value[:ROWS]
                inside = row >= down
                value = rows_of(
                    jnp.where(inside, first, 0.0), value[ROWS:], jnp.where(inside, 0.0, first)
                )
                total[plane, pl.ds(top, size + ROWS), wide] += value

    for source, owner in ((kept, here), (arrived, 1 - here)):
        for place in range(count):
            add(sections * place + owner, source, place)
    body = (pl.ds(half, tile_rows), pl.ds(half, tile_cols))
    copy = pltpu.make_async_copy(total.at[(slice(None),) + body], tile, sems.at[0])
    copy.start()
    for (down, across), strip in zip(edges, strips):
        rows = span(down, offsets, names, half, body[0])
        cols = span(across, offsets, names, half, body[1])
        for plane in range(2):
            strip[plane] = total[plane, rows, cols].astype(bf16)
    copy.wait()


def scatter(places, live, offsets, kept, arrived, edges, names, tile_rows, tile_cols):
    count, _, size, _ = kept.shape
    half = size // 2
    vmem = pl.BlockSpec(memory_space=pltpu.VMEM)
    return pl.pallas_call(
        functools.partial(scatter_kernel, edges, names, half),
        in_specs=[SMEM, SMEM, SMEM, vmem, vmem],
        out_specs=[HBM] + [vmem] * len(edges),
        out_shape=[jax.ShapeDtypeStruct((2, tile_rows, tile_cols), f32)]
        + strip_shapes(edges, tile_rows, tile_cols, half),
        scratch_shapes=[
            pltpu.VMEM((2, tile_rows + 2 * half, tile_cols + 2 * half), f32),
            pltpu.SemaphoreType.DMA((1,)),
        ],
        compiler_params=pltpu.CompilerParams(vmem_limit_bytes=20 * MIB),
        cost_estimate=pl.CostEstimate(
            flops=0, bytes_accessed=16 * tile_rows * tile_cols, transcendentals=0
        ),
        name="scatter",
    )(places, live, offsets, kept, arrived)


def border_kernel(edges, names, half, offsets, tile_in, part, other, *rest):
    strips, rest = rest[: len(edges)], rest[len(edges) :]
    tile, probe_share, bands, sides, in_sems, out_sems = rest
    tile_rows, tile_cols = tile.shape[1:]
    strips = dict(zip(edges, strips))
    downs = [key for key in names if key[0] == "row"]
    acrosses = [key for key in names if key[0] == "col"]
    tall = sides.shape[2]
    rest_rows = pl.ds(pl.multiple_of(offsets[len(names)], half), tall)
    spans = {key: span(key, offsets, names, half, None) for key in names}
    regions = []
    for k, key in enumerate(acrosses):
        regions.append((key, sides.at[k], rest_rows, spans[key]))
    for k, key in enumerate(downs):
        regions.append((key, bands.at[k], spans[key], pl.ds(0, tile_cols)))

    def copy(k, out):
        _, block, rows, cols = regions[k]
        if out:
            return pltpu.make_async_copy(block, tile.at[:, rows, cols], out_sems.at[k])
        return pltpu.make_async_copy(tile_in.at[:, rows, cols], block, in_sems.at[k])

    for k in range(len(regions)):
        copy(k, False).start()
    probe_share[...] = part[...].astype(f32) + other[...].astype(f32)
    for k, (key, block, rows, cols) in enumerate(regions):
        copy(k, False).wait()
        for plane in range(2):
            if key in downs:
                block[plane] += strips[(key, None)][plane].astype(f32)
                for across in acrosses:
                    block[plane, :, spans[across]] += strips[(key, across)][plane].astype(
                        f32
                    ) + strips[(None, across)][plane, rows, :].astype(f32)
            else:
                block[plane] += strips[(None, key)][plane, rows, :].astype(f32)
        copy(k, True).start()
    for k in range(len(regions)):
        copy(k, True).wait()


def add_borders(offsets, tile, probe_parts, edges, names, strips, half):
    vmem = pl.BlockSpec(memory_space=pltpu.VMEM)
    downs = sum(key[0] == "row" for key in names)
    acrosses = len(names) - downs
    tile_rows, tile_cols = tile.shape[1:]
    return pl.pallas_call(
        functools.partial(border_kernel, edges, names, half),
        in_specs=[SMEM, HBM] + [vmem] * (2 + len(strips)),
        out_specs=[HBM, vmem],
        out_shape=[
            jax.ShapeDtypeStruct(tile.shape, f32),
            jax.ShapeDtypeStruct(probe_parts[0].shape, f32),
        ],
        scratch_shapes=[
            pltpu.VMEM((max(downs, 1), 2, half, tile_cols), f32),
            pltpu.VMEM((max(acrosses, 1), 2, tile_rows - downs * half, half), f32),
            pltpu.SemaphoreType.DMA((max(len(names), 1),)),
            pltpu.SemaphoreType.DMA((max(len(names), 1),)),
        ],
        input_output_aliases={1: 0},
        compiler_params=pltpu.CompilerParams(vmem_limit_bytes=12 * MIB),
        cost_estimate=pl.CostEstimate(
            flops=2 * tile_rows * tile_cols,
            bytes_accessed=16 * tile_rows * tile_cols,
            transcendentals=0,
        ),
        name="borders",
    )(offsets, tile, *probe_parts, *strips)


def partner(index, kind):
    return index ^ 1 if kind == 0 else ((index + 1) ^ 1) - 1


def route(edge, rows, cols):
    down, across = edge
    pairs = []
    for r in range(rows):
        to_row = partner(r, down[1]) if down else r
        for c in range(cols):
            to_col = partner(c, across[1]) if across else c
            if 0 <= to_row < rows and 0 <= to_col < cols:
                pairs.append((r * cols + c, to_row * cols + to_col))
    return pairs


def doublings(axis):
    size = lax.axis_size(axis)
    assert size & (size - 1) == 0
    return size.bit_length() - 1


def shards(probe, object_re, object_im, phases, centres, occupied, measured):
    size = probe.shape[1]
    half = size // 2
    rows, cols = lax.axis_size("row"), lax.axis_size("col")
    sections = lax.axis_size("depth")
    assert sections == 2 and object_re.shape[0] == 1
    here = lax.axis_index("depth").astype(jnp.int32)
    row_at = lax.axis_index("row").astype(jnp.int32)
    tile_rows, tile_cols = object_re.shape[1:]
    batches, slots = centres.shape[2:4]
    spots = batches * slots
    count = spots // sections

    places = centres.reshape(2 * spots)
    slot_ids = jnp.arange(slots, dtype=jnp.int32)
    live = (slot_ids[None, :] < occupied[0, 0][:, None]).astype(jnp.int32)
    my_places = lax.dynamic_index_in_dim(
        centres.reshape(count, sections, 2), here, 1, False
    ).reshape(2 * count)
    my_live = lax.dynamic_index_in_dim(live.reshape(count, sections), here, 1, False)
    live = live.reshape(spots)
    frames = lax.dynamic_index_in_dim(
        measured.reshape(count, sections, size, size), here, 1, False
    )

    names, tile_at, padded_at = [], [], []
    for axis, extent, own, length in (
        ("row", rows, row_at, tile_rows),
        ("col", cols, lax.axis_index("col").astype(jnp.int32), tile_cols),
    ):
        for kind in range(min(2, extent - 1)):
            forward = own % 2 == kind
            names.append((axis, kind))
            tile_at.append(jnp.where(forward, length - half, 0))
            padded_at.append(jnp.where(forward, length + half, 0))
    downs = [key for key in names if key[0] == "row"]
    acrosses = [key for key in names if key[0] == "col"]
    edges = [(key, None) for key in downs] + [(None, key) for key in acrosses]
    edges += [(down, across) for down in downs for across in acrosses]
    paths = [route(edge, rows, cols) for edge in edges]
    both = ("row", "col")

    def numbers(*values):
        return jnp.stack(values).astype(jnp.int32)

    padded_at = numbers(*padded_at, here)
    tile_at = numbers(*tile_at, here)
    bulk = len(names)
    own = pack(tile_at, object_re, object_im, edges, names, half)
    strips = [lax.ppermute(strip, both, path) for strip, path in zip(own, paths)]
    kern, sorted_frames, waves = prepare(my_places, probe, phases, frames)
    mine, other = gather(
        places, padded_at, object_re, object_im, waves, edges, names, strips, size
    )
    across_depth = [(i, 1 - i) for i in range(sections)]
    theirs = lax.ppermute(other, "depth", across_depth)
    keep, send, pulled_keep, pulled_send = chain(
        my_places, my_live, here.reshape(1), kern, mine, theirs, sorted_frames, waves, 2
    )
    arrived = lax.ppermute(send, "depth", across_depth)
    pulled = pulled_keep + lax.ppermute(pulled_send, "depth", across_depth)

    tile, *own = scatter(
        places, live, padded_at, keep, arrived, edges, names, tile_rows, tile_cols
    )

    steps = [(axis, 1 << k) for axis in ("row", "col") for k in range(doublings(axis))]
    if len(steps) < 3:
        added = [lax.ppermute(strip, both, path) for strip, path in zip(own, paths)]
    for at, (axis, step) in enumerate(steps):
        mine = pulled.astype(bf16)
        theirs = lax.ppermute(mine, axis, [(i, i ^ step) for i in range(lax.axis_size(axis))])
        if at == len(steps) - 3:
            theirs, *own = lax.optimization_barrier((theirs, *own))
            added = [lax.ppermute(strip, both, path) for strip, path in zip(own, paths)]
        if at < len(steps) - 1:
            pulled = mine.astype(f32) + theirs.astype(f32)
    if rows == 2:
        first_row = jnp.where(row_at == 0, 0, half)
    else:
        first_row = jnp.int32(half if downs else 0)
    gradient, probe_share = add_borders(lax.dynamic_update_index_in_dim(tile_at, first_row.astype(jnp.int32), bulk, 0), tile, (mine, theirs), edges, names, added, half)
    return (gradient[:, None], probe_share)


def solution(mesh):
    in_specs = (
        P(),
        P("depth", "row", "col"),
        P("depth", "row", "col"),
        P(),
        P("row", "col", None, None, None),
        P("row", "col", None),
        P("row", "col", None, None, None, None),
    )
    out_specs = (P(None, "depth", "row", "col"), P(None, "depth", None))
    return jax.shard_map(shards, mesh=mesh, in_specs=in_specs, out_specs=out_specs, check_vma=False)
```

```python
import functools

import jax
import jax.numpy as jnp
import numpy as np
from jax import lax
from jax.experimental import pallas as pl
from jax.experimental.pallas import tpu as pltpu
from jax.sharding import PartitionSpec as P

f32 = jnp.float32
bf16 = jnp.bfloat16
ROWS = 16
LANES = 128
ANY = pl.BlockSpec(memory_space=pl.ANY)
HBM = pl.BlockSpec(memory_space=pltpu.HBM)
SMEM = pl.BlockSpec(memory_space=pltpu.SMEM)
MIB = 1024 * 1024


def dft_tables(size):
    half = size // 2
    rows = np.arange(half)[:, None]
    cols = np.arange(half)[None, :]

    def packed(turns):
        angle = -2.0 * np.pi * (turns % size) / size
        re, im = np.cos(angle) / np.sqrt(size), np.sin(angle) / np.sqrt(size)
        return np.block([[re, im], [-im, re]])

    even, odd = packed(rows * 2 * cols), packed(rows * (2 * cols + 1))
    full = np.stack([even, odd, even.T, odd.T]).astype(np.float32)
    high = full.astype(jnp.bfloat16)
    low = (full - high.astype(np.float32)).astype(jnp.bfloat16)
    return np.stack([high, low], axis=1)


def sorting_table(size):
    order = np.concatenate([np.arange(0, size, 2), np.arange(1, size, 2)])
    table = np.zeros((size, size), np.float32)
    table[order, np.arange(size)] = 1.0
    return table.astype(jnp.bfloat16)


def split(x):
    high = x.astype(bf16)
    return high, (x - high.astype(f32)).astype(bf16)


def dot3(left, right):
    lhs = jnp.concatenate([left[0], left[0], left[1]], axis=1)
    rhs = jnp.concatenate([right[0], right[1], right[0]], axis=0)
    return jnp.dot(lhs, rhs, preferred_element_type=f32)


def rows_of(*parts):
    return jnp.concatenate(parts, axis=0)


def cols_of(*parts):
    return jnp.concatenate(parts, axis=1)


def prep_kernel(places, order_t, after, probe, *refs):
    step = pl.program_id(0)
    size = probe.shape[-1]
    half = size // 2
    blocks = size // LANES
    phases, frames = refs[:blocks], refs[blocks : 2 * blocks]
    kern, sorted_frames, waves = refs[2 * blocks :]

    def halved(parts, at):
        ids = [(at, pl.ds(start, half, stride=2), slice(None)) for start in range(2)]
        return rows_of(*(cols_of(*(part[i] for part in parts)) for i in ids))

    def in_order(rows):
        first, rest = split(rows)
        second, third = split(rows - first.astype(f32))
        table = order_t[...]
        return jnp.dot(
            cols_of(first, second, third), rows_of(table, table, table), preferred_element_type=f32
        )

    @pl.when(step == 0)
    def _():
        angles = in_order(halved(phases, 0))
        kern[0] = jnp.cos(angles)
        kern[1] = jnp.sin(angles)

    sorted_frames[0] = in_order(halved(frames, 0))
    down = places[2 * step] % ROWS
    across = places[2 * step + 1] % LANES
    for plane in range(2):
        moved = pltpu.roll(probe[plane], across, axis=1)
        waves[0, plane] = pltpu.roll(moved, down, axis=0)


def prepare(places, after, probe, phases, frames):
    count, size = frames.shape[0], phases.shape[-1]
    blocks = size // LANES
    full = lambda *shape: pl.BlockSpec(shape, lambda i: (0,) * len(shape))
    return pl.pallas_call(
        prep_kernel,
        grid=(count,),
        in_specs=[
            SMEM,
            full(size, size),
            ANY,
            full(2, size, size),
            *(pl.BlockSpec((1, size, LANES), lambda i, b=b: (0, 0, b)) for b in range(blocks)),
            *(pl.BlockSpec((1, size, LANES), lambda i, b=b: (i, 0, b)) for b in range(blocks)),
        ],
        out_specs=[
            full(2, size, size),
            pl.BlockSpec((1, size, size), lambda i: (i, 0, 0)),
            pl.BlockSpec((1, 2, size, size), lambda i: (i, 0, 0, 0)),
        ],
        out_shape=[
            jax.ShapeDtypeStruct((2, size, size), f32),
            jax.ShapeDtypeStruct((count, size, size), f32),
            jax.ShapeDtypeStruct((count, 2, size, size), f32),
        ],
        compiler_params=pltpu.CompilerParams(vmem_limit_bytes=16 * MIB),
        cost_estimate=pl.CostEstimate(flops=0, bytes_accessed=0, transcendentals=0),
        name="prepare",
    )(
        places,
        jnp.asarray(sorting_table(size)),
        after,
        probe,
        *[phases[None]] * blocks,
        *[frames] * blocks,
    )


def span(key, offsets, names, half, whole):
    if key is None:
        return whole
    return pl.ds(pl.multiple_of(offsets[names.index(key)], half), half)


def pack_kernel(edges, names, half, offsets, tile_re, tile_im, *rest):
    strips, sems = rest[:-1], rest[-1]
    tile_rows, tile_cols = tile_re.shape[1:]
    copies = []
    for (down, across), strip in zip(edges, strips):
        rows = span(down, offsets, names, half, pl.ds(0, tile_rows))
        cols = span(across, offsets, names, half, pl.ds(0, tile_cols))
        for plane, tile in enumerate((tile_re, tile_im)):
            copies.append(
                pltpu.make_async_copy(
                    tile.at[0, rows, cols], strip.at[plane], sems.at[len(copies)]
                )
            )
            copies[-1].start()
    for copy in copies:
        copy.wait()


def strip_shapes(edges, tile_rows, tile_cols, half):
    return [
        jax.ShapeDtypeStruct(
            (2, half if down else tile_rows, half if across else tile_cols), bf16
        )
        for down, across in edges
    ]


def pack(offsets, tile_re, tile_im, edges, names, half):
    vmem = pl.BlockSpec(memory_space=pltpu.VMEM)
    return pl.pallas_call(
        functools.partial(pack_kernel, edges, names, half),
        in_specs=[SMEM, HBM, HBM],
        out_specs=[vmem] * len(edges),
        out_shape=strip_shapes(edges, *tile_re.shape[1:], half),
        scratch_shapes=[pltpu.SemaphoreType.DMA((2 * len(edges),))],
        compiler_params=pltpu.CompilerParams(vmem_limit_bytes=56 * MIB),
        name="pack",
    )(offsets, tile_re, tile_im)


def spot(places, at):
    row, col = places[2 * at], places[2 * at + 1]
    down, across = row % ROWS, col % LANES
    return down, across, pl.multiple_of(row - down, ROWS), pl.multiple_of(col - across, LANES)


def gather_kernel(spots, edges, names, half, places, offsets, tile_re, tile_im, *rest):
    strips, (mine, other, padded, sems) = rest[:-4], rest[-4:]
    tile_rows, tile_cols = tile_re.shape[1:]
    size = mine.shape[-1]
    body = (pl.ds(half, tile_rows), pl.ds(half, tile_cols))
    copies = []

    def bring(source, target):
        copies.append(pltpu.make_async_copy(source, target, sems.at[len(copies)]))
        copies[-1].start()

    bring(tile_re.at[0], padded.at[(0,) + body])
    bring(tile_im.at[0], padded.at[(1,) + body])
    for (down, across), strip in zip(edges, strips):
        rows = span(down, offsets, names, half, body[0])
        cols = span(across, offsets, names, half, body[1])
        bring(strip, padded.at[:, rows, cols])
    for copy in copies:
        copy.wait()

    sections = 2
    lane = lax.broadcasted_iota(jnp.int32, (size, LANES), 1)
    top_lane = lax.broadcasted_iota(jnp.int32, (ROWS, LANES), 1)
    top_row = lax.broadcasted_iota(jnp.int32, (ROWS, size), 0)
    here = offsets[offsets.shape[0] - 1]

    def cut(at, target, place):
        down, across, top, left = spot(places, at)
        inner = size - LANES
        rest = pl.ds(pl.multiple_of(top + ROWS, ROWS), size - ROWS)

        def cols(start, width):
            return pl.ds(pl.multiple_of(left + start, LANES), width)

        for plane in range(2):
            target[place, plane, ROWS:, LANES:] = padded[plane, rest, cols(LANES, inner)]
            near = padded[plane, rest, cols(0, LANES)].astype(f32)
            far = padded[plane, rest, cols(size, LANES)].astype(f32)
            target[place, plane, ROWS:, :LANES] = jnp.where(
                lane[ROWS:] < across, far, near
            ).astype(bf16)
            rows = []
            for start in (0, size):
                block = padded[
                    plane, pl.ds(pl.multiple_of(top + start, ROWS), ROWS), cols(0, size + LANES)
                ].astype(f32)
                first = jnp.where(top_lane < across, block[:, size:], block[:, :LANES])
                rows.append(cols_of(first, block[:, LANES:size]))
            target[place, plane, :ROWS, :] = jnp.where(top_row < down, rows[1], rows[0]).astype(
                bf16
            )

    for place in range(spots // sections):
        cut(sections * place + 1 - here, other, place)
        cut(sections * place + here, mine, place)


def gather(places, offsets, tile_re, tile_im, edges, names, strips, size):
    half = size // 2
    spots = places.shape[0] // 2
    tile_rows, tile_cols = tile_re.shape[1:]
    shape = jax.ShapeDtypeStruct((spots // 2, 2, size, size), bf16)
    vmem = pl.BlockSpec(memory_space=pltpu.VMEM)
    return pl.pallas_call(
        functools.partial(gather_kernel, spots, edges, names, half),
        in_specs=[SMEM, SMEM, HBM, HBM] + [ANY] * len(strips),
        out_specs=[vmem, vmem],
        out_shape=[shape, shape],
        scratch_shapes=[
            pltpu.VMEM((2, tile_rows + 2 * half, tile_cols + 2 * half), bf16),
            pltpu.SemaphoreType.DMA((2 + len(strips),)),
        ],
        compiler_params=pltpu.CompilerParams(vmem_limit_bytes=16 * MIB),
        name="gather",
    )(places, offsets, tile_re, tile_im, *strips)


def chain_kernel(
    group, places, live, here, tables, kern, mine, theirs, frames, waves,
    keep, send, pulled_keep, pulled_send, windows, middle, terms, pulled, sems,
):
    step = pl.program_id(0)
    steps = pl.num_programs(0)
    size = kern.shape[-1]
    half = size // 2
    me = here[0]

    def fetch(at, which):
        source, slot = ((mine, me), (theirs, 1 - me))[which]
        rows = pl.ds(at * group, group)
        return pltpu.make_async_copy(
            source.at[rows], windows.at[at, slot], sems.at[2 * at + which]
        )

    @pl.when(step == 0)
    def _():
        for at in range(windows.shape[0]):
            fetch(at, 0).start()
            fetch(at, 1).start()
        pulled[...] = jnp.zeros_like(pulled)

    fetch(step, 0).wait()
    fetch(step, 1).wait()

    def table(which):
        return tables[which, 0], tables[which, 1]

    group_ids = range(group)

    def forward(waves):
        halves = []
        for sign, which in ((1, 2), (-1, 3)):
            parts = []
            for pair in waves:
                if sign > 0:
                    parts.append(rows_of(*(x[:half] + x[half:] for x in pair)))
                else:
                    parts.append(rows_of(*(x[:half] - x[half:] for x in pair)))
            halves.append(dot3(table(which), split(cols_of(*parts))))
        outs = []
        for sign, which in ((1, 0), (-1, 1)):
            parts = []
            for at in group_ids:
                for out in halves:
                    x = out[:, at * size : (at + 1) * size]
                    if sign > 0:
                        x = x[:, :half] + x[:, half:]
                    else:
                        x = x[:, :half] - x[:, half:]
                    parts.append(cols_of(x[:half], x[half:]))
            outs.append(dot3(split(rows_of(*parts)), table(which)))
        return [[out[at * size : (at + 1) * size] for out in outs] for at in group_ids]

    def inverse(parts):
        first = dot3(split(rows_of(*(part[0] for part in parts))), table(2))
        second = dot3(split(rows_of(*(part[1] for part in parts))), table(3))
        evens, odds = [], []
        for at in group_ids:
            rows = slice(at * size, (at + 1) * size)
            plus, minus = first[rows] + second[rows], first[rows] - second[rows]
            re = cols_of(plus[:, :half], minus[:, :half])
            im = cols_of(plus[:, half:], minus[:, half:])
            evens.append(rows_of(re[:half], im[:half]))
            odds.append(rows_of(re[half:], im[half:]))
        first = dot3(table(0), split(cols_of(*evens)))
        second = dot3(table(1), split(cols_of(*odds)))
        outs = []
        for at in group_ids:
            cols = slice(at * size, (at + 1) * size)
            plus, minus = first[:, cols] + second[:, cols], first[:, cols] - second[:, cols]
            outs.append((rows_of(plus[:half], minus[:half]), rows_of(plus[half:], minus[half:])))
        return outs

    def propagate(waves, sign):
        kept = []
        for parts in forward(waves):
            outs = []
            for k, part in enumerate(parts):
                cols = slice(k * half, (k + 1) * half)
                kre, kim = kern[0, :, cols], kern[1, :, cols] * sign
                re, im = part[:, :half], part[:, half:]
                outs.append(cols_of(re * kre - im * kim, re * kim + im * kre))
            kept.append(outs)
        return inverse(kept)

    def product(left, right):
        return left[0] * right[0] - left[1] * right[1], left[0] * right[1] + left[1] * right[0]

    def conj_product(left, right):
        return left[0] * right[0] + left[1] * right[1], left[0] * right[1] - left[1] * right[0]

    def rounded(x):
        return x.astype(bf16).astype(f32)

    def window(slot, at):
        return windows[step, slot, at, 0].astype(f32), windows[step, slot, at, 1].astype(f32)

    def wave(at):
        return waves[at, 0], waves[at, 1]

    def passed(at):
        return middle[at, 0].astype(f32), middle[at, 1].astype(f32)

    outs = propagate([product(wave(at), window(0, at)) for at in group_ids], 1.0)
    for at in group_ids:
        middle[at, 0] = outs[at][0].astype(bf16)
        middle[at, 1] = outs[at][1].astype(bf16)

    far = forward([product(passed(at), window(1, at)) for at in group_ids])
    for at in group_ids:
        for k, part in enumerate(far[at]):
            re, im = part[:, :half], part[:, half:]
            misfit = re * re + im * im - frames[at, :, k * half : (k + 1) * half]
            far[at][k] = cols_of(re * misfit, im * misfit)
    pulls = []
    for at, chi in enumerate(inverse(far)):
        terms[1, at, 0], terms[1, at, 1] = conj_product(passed(at), chi)
        pulls.append(conj_product(window(1, at), chi))

    for at, chi in enumerate(propagate(pulls, -1.0)):
        chi = rounded(chi[0]), rounded(chi[1])
        terms[0, at, 0], terms[0, at, 1] = conj_product(wave(at), chi)
        spot_at = step * group + at
        up = (size - places[2 * spot_at] % ROWS) % size
        back_by = (size - places[2 * spot_at + 1] % LANES) % size
        weight = live[spot_at].astype(f32)
        for plane, value in enumerate(conj_product(window(0, at), chi)):
            value = pltpu.roll(pltpu.roll(value * weight, back_by, axis=1), up, axis=0)
            pulled[plane] += value

    keep[...] = terms[me].astype(bf16)
    send[...] = terms[1 - me].astype(bf16)

    @pl.when(step == steps - 1)
    def _():
        share = pulled_keep.shape[1]
        for plane in range(2):
            pulled_keep[plane] = pulled[plane, pl.ds(pl.multiple_of(me * share, share), share), :]
            pulled_send[plane] = pulled[
                plane, pl.ds(pl.multiple_of((1 - me) * share, share), share), :
            ]


def chain(places, live, here, kern, mine, theirs, frames, waves, group):
    count, size = frames.shape[0], frames.shape[-1]
    full = lambda *shape: pl.BlockSpec(shape, lambda i: (0,) * len(shape))
    block = pl.BlockSpec((group, 2, size, size), lambda i: (i, 0, 0, 0))
    return pl.pallas_call(
        functools.partial(chain_kernel, group),
        grid=(count // group,),
        in_specs=[
            SMEM,
            SMEM,
            SMEM,
            full(4, 2, size, size),
            full(2, size, size),
            ANY,
            ANY,
            pl.BlockSpec((group, size, size), lambda i: (i, 0, 0)),
            block,
        ],
        out_specs=[block, block, full(2, size // 2, size), full(2, size // 2, size)],
        out_shape=[
            jax.ShapeDtypeStruct((count, 2, size, size), bf16),
            jax.ShapeDtypeStruct((count, 2, size, size), bf16),
            jax.ShapeDtypeStruct((2, size // 2, size), f32),
            jax.ShapeDtypeStruct((2, size // 2, size), f32),
        ],
        scratch_shapes=[
            pltpu.VMEM((count // group, 2, group, 2, size, size), bf16),
            pltpu.VMEM((group, 2, size, size), bf16),
            pltpu.VMEM((2, group, 2, size, size), f32),
            pltpu.VMEM((2, size, size), f32),
            pltpu.SemaphoreType.DMA((2 * (count // group),)),
        ],
        compiler_params=pltpu.CompilerParams(vmem_limit_bytes=40 * MIB),
        name="chain",
    )(places, live, here, jnp.asarray(dft_tables(size)), kern, mine, theirs, frames, waves)


def scatter_kernel(edges, names, half, places, live, offsets, kept, arrived, tile, *rest):
    strips, (total, sems) = rest[:-2], rest[-2:]
    count, size = kept.shape[0], kept.shape[-1]
    tile_rows, tile_cols = tile.shape[1:]
    sections = 2
    here = offsets[offsets.shape[0] - 1]

    total[...] = jnp.zeros_like(total)
    lane = lax.broadcasted_iota(jnp.int32, (size, LANES), 1)
    row = lax.broadcasted_iota(jnp.int32, (ROWS, size + LANES), 0)

    def add(at, source, place):
        down, across, top, left = spot(places, at)
        wide = pl.ds(left, size + LANES)

        @pl.when(live[at] > 0)
        def _():
            for plane in range(2):
                value = source[place, plane].astype(f32)
                first = value[:, :LANES]
                inside = lane >= across
                value = cols_of(
                    jnp.where(inside, first, 0.0), value[:, LANES:], jnp.where(inside, 0.0, first)
                )
                first = value[:ROWS]
                inside = row >= down
                value = rows_of(
                    jnp.where(inside, first, 0.0), value[ROWS:], jnp.where(inside, 0.0, first)
                )
                total[plane, pl.ds(top, size + ROWS), wide] += value

    for source, owner in ((kept, here), (arrived, 1 - here)):
        for place in range(count):
            add(sections * place + owner, source, place)
    body = (pl.ds(half, tile_rows), pl.ds(half, tile_cols))
    copy = pltpu.make_async_copy(total.at[(slice(None),) + body], tile, sems.at[0])
    copy.start()
    for (down, across), strip in zip(edges, strips):
        rows = span(down, offsets, names, half, body[0])
        cols = span(across, offsets, names, half, body[1])
        for plane in range(2):
            strip[plane] = total[plane, rows, cols].astype(bf16)
    for (down, acrosses), strip in zip(corner_keys(names), strips[len(edges) :]):
        rows = span(down, offsets, names, half, None)
        for k, across in enumerate(acrosses):
            cols = span(across, offsets, names, half, None)
            for plane in range(2):
                strip[plane, k] = total[plane, rows, cols].astype(bf16)
    copy.wait()


def corner_keys(names):
    acrosses = [key for key in names if key[0] == "col"]
    return [(key, acrosses) for key in names if key[0] == "row" and acrosses]


def scatter(places, live, offsets, kept, arrived, edges, names, tile_rows, tile_cols):
    count, _, size, _ = kept.shape
    half = size // 2
    corners = corner_keys(names)
    vmem = pl.BlockSpec(memory_space=pltpu.VMEM)
    return pl.pallas_call(
        functools.partial(scatter_kernel, edges, names, half),
        in_specs=[SMEM, SMEM, SMEM, vmem, vmem],
        out_specs=[HBM] + [vmem] * (len(edges) + len(corners)),
        out_shape=[jax.ShapeDtypeStruct((2, tile_rows, tile_cols), f32)]
        + strip_shapes(edges, tile_rows, tile_cols, half)
        + [jax.ShapeDtypeStruct((2, len(keys), half, half), bf16) for _, keys in corners],
        scratch_shapes=[
            pltpu.VMEM((2, tile_rows + 2 * half, tile_cols + 2 * half), f32),
            pltpu.SemaphoreType.DMA((1,)),
        ],
        compiler_params=pltpu.CompilerParams(vmem_limit_bytes=20 * MIB),
        cost_estimate=pl.CostEstimate(
            flops=0, bytes_accessed=16 * tile_rows * tile_cols, transcendentals=0
        ),
        name="scatter",
    )(places, live, offsets, kept, arrived)


def corner_kernel(names, half, offsets, *refs):
    corners = corner_keys(names)
    arrived, refs = refs[: len(corners)], refs[len(corners) :]
    ins, outs = refs[: len(refs) // 2], refs[len(refs) // 2 :]
    for k, (before, strip) in enumerate(zip(ins, outs)):
        strip[...] = before[...]
        for (down, _), block in zip(corners, arrived):
            rows = span(down, offsets, names, half, None)
            for plane in range(2):
                strip[plane, rows, :] = (
                    strip[plane, rows, :].astype(f32) + block[plane, k].astype(f32)
                ).astype(bf16)


def add_corners(offsets, strips, arrived, names, half):
    vmem = pl.BlockSpec(memory_space=pltpu.VMEM)
    return pl.pallas_call(
        functools.partial(corner_kernel, names, half),
        in_specs=[SMEM] + [vmem] * (len(arrived) + len(strips)),
        out_specs=[vmem] * len(strips),
        out_shape=[jax.ShapeDtypeStruct(strip.shape, bf16) for strip in strips],
        compiler_params=pltpu.CompilerParams(vmem_limit_bytes=8 * MIB),
        name="corners",
    )(offsets, *arrived, *strips)


def border_kernel(edges, names, half, offsets, tile_in, part, other, *rest):
    strips, rest = rest[: len(edges)], rest[len(edges) :]
    tile, probe_share, bands, sides, in_sems, out_sems = rest
    tile_rows, tile_cols = tile.shape[1:]
    strips = dict(zip(edges, strips))
    downs = [key for key in names if key[0] == "row"]
    acrosses = [key for key in names if key[0] == "col"]
    tall = sides.shape[2]
    rest_rows = pl.ds(pl.multiple_of(offsets[len(names)], half), tall)
    spans = {key: span(key, offsets, names, half, None) for key in names}
    regions = []
    for k, key in enumerate(acrosses):
        regions.append((key, sides.at[k], rest_rows, spans[key]))
    for k, key in enumerate(downs):
        regions.append((key, bands.at[k], spans[key], pl.ds(0, tile_cols)))

    def copy(k, out):
        _, block, rows, cols = regions[k]
        if out:
            return pltpu.make_async_copy(block, tile.at[:, rows, cols], out_sems.at[k])
        return pltpu.make_async_copy(tile_in.at[:, rows, cols], block, in_sems.at[k])

    for k in range(len(regions)):
        copy(k, False).start()
    probe_share[...] = part[...].astype(f32) + other[...].astype(f32)
    for k, (key, block, rows, cols) in enumerate(regions):
        copy(k, False).wait()
        for plane in range(2):
            if key in downs:
                block[plane] += strips[(key, None)][plane].astype(f32)
                for across in acrosses:
                    block[plane, :, spans[across]] += strips[(None, across)][
                        plane, rows, :
                    ].astype(f32)
            else:
                block[plane] += strips[(None, key)][plane, rows, :].astype(f32)
        copy(k, True).start()
    for k in range(len(regions)):
        copy(k, True).wait()


def add_borders(offsets, tile, probe_parts, edges, names, strips, half):
    vmem = pl.BlockSpec(memory_space=pltpu.VMEM)
    downs = sum(key[0] == "row" for key in names)
    acrosses = len(names) - downs
    tile_rows, tile_cols = tile.shape[1:]
    return pl.pallas_call(
        functools.partial(border_kernel, edges, names, half),
        in_specs=[SMEM, HBM] + [vmem] * (2 + len(strips)),
        out_specs=[HBM, vmem],
        out_shape=[
            jax.ShapeDtypeStruct(tile.shape, f32),
            jax.ShapeDtypeStruct(probe_parts[0].shape, f32),
        ],
        scratch_shapes=[
            pltpu.VMEM((max(downs, 1), 2, half, tile_cols), f32),
            pltpu.VMEM((max(acrosses, 1), 2, tile_rows - downs * half, half), f32),
            pltpu.SemaphoreType.DMA((max(len(names), 1),)),
            pltpu.SemaphoreType.DMA((max(len(names), 1),)),
        ],
        input_output_aliases={1: 0},
        compiler_params=pltpu.CompilerParams(vmem_limit_bytes=12 * MIB),
        cost_estimate=pl.CostEstimate(
            flops=2 * tile_rows * tile_cols,
            bytes_accessed=16 * tile_rows * tile_cols,
            transcendentals=0,
        ),
        name="borders",
    )(offsets, tile, *probe_parts, *strips)


def partner(index, kind):
    return index ^ 1 if kind == 0 else ((index + 1) ^ 1) - 1


def route(edge, rows, cols):
    down, across = edge
    pairs = []
    for r in range(rows):
        to_row = partner(r, down[1]) if down else r
        for c in range(cols):
            to_col = partner(c, across[1]) if across else c
            if 0 <= to_row < rows and 0 <= to_col < cols:
                pairs.append((r * cols + c, to_row * cols + to_col))
    return pairs


def shards(probe, object_re, object_im, phases, centres, occupied, measured):
    size = probe.shape[1]
    half = size // 2
    rows, cols = lax.axis_size("row"), lax.axis_size("col")
    sections = lax.axis_size("depth")
    assert sections == 2 and object_re.shape[0] == 1
    here = lax.axis_index("depth").astype(jnp.int32)
    row_at = lax.axis_index("row").astype(jnp.int32)
    tile_rows, tile_cols = object_re.shape[1:]
    batches, slots = centres.shape[2:4]
    spots = batches * slots
    count = spots // sections

    places = centres.reshape(2 * spots)
    slot_ids = jnp.arange(slots, dtype=jnp.int32)
    live = (slot_ids[None, :] < occupied[0, 0][:, None]).astype(jnp.int32)
    my_places = lax.dynamic_index_in_dim(
        centres.reshape(count, sections, 2), here, 1, False
    ).reshape(2 * count)
    my_live = lax.dynamic_index_in_dim(live.reshape(count, sections), here, 1, False)
    live = live.reshape(spots)
    frames = lax.dynamic_index_in_dim(
        measured.reshape(count, sections, size, size), here, 1, False
    )

    names, tile_at, padded_at = [], [], []
    for axis, extent, own, length in (
        ("row", rows, row_at, tile_rows),
        ("col", cols, lax.axis_index("col").astype(jnp.int32), tile_cols),
    ):
        for kind in range(min(2, extent - 1)):
            forward = own % 2 == kind
            names.append((axis, kind))
            tile_at.append(jnp.where(forward, length - half, 0))
            padded_at.append(jnp.where(forward, length + half, 0))
    downs = [key for key in names if key[0] == "row"]
    acrosses = [key for key in names if key[0] == "col"]
    edges = [(key, None) for key in downs] + [(None, key) for key in acrosses]
    outer, paths = edges, [route(edge, rows, cols) for edge in edges]
    edges = edges + [(down, across) for down in downs for across in acrosses]
    paths += [route(edge, rows, cols) for edge in edges[len(outer) :]]
    both = ("row", "col")

    def numbers(*values):
        return jnp.stack(values).astype(jnp.int32)

    padded_at = numbers(*padded_at, here)
    tile_at = numbers(*tile_at, here)
    bulk = len(names)
    own = pack(tile_at, object_re, object_im, edges, names, half)
    strips = [lax.ppermute(strip, both, path) for strip, path in zip(own, paths)]
    mine, other = gather(places, padded_at, object_re, object_im, edges, names, strips, size)
    across_depth = [(i, 1 - i) for i in range(sections)]
    theirs = lax.ppermute(other, "depth", across_depth)
    kern, sorted_frames, waves = prepare(my_places, mine, probe, phases, frames)
    keep, send, pulled_keep, pulled_send = chain(
        my_places, my_live, here.reshape(1), kern, mine, theirs, sorted_frames, waves, count
    )
    arrived = lax.ppermute(send, "depth", across_depth)
    pulled = pulled_keep + lax.ppermute(pulled_send, "depth", across_depth)

    tile, *own = scatter(
        places, live, padded_at, keep, arrived, outer, names, tile_rows, tile_cols
    )

    bits = rows.bit_length() + cols.bit_length() - 2
    assert rows * cols == 1 << bits
    flips = [cols << k for k in range(rows.bit_length() - 1)]
    flips += [1 << k for k in range(cols.bit_length() - 1)]
    early, late = flips[: max(bits - 2, 0)], flips[max(bits - 2, 0) :]
    rounds = [early[k : k + 2] for k in range(0, len(early), 2)] + [[flip] for flip in late]

    def fetch(block, flip):
        return lax.ppermute(block, both, [(i, i ^ flip) for i in range(rows * cols)])

    def sent(own):
        own, corners = own[: len(outer)], own[len(outer) :]
        if corners:
            corners = [lax.ppermute(x, both, path) for x, path in zip(corners, paths)]
            own[len(downs) :] = add_corners(tile_at, own[len(downs) :], corners, names, half)
        return [lax.ppermute(strip, both, path) for strip, path in zip(own, paths)]

    added = None
    for at, flips in enumerate(rounds):
        mine = pulled.astype(bf16)
        theirs = [fetch(mine, flip) for flip in flips]
        if len(flips) == 2:
            theirs.append(fetch(mine, flips[0] ^ flips[1]))
        if added is None and at >= len(rounds) - 3:
            *theirs, own = lax.optimization_barrier((*theirs, own))
            added = sent(own)
        if at < len(rounds) - 1:
            sums = [part.astype(f32) for part in (mine, *theirs)]
            pulled = sums[0] + sums[1]
            if len(flips) == 2:
                pulled = pulled + (sums[2] + sums[3])
    (theirs,) = theirs
    if rows == 2:
        first_row = jnp.where(row_at == 0, 0, half)
    else:
        first_row = jnp.int32(half if downs else 0)
    gradient, probe_share = add_borders(lax.dynamic_update_index_in_dim(tile_at, first_row.astype(jnp.int32), bulk, 0), tile, (mine, theirs), outer, names, added, half)
    return (gradient[:, None], probe_share)


def solution(mesh):
    in_specs = (
        P(),
        P("depth", "row", "col"),
        P("depth", "row", "col"),
        P(),
        P("row", "col", None, None, None),
        P("row", "col", None),
        P("row", "col", None, None, None, None),
    )
    out_specs = (P(None, "depth", "row", "col"), P(None, "depth", None))
    return jax.shard_map(shards, mesh=mesh, in_specs=in_specs, out_specs=out_specs, check_vma=False)
```

```python
import functools

import jax
import jax.numpy as jnp
import numpy as np
from jax import lax
from jax.experimental import pallas as pl
from jax.experimental.pallas import tpu as pltpu
from jax.sharding import PartitionSpec as P

f32 = jnp.float32
bf16 = jnp.bfloat16
ROWS = 16
LANES = 128
ANY = pl.BlockSpec(memory_space=pl.ANY)
HBM = pl.BlockSpec(memory_space=pltpu.HBM)
SMEM = pl.BlockSpec(memory_space=pltpu.SMEM)
MIB = 1024 * 1024


def dft_tables(size):
    half = size // 2
    rows = np.arange(half)[:, None]
    cols = np.arange(half)[None, :]

    def packed(turns):
        angle = -2.0 * np.pi * (turns % size) / size
        re, im = np.cos(angle) / np.sqrt(size), np.sin(angle) / np.sqrt(size)
        return np.block([[re, im], [-im, re]])

    even, odd = packed(rows * 2 * cols), packed(rows * (2 * cols + 1))
    full = np.stack([even, odd, even.T, odd.T]).astype(np.float32)
    high = full.astype(jnp.bfloat16)
    low = (full - high.astype(np.float32)).astype(jnp.bfloat16)
    return np.stack([high, low], axis=1)


def sorting_table(size):
    order = np.concatenate([np.arange(0, size, 2), np.arange(1, size, 2)])
    table = np.zeros((size, size), np.float32)
    table[order, np.arange(size)] = 1.0
    return table.astype(jnp.bfloat16)


def split(x):
    high = x.astype(bf16)
    return high, (x - high.astype(f32)).astype(bf16)


def dot3(left, right):
    lhs = jnp.concatenate([left[0], left[0], left[1]], axis=1)
    rhs = jnp.concatenate([right[0], right[1], right[0]], axis=0)
    return jnp.dot(lhs, rhs, preferred_element_type=f32)


def rows_of(*parts):
    return jnp.concatenate(parts, axis=0)


def cols_of(*parts):
    return jnp.concatenate(parts, axis=1)


def prep_kernel(places, offsets, order_t, after, probe, *refs):
    step = pl.program_id(0)
    size = probe.shape[-1]
    half = size // 2
    blocks = size // LANES
    phases, frames = refs[:blocks], refs[blocks : 2 * blocks]
    kern, sorted_frames, waves = refs[2 * blocks :]

    def halved(parts, at):
        ids = [at + (pl.ds(start, half, stride=2), slice(None)) for start in range(2)]
        return rows_of(*(cols_of(*(part[i] for part in parts)) for i in ids))

    def in_order(rows):
        first, rest = split(rows)
        second, third = split(rows - first.astype(f32))
        table = order_t[...]
        return jnp.dot(
            cols_of(first, second, third), rows_of(table, table, table), preferred_element_type=f32
        )

    @pl.when(step == 0)
    def _():
        angles = in_order(halved(phases, ()))
        kern[0] = jnp.cos(angles)
        kern[1] = jnp.sin(angles)

    sorted_frames[0] = in_order(halved(frames, (0, 0)))
    at = 2 * step + offsets[offsets.shape[0] - 1]
    down = places[2 * at] % ROWS
    across = places[2 * at + 1] % LANES
    for plane in range(2):
        moved = pltpu.roll(probe[plane], across, axis=1)
        waves[0, plane] = pltpu.roll(moved, down, axis=0)


def prepare(places, offsets, after, probe, phases, frames):
    count, sections, size = frames.shape[:3]
    blocks = size // LANES
    last = offsets.shape[0] - 1
    full = lambda *shape: pl.BlockSpec(shape, lambda i, p, o: (0,) * len(shape))
    return pl.pallas_call(
        prep_kernel,
        grid_spec=pltpu.PrefetchScalarGridSpec(
            num_scalar_prefetch=2,
            grid=(count,),
            in_specs=[
                full(size, size),
                ANY,
                full(2, size, size),
                *(
                    pl.BlockSpec((size, LANES), lambda i, p, o, b=b: (0, b))
                    for b in range(blocks)
                ),
                *(
                    pl.BlockSpec((1, 1, size, LANES), lambda i, p, o, b=b: (i, o[last], 0, b))
                    for b in range(blocks)
                ),
            ],
            out_specs=[
                full(2, size, size),
                pl.BlockSpec((1, size, size), lambda i, p, o: (i, 0, 0)),
                pl.BlockSpec((1, 2, size, size), lambda i, p, o: (i, 0, 0, 0)),
            ],
        ),
        out_shape=[
            jax.ShapeDtypeStruct((2, size, size), f32),
            jax.ShapeDtypeStruct((count, size, size), f32),
            jax.ShapeDtypeStruct((count, 2, size, size), f32),
        ],
        compiler_params=pltpu.CompilerParams(vmem_limit_bytes=16 * MIB),
        cost_estimate=pl.CostEstimate(flops=0, bytes_accessed=0, transcendentals=0),
        name="prepare",
    )(
        places,
        offsets,
        jnp.asarray(sorting_table(size)),
        after,
        probe,
        *[phases] * blocks,
        *[frames] * blocks,
    )


def span(key, offsets, names, half, whole):
    if key is None:
        return whole
    return pl.ds(pl.multiple_of(offsets[names.index(key)], half), half)


def pack_kernel(edges, names, half, offsets, tile_re, tile_im, *rest):
    strips, sems = rest[:-1], rest[-1]
    tile_rows, tile_cols = tile_re.shape[1:]
    copies = []
    for (down, across), strip in zip(edges, strips):
        rows = span(down, offsets, names, half, pl.ds(0, tile_rows))
        cols = span(across, offsets, names, half, pl.ds(0, tile_cols))
        for plane, tile in enumerate((tile_re, tile_im)):
            copies.append(
                pltpu.make_async_copy(
                    tile.at[0, rows, cols], strip.at[plane], sems.at[len(copies)]
                )
            )
            copies[-1].start()
    for copy in copies:
        copy.wait()


def strip_shapes(edges, tile_rows, tile_cols, half):
    return [
        jax.ShapeDtypeStruct(
            (2, half if down else tile_rows, half if across else tile_cols), bf16
        )
        for down, across in edges
    ]


def pack(offsets, tile_re, tile_im, edges, names, half):
    return pl.pallas_call(
        functools.partial(pack_kernel, edges, names, half),
        in_specs=[SMEM, HBM, HBM],
        out_specs=[ANY] * len(edges),
        out_shape=strip_shapes(edges, *tile_re.shape[1:], half),
        scratch_shapes=[pltpu.SemaphoreType.DMA((2 * len(edges),))],
        compiler_params=pltpu.CompilerParams(vmem_limit_bytes=4 * MIB),
        name="pack",
    )(offsets, tile_re, tile_im)


def spot(places, at):
    row, col = places[2 * at], places[2 * at + 1]
    down, across = row % ROWS, col % LANES
    return down, across, pl.multiple_of(row - down, ROWS), pl.multiple_of(col - across, LANES)


def is_live(occupied, places, at):
    slots = places.shape[0] // 2 // occupied.shape[0]
    return at % slots < occupied[at // slots]


def gather_kernel(spots, edges, names, half, places, offsets, tile_re, tile_im, *rest):
    strips, (mine, other, padded, sems) = rest[:-4], rest[-4:]
    tile_rows, tile_cols = tile_re.shape[1:]
    size = mine.shape[-1]
    body = (pl.ds(half, tile_rows), pl.ds(half, tile_cols))
    copies = []

    def bring(source, target):
        copies.append(pltpu.make_async_copy(source, target, sems.at[len(copies)]))
        copies[-1].start()

    bring(tile_re.at[0], padded.at[(0,) + body])
    bring(tile_im.at[0], padded.at[(1,) + body])
    for (down, across), strip in zip(edges, strips):
        rows = span(down, offsets, names, half, body[0])
        cols = span(across, offsets, names, half, body[1])
        bring(strip, padded.at[:, rows, cols])
    for copy in copies:
        copy.wait()

    sections = 2
    lane = lax.broadcasted_iota(jnp.int32, (size, LANES), 1)
    top_lane = lax.broadcasted_iota(jnp.int32, (ROWS, LANES), 1)
    top_row = lax.broadcasted_iota(jnp.int32, (ROWS, size), 0)
    here = offsets[offsets.shape[0] - 1]

    def cut(at, target, place):
        down, across, top, left = spot(places, at)
        inner = size - LANES
        rest = pl.ds(pl.multiple_of(top + ROWS, ROWS), size - ROWS)

        def cols(start, width):
            return pl.ds(pl.multiple_of(left + start, LANES), width)

        for plane in range(2):
            target[place, plane, ROWS:, LANES:] = padded[plane, rest, cols(LANES, inner)]
            near = padded[plane, rest, cols(0, LANES)].astype(f32)
            far = padded[plane, rest, cols(size, LANES)].astype(f32)
            target[place, plane, ROWS:, :LANES] = jnp.where(
                lane[ROWS:] < across, far, near
            ).astype(bf16)
            rows = []
            for start in (0, size):
                block = padded[
                    plane, pl.ds(pl.multiple_of(top + start, ROWS), ROWS), cols(0, size + LANES)
                ].astype(f32)
                first = jnp.where(top_lane < across, block[:, size:], block[:, :LANES])
                rows.append(cols_of(first, block[:, LANES:size]))
            target[place, plane, :ROWS, :] = jnp.where(top_row < down, rows[1], rows[0]).astype(
                bf16
            )

    for place in range(spots // sections):
        cut(sections * place + 1 - here, other, place)
        cut(sections * place + here, mine, place)


def gather(places, offsets, tile_re, tile_im, edges, names, strips, size):
    half = size // 2
    spots = places.shape[0] // 2
    tile_rows, tile_cols = tile_re.shape[1:]
    shape = jax.ShapeDtypeStruct((spots // 2, 2, size, size), bf16)
    vmem = pl.BlockSpec(memory_space=pltpu.VMEM)
    return pl.pallas_call(
        functools.partial(gather_kernel, spots, edges, names, half),
        in_specs=[SMEM, SMEM, HBM, HBM] + [ANY] * len(strips),
        out_specs=[vmem, vmem],
        out_shape=[shape, shape],
        scratch_shapes=[
            pltpu.VMEM((2, tile_rows + 2 * half, tile_cols + 2 * half), bf16),
            pltpu.SemaphoreType.DMA((2 + len(strips),)),
        ],
        compiler_params=pltpu.CompilerParams(vmem_limit_bytes=16 * MIB),
        name="gather",
    )(places, offsets, tile_re, tile_im, *strips)


def chain_kernel(
    group, places, occupied, offsets, tables, kern, mine, theirs, frames, waves,
    keep, send, pulled_keep, pulled_send, windows, middle, terms, pulled, sems,
):
    step = pl.program_id(0)
    steps = pl.num_programs(0)
    size = kern.shape[-1]
    half = size // 2
    me = offsets[offsets.shape[0] - 1]

    def fetch(at, which):
        source, slot = ((mine, me), (theirs, 1 - me))[which]
        rows = pl.ds(at * group, group)
        return pltpu.make_async_copy(
            source.at[rows], windows.at[at, slot], sems.at[2 * at + which]
        )

    @pl.when(step == 0)
    def _():
        for at in range(windows.shape[0]):
            fetch(at, 0).start()
            fetch(at, 1).start()
        pulled[...] = jnp.zeros_like(pulled)

    fetch(step, 0).wait()
    fetch(step, 1).wait()

    def table(which):
        return tables[which, 0], tables[which, 1]

    group_ids = range(group)

    def forward(waves):
        halves = []
        for sign, which in ((1, 2), (-1, 3)):
            parts = []
            for pair in waves:
                if sign > 0:
                    parts.append(rows_of(*(x[:half] + x[half:] for x in pair)))
                else:
                    parts.append(rows_of(*(x[:half] - x[half:] for x in pair)))
            halves.append(dot3(table(which), split(cols_of(*parts))))
        outs = []
        for sign, which in ((1, 0), (-1, 1)):
            parts = []
            for at in group_ids:
                for out in halves:
                    x = out[:, at * size : (at + 1) * size]
                    if sign > 0:
                        x = x[:, :half] + x[:, half:]
                    else:
                        x = x[:, :half] - x[:, half:]
                    parts.append(cols_of(x[:half], x[half:]))
            outs.append(dot3(split(rows_of(*parts)), table(which)))
        return [[out[at * size : (at + 1) * size] for out in outs] for at in group_ids]

    def inverse(parts):
        first = dot3(split(rows_of(*(part[0] for part in parts))), table(2))
        second = dot3(split(rows_of(*(part[1] for part in parts))), table(3))
        evens, odds = [], []
        for at in group_ids:
            rows = slice(at * size, (at + 1) * size)
            plus, minus = first[rows] + second[rows], first[rows] - second[rows]
            re = cols_of(plus[:, :half], minus[:, :half])
            im = cols_of(plus[:, half:], minus[:, half:])
            evens.append(rows_of(re[:half], im[:half]))
            odds.append(rows_of(re[half:], im[half:]))
        first = dot3(table(0), split(cols_of(*evens)))
        second = dot3(table(1), split(cols_of(*odds)))
        outs = []
        for at in group_ids:
            cols = slice(at * size, (at + 1) * size)
            plus, minus = first[:, cols] + second[:, cols], first[:, cols] - second[:, cols]
            outs.append((rows_of(plus[:half], minus[:half]), rows_of(plus[half:], minus[half:])))
        return outs

    def propagate(waves, sign):
        kept = []
        for parts in forward(waves):
            outs = []
            for k, part in enumerate(parts):
                cols = slice(k * half, (k + 1) * half)
                kre, kim = kern[0, :, cols], kern[1, :, cols] * sign
                re, im = part[:, :half], part[:, half:]
                outs.append(cols_of(re * kre - im * kim, re * kim + im * kre))
            kept.append(outs)
        return inverse(kept)

    def product(left, right):
        return left[0] * right[0] - left[1] * right[1], left[0] * right[1] + left[1] * right[0]

    def conj_product(left, right):
        return left[0] * right[0] + left[1] * right[1], left[0] * right[1] - left[1] * right[0]

    def rounded(x):
        return x.astype(bf16).astype(f32)

    def window(slot, at):
        return windows[step, slot, at, 0].astype(f32), windows[step, slot, at, 1].astype(f32)

    def wave(at):
        return waves[at, 0], waves[at, 1]

    def passed(at):
        return middle[at, 0].astype(f32), middle[at, 1].astype(f32)

    outs = propagate([product(wave(at), window(0, at)) for at in group_ids], 1.0)
    for at in group_ids:
        middle[at, 0] = outs[at][0].astype(bf16)
        middle[at, 1] = outs[at][1].astype(bf16)

    far = forward([product(passed(at), window(1, at)) for at in group_ids])
    for at in group_ids:
        for k, part in enumerate(far[at]):
            re, im = part[:, :half], part[:, half:]
            misfit = re * re + im * im - frames[at, :, k * half : (k + 1) * half]
            far[at][k] = cols_of(re * misfit, im * misfit)
    pulls = []
    for at, chi in enumerate(inverse(far)):
        terms[1, at, 0], terms[1, at, 1] = conj_product(passed(at), chi)
        pulls.append(conj_product(window(1, at), chi))

    for at, chi in enumerate(propagate(pulls, -1.0)):
        chi = rounded(chi[0]), rounded(chi[1])
        terms[0, at, 0], terms[0, at, 1] = conj_product(wave(at), chi)
        spot_at = 2 * (step * group + at) + me
        up = (size - places[2 * spot_at] % ROWS) % size
        back_by = (size - places[2 * spot_at + 1] % LANES) % size
        weight = is_live(occupied, places, spot_at).astype(f32)
        for plane, value in enumerate(conj_product(window(0, at), chi)):
            value = pltpu.roll(pltpu.roll(value * weight, back_by, axis=1), up, axis=0)
            pulled[plane] += value

    keep[...] = terms[me].astype(bf16)
    send[...] = terms[1 - me].astype(bf16)

    @pl.when(step == steps - 1)
    def _():
        share = pulled_keep.shape[1]
        for plane in range(2):
            pulled_keep[plane] = pulled[plane, pl.ds(pl.multiple_of(me * share, share), share), :]
            pulled_send[plane] = pulled[
                plane, pl.ds(pl.multiple_of((1 - me) * share, share), share), :
            ]


def chain(places, occupied, offsets, kern, mine, theirs, frames, waves, group):
    count, size = waves.shape[0], waves.shape[-1]
    full = lambda *shape: pl.BlockSpec(shape, lambda i: (0,) * len(shape))
    block = pl.BlockSpec((group, 2, size, size), lambda i: (i, 0, 0, 0))
    return pl.pallas_call(
        functools.partial(chain_kernel, group),
        grid=(count // group,),
        in_specs=[
            SMEM,
            SMEM,
            SMEM,
            full(4, 2, size, size),
            full(2, size, size),
            ANY,
            ANY,
            pl.BlockSpec((group, size, size), lambda i: (i, 0, 0)),
            block,
        ],
        out_specs=[block, block, full(2, size // 2, size), full(2, size // 2, size)],
        out_shape=[
            jax.ShapeDtypeStruct((count, 2, size, size), bf16),
            jax.ShapeDtypeStruct((count, 2, size, size), bf16),
            jax.ShapeDtypeStruct((2, size // 2, size), f32),
            jax.ShapeDtypeStruct((2, size // 2, size), f32),
        ],
        scratch_shapes=[
            pltpu.VMEM((count // group, 2, group, 2, size, size), bf16),
            pltpu.VMEM((group, 2, size, size), bf16),
            pltpu.VMEM((2, group, 2, size, size), f32),
            pltpu.VMEM((2, size, size), f32),
            pltpu.SemaphoreType.DMA((2 * (count // group),)),
        ],
        compiler_params=pltpu.CompilerParams(vmem_limit_bytes=40 * MIB),
        name="chain",
    )(places, occupied, offsets, jnp.asarray(dft_tables(size)), kern, mine, theirs, frames, waves)


def scatter_kernel(edges, names, half, places, occupied, offsets, kept, arrived, tile, *rest):
    strips, (total, sems) = rest[:-2], rest[-2:]
    count, size = kept.shape[0], kept.shape[-1]
    tile_rows, tile_cols = tile.shape[1:]
    sections = 2
    here = offsets[offsets.shape[0] - 1]

    total[...] = jnp.zeros_like(total)
    lane = lax.broadcasted_iota(jnp.int32, (size, LANES), 1)
    row = lax.broadcasted_iota(jnp.int32, (ROWS, size + LANES), 0)

    def add(at, source, place):
        down, across, top, left = spot(places, at)
        wide = pl.ds(left, size + LANES)

        @pl.when(is_live(occupied, places, at))
        def _():
            for plane in range(2):
                value = source[place, plane].astype(f32)
                first = value[:, :LANES]
                inside = lane >= across
                value = cols_of(
                    jnp.where(inside, first, 0.0), value[:, LANES:], jnp.where(inside, 0.0, first)
                )
                first = value[:ROWS]
                inside = row >= down
                value = rows_of(
                    jnp.where(inside, first, 0.0), value[ROWS:], jnp.where(inside, 0.0, first)
                )
                total[plane, pl.ds(top, size + ROWS), wide] += value

    for source, owner in ((kept, here), (arrived, 1 - here)):
        for place in range(count):
            add(sections * place + owner, source, place)
    body = (pl.ds(half, tile_rows), pl.ds(half, tile_cols))
    copy = pltpu.make_async_copy(total.at[(slice(None),) + body], tile, sems.at[0])
    copy.start()
    for (down, across), strip in zip(edges, strips):
        rows = span(down, offsets, names, half, body[0])
        cols = span(across, offsets, names, half, body[1])
        for plane in range(2):
            strip[plane] = total[plane, rows, cols].astype(bf16)
    for (down, acrosses), strip in zip(corner_keys(names), strips[len(edges) :]):
        rows = span(down, offsets, names, half, None)
        for k, across in enumerate(acrosses):
            cols = span(across, offsets, names, half, None)
            for plane in range(2):
                strip[plane, k] = total[plane, rows, cols].astype(bf16)
    copy.wait()


def corner_keys(names):
    acrosses = [key for key in names if key[0] == "col"]
    return [(key, acrosses) for key in names if key[0] == "row" and acrosses]


def scatter(places, occupied, offsets, kept, arrived, edges, names, tile_rows, tile_cols):
    count, _, size, _ = kept.shape
    half = size // 2
    corners = corner_keys(names)
    vmem = pl.BlockSpec(memory_space=pltpu.VMEM)
    return pl.pallas_call(
        functools.partial(scatter_kernel, edges, names, half),
        in_specs=[SMEM, SMEM, SMEM, vmem, vmem],
        out_specs=[HBM] + [vmem] * (len(edges) + len(corners)),
        out_shape=[jax.ShapeDtypeStruct((2, tile_rows, tile_cols), f32)]
        + strip_shapes(edges, tile_rows, tile_cols, half)
        + [jax.ShapeDtypeStruct((2, len(keys), half, half), bf16) for _, keys in corners],
        scratch_shapes=[
            pltpu.VMEM((2, tile_rows + 2 * half, tile_cols + 2 * half), f32),
            pltpu.SemaphoreType.DMA((1,)),
        ],
        compiler_params=pltpu.CompilerParams(vmem_limit_bytes=20 * MIB),
        cost_estimate=pl.CostEstimate(
            flops=0, bytes_accessed=16 * tile_rows * tile_cols, transcendentals=0
        ),
        name="scatter",
    )(places, occupied, offsets, kept, arrived)


def corner_kernel(names, half, offsets, *refs):
    corners = corner_keys(names)
    arrived, refs = refs[: len(corners)], refs[len(corners) :]
    ins, outs = refs[: len(refs) // 2], refs[len(refs) // 2 :]
    for k, (before, strip) in enumerate(zip(ins, outs)):
        strip[...] = before[...]
        for (down, _), block in zip(corners, arrived):
            rows = span(down, offsets, names, half, None)
            for plane in range(2):
                strip[plane, rows, :] = (
                    strip[plane, rows, :].astype(f32) + block[plane, k].astype(f32)
                ).astype(bf16)


def add_corners(offsets, strips, arrived, names, half):
    vmem = pl.BlockSpec(memory_space=pltpu.VMEM)
    return pl.pallas_call(
        functools.partial(corner_kernel, names, half),
        in_specs=[SMEM] + [vmem] * (len(arrived) + len(strips)),
        out_specs=[vmem] * len(strips),
        out_shape=[jax.ShapeDtypeStruct(strip.shape, bf16) for strip in strips],
        compiler_params=pltpu.CompilerParams(vmem_limit_bytes=8 * MIB),
        name="corners",
    )(offsets, *arrived, *strips)


def border_kernel(edges, names, half, offsets, tile_in, part, other, *rest):
    strips, rest = rest[: len(edges)], rest[len(edges) :]
    tile, probe_share, bands, sides, in_sems, out_sems = rest
    tile_rows, tile_cols = tile.shape[1:]
    strips = dict(zip(edges, strips))
    downs = [key for key in names if key[0] == "row"]
    acrosses = [key for key in names if key[0] == "col"]
    tall = sides.shape[2]
    rest_rows = pl.ds(pl.multiple_of(offsets[len(names)], half), tall)
    spans = {key: span(key, offsets, names, half, None) for key in names}
    regions = []
    for k, key in enumerate(acrosses):
        regions.append((key, sides.at[k], rest_rows, spans[key]))
    for k, key in enumerate(downs):
        regions.append((key, bands.at[k], spans[key], pl.ds(0, tile_cols)))

    def copy(k, out):
        _, block, rows, cols = regions[k]
        if out:
            return pltpu.make_async_copy(block, tile.at[:, rows, cols], out_sems.at[k])
        return pltpu.make_async_copy(tile_in.at[:, rows, cols], block, in_sems.at[k])

    for k in range(len(regions)):
        copy(k, False).start()
    probe_share[...] = part[...].astype(f32) + other[...].astype(f32)
    for k, (key, block, rows, cols) in enumerate(regions):
        copy(k, False).wait()
        for plane in range(2):
            if key in downs:
                block[plane] += strips[(key, None)][plane].astype(f32)
                for across in acrosses:
                    block[plane, :, spans[across]] += strips[(None, across)][
                        plane, rows, :
                    ].astype(f32)
            else:
                block[plane] += strips[(None, key)][plane, rows, :].astype(f32)
        copy(k, True).start()
    for k in range(len(regions)):
        copy(k, True).wait()


def add_borders(offsets, tile, probe_parts, edges, names, strips, half):
    vmem = pl.BlockSpec(memory_space=pltpu.VMEM)
    downs = sum(key[0] == "row" for key in names)
    acrosses = len(names) - downs
    tile_rows, tile_cols = tile.shape[1:]
    return pl.pallas_call(
        functools.partial(border_kernel, edges, names, half),
        in_specs=[SMEM, HBM] + [vmem] * (2 + len(strips)),
        out_specs=[HBM, vmem],
        out_shape=[
            jax.ShapeDtypeStruct(tile.shape, f32),
            jax.ShapeDtypeStruct(probe_parts[0].shape, f32),
        ],
        scratch_shapes=[
            pltpu.VMEM((max(downs, 1), 2, half, tile_cols), f32),
            pltpu.VMEM((max(acrosses, 1), 2, tile_rows - downs * half, half), f32),
            pltpu.SemaphoreType.DMA((max(len(names), 1),)),
            pltpu.SemaphoreType.DMA((max(len(names), 1),)),
        ],
        input_output_aliases={1: 0},
        compiler_params=pltpu.CompilerParams(vmem_limit_bytes=12 * MIB),
        cost_estimate=pl.CostEstimate(
            flops=2 * tile_rows * tile_cols,
            bytes_accessed=16 * tile_rows * tile_cols,
            transcendentals=0,
        ),
        name="borders",
    )(offsets, tile, *probe_parts, *strips)


def partner(index, kind):
    return index ^ 1 if kind == 0 else ((index + 1) ^ 1) - 1


def route(edge, rows, cols):
    down, across = edge
    pairs = []
    for r in range(rows):
        to_row = partner(r, down[1]) if down else r
        for c in range(cols):
            to_col = partner(c, across[1]) if across else c
            if 0 <= to_row < rows and 0 <= to_col < cols:
                pairs.append((r * cols + c, to_row * cols + to_col))
    return pairs


def shards(probe, object_re, object_im, phases, centres, occupied, measured):
    size = probe.shape[1]
    half = size // 2
    rows, cols = lax.axis_size("row"), lax.axis_size("col")
    sections = lax.axis_size("depth")
    assert sections == 2 and object_re.shape[0] == 1
    here = lax.axis_index("depth").astype(jnp.int32)
    row_at = lax.axis_index("row").astype(jnp.int32)
    tile_rows, tile_cols = object_re.shape[1:]
    batches, slots = centres.shape[2:4]
    spots = batches * slots
    count = spots // sections

    places = centres.reshape(2 * spots)
    live_counts = occupied.reshape(batches)
    frames = measured.reshape(count, sections, size, size)

    names, tile_at, padded_at = [], [], []
    for axis, extent, own, length in (
        ("row", rows, row_at, tile_rows),
        ("col", cols, lax.axis_index("col").astype(jnp.int32), tile_cols),
    ):
        for kind in range(min(2, extent - 1)):
            forward = own % 2 == kind
            names.append((axis, kind))
            tile_at.append(jnp.where(forward, length - half, 0))
            padded_at.append(jnp.where(forward, length + half, 0))
    downs = [key for key in names if key[0] == "row"]
    acrosses = [key for key in names if key[0] == "col"]
    edges = [(key, None) for key in downs] + [(None, key) for key in acrosses]
    outer, paths = edges, [route(edge, rows, cols) for edge in edges]
    edges = edges + [(down, across) for down in downs for across in acrosses]
    paths += [route(edge, rows, cols) for edge in edges[len(outer) :]]
    both = ("row", "col")

    def numbers(*values):
        return jnp.stack(values).astype(jnp.int32)

    padded_at = numbers(*padded_at, here)
    tile_at = numbers(*tile_at, here)
    bulk = len(names)
    own = pack(tile_at, object_re, object_im, edges, names, half)
    strips = [lax.ppermute(strip, both, path) for strip, path in zip(own, paths)]
    mine, other = gather(places, padded_at, object_re, object_im, edges, names, strips, size)
    across_depth = [(i, 1 - i) for i in range(sections)]
    theirs = lax.ppermute(other, "depth", across_depth)
    kern, sorted_frames, waves = prepare(places, padded_at, mine, probe, phases, frames)
    keep, send, pulled_keep, pulled_send = chain(
        places, live_counts, padded_at, kern, mine, theirs, sorted_frames, waves, count
    )
    arrived = lax.ppermute(send, "depth", across_depth)
    pulled = pulled_keep + lax.ppermute(pulled_send, "depth", across_depth)

    tile, *own = scatter(
        places, live_counts, padded_at, keep, arrived, outer, names, tile_rows, tile_cols
    )
    own, corners = own[: len(outer)], own[len(outer) :]

    bits = rows.bit_length() + cols.bit_length() - 2
    assert rows * cols == 1 << bits
    flips = [cols << k for k in range(rows.bit_length() - 1)]
    flips += [1 << k for k in range(cols.bit_length() - 1)]
    early, late = flips[: max(bits - 2, 0)], flips[max(bits - 2, 0) :]
    rounds = [early[k : k + 2] for k in range(0, len(early), 2)] + [[flip] for flip in late]

    def fetch(block, flip):
        return lax.ppermute(block, both, [(i, i ^ flip) for i in range(rows * cols)])

    *own, pulled = lax.optimization_barrier((*own, pulled))
    if corners:
        corners = [lax.ppermute(x, both, path) for x, path in zip(corners, paths)]
    added = None
    for at, flips in enumerate(rounds):
        mine = pulled.astype(bf16)
        theirs = [fetch(mine, flip) for flip in flips]
        if len(flips) == 2:
            theirs.append(fetch(mine, flips[0] ^ flips[1]))
        if at == 0 and corners:
            theirs, corners = lax.optimization_barrier((theirs, corners))
            own[len(downs) :] = add_corners(tile_at, own[len(downs) :], corners, names, half)
        if added is None and at >= len(rounds) - 3:
            if at:
                theirs, own = lax.optimization_barrier((theirs, own))
            added = [lax.ppermute(strip, both, path) for strip, path in zip(own, paths)]
        if at < len(rounds) - 1:
            sums = [part.astype(f32) for part in (mine, *theirs)]
            pulled = sums[0] + sums[1]
            if len(flips) == 2:
                pulled = pulled + (sums[2] + sums[3])
    (theirs,) = theirs
    if rows == 2:
        first_row = jnp.where(row_at == 0, 0, half)
    else:
        first_row = jnp.int32(half if downs else 0)
    fold_at = numbers(*(tile_at[k] for k in range(bulk)), first_row)
    gradient, probe_share = add_borders(
        fold_at, tile, (mine, theirs), outer, names, added, half
    )
    return (gradient[:, None], probe_share)


def solution(mesh):
    in_specs = (
        P(),
        P("depth", "row", "col"),
        P("depth", "row", "col"),
        P(),
        P("row", "col", None, None, None),
        P("row", "col", None),
        P("row", "col", None, None, None, None),
    )
    out_specs = (P(None, "depth", "row", "col"), P(None, "depth", None))
    return jax.shard_map(shards, mesh=mesh, in_specs=in_specs, out_specs=out_specs, check_vma=False)
```

```python
import functools

import jax
import jax.numpy as jnp
import numpy as np
from jax import lax
from jax.experimental import pallas as pl
from jax.experimental.pallas import tpu as pltpu
from jax.sharding import PartitionSpec as P

f32 = jnp.float32
bf16 = jnp.bfloat16
ROWS = 16
LANES = 128
ANY = pl.BlockSpec(memory_space=pl.ANY)
HBM = pl.BlockSpec(memory_space=pltpu.HBM)
SMEM = pl.BlockSpec(memory_space=pltpu.SMEM)
MIB = 1024 * 1024


def dft_tables(size):
    half = size // 2
    rows = np.arange(half)[:, None]
    cols = np.arange(half)[None, :]

    def packed(turns):
        angle = -2.0 * np.pi * (turns % size) / size
        re, im = np.cos(angle) / np.sqrt(size), np.sin(angle) / np.sqrt(size)
        return np.block([[re, im], [-im, re]])

    even, odd = packed(rows * 2 * cols), packed(rows * (2 * cols + 1))
    full = np.stack([even, odd, even.T, odd.T]).astype(np.float32)
    high = full.astype(jnp.bfloat16)
    low = (full - high.astype(np.float32)).astype(jnp.bfloat16)
    return np.stack([high, low], axis=1)


def sorting_table(size):
    order = np.concatenate([np.arange(0, size, 2), np.arange(1, size, 2)])
    table = np.zeros((size, size), np.float32)
    table[order, np.arange(size)] = 1.0
    return table.astype(jnp.bfloat16)


def split(x):
    high = x.astype(bf16)
    return high, (x - high.astype(f32)).astype(bf16)


def dot3(left, right):
    lhs = jnp.concatenate([left[0], left[0], left[1]], axis=1)
    rhs = jnp.concatenate([right[0], right[1], right[0]], axis=0)
    return jnp.dot(lhs, rhs, preferred_element_type=f32)


def dot(left, right):
    if len(left) == 2 and len(right) == 2:
        return dot3(left, right)
    lhs = left if len(left) == 2 else left * 2
    rhs = right if len(right) == 2 else right * 2
    return jnp.dot(cols_of(*lhs), rows_of(*rhs), preferred_element_type=f32)


def rows_of(*parts):
    return jnp.concatenate(parts, axis=0)


def cols_of(*parts):
    return jnp.concatenate(parts, axis=1)


def prep_kernel(places, offsets, order_t, after, probe, *refs):
    step = pl.program_id(0)
    size = probe.shape[-1]
    half = size // 2
    blocks = size // LANES
    phases, frames = refs[:blocks], refs[blocks : 2 * blocks]
    kern, sorted_frames, waves = refs[2 * blocks :]

    def halved(parts, at):
        ids = [at + (pl.ds(start, half, stride=2), slice(None)) for start in range(2)]
        return rows_of(*(cols_of(*(part[i] for part in parts)) for i in ids))

    def in_order(rows):
        first, rest = split(rows)
        second, third = split(rows - first.astype(f32))
        table = order_t[...]
        return jnp.dot(
            cols_of(first, second, third), rows_of(table, table, table), preferred_element_type=f32
        )

    @pl.when(step == 0)
    def _():
        angles = in_order(halved(phases, ()))
        kern[0] = jnp.cos(angles)
        kern[1] = jnp.sin(angles)

    sorted_frames[0] = in_order(halved(frames, (0, 0)))
    at = 2 * step + offsets[offsets.shape[0] - 1]
    down = places[2 * at] % ROWS
    across = places[2 * at + 1] % LANES
    for plane in range(2):
        moved = pltpu.roll(probe[plane], across, axis=1)
        waves[0, plane] = pltpu.roll(moved, down, axis=0)


def prepare(places, offsets, after, probe, phases, frames):
    count, sections, size = frames.shape[:3]
    blocks = size // LANES
    last = offsets.shape[0] - 1
    full = lambda *shape: pl.BlockSpec(shape, lambda i, p, o: (0,) * len(shape))
    return pl.pallas_call(
        prep_kernel,
        grid_spec=pltpu.PrefetchScalarGridSpec(
            num_scalar_prefetch=2,
            grid=(count,),
            in_specs=[
                full(size, size),
                ANY,
                full(2, size, size),
                *(
                    pl.BlockSpec((size, LANES), lambda i, p, o, b=b: (0, b))
                    for b in range(blocks)
                ),
                *(
                    pl.BlockSpec((1, 1, size, LANES), lambda i, p, o, b=b: (i, o[last], 0, b))
                    for b in range(blocks)
                ),
            ],
            out_specs=[
                full(2, size, size),
                pl.BlockSpec((1, size, size), lambda i, p, o: (i, 0, 0)),
                pl.BlockSpec((1, 2, size, size), lambda i, p, o: (i, 0, 0, 0)),
            ],
        ),
        out_shape=[
            jax.ShapeDtypeStruct((2, size, size), f32),
            jax.ShapeDtypeStruct((count, size, size), f32),
            jax.ShapeDtypeStruct((count, 2, size, size), f32),
        ],
        compiler_params=pltpu.CompilerParams(vmem_limit_bytes=16 * MIB),
        cost_estimate=pl.CostEstimate(flops=0, bytes_accessed=0, transcendentals=0),
        name="prepare",
    )(
        places,
        offsets,
        jnp.asarray(sorting_table(size)),
        after,
        probe,
        *[phases] * blocks,
        *[frames] * blocks,
    )


def span(key, offsets, names, half, whole):
    if key is None:
        return whole
    return pl.ds(pl.multiple_of(offsets[names.index(key)], half), half)


def pack_kernel(edges, names, half, offsets, tile_re, tile_im, *rest):
    strips, sems = rest[:-1], rest[-1]
    tile_rows, tile_cols = tile_re.shape[1:]
    copies = []
    for (down, across), strip in zip(edges, strips):
        rows = span(down, offsets, names, half, pl.ds(0, tile_rows))
        cols = span(across, offsets, names, half, pl.ds(0, tile_cols))
        for plane, tile in enumerate((tile_re, tile_im)):
            copies.append(
                pltpu.make_async_copy(
                    tile.at[0, rows, cols], strip.at[plane], sems.at[len(copies)]
                )
            )
            copies[-1].start()
    for copy in copies:
        copy.wait()


def strip_shapes(edges, tile_rows, tile_cols, half):
    return [
        jax.ShapeDtypeStruct(
            (2, half if down else tile_rows, half if across else tile_cols), bf16
        )
        for down, across in edges
    ]


def pack(offsets, tile_re, tile_im, edges, names, half):
    return pl.pallas_call(
        functools.partial(pack_kernel, edges, names, half),
        in_specs=[SMEM, HBM, HBM],
        out_specs=[ANY] * len(edges),
        out_shape=strip_shapes(edges, *tile_re.shape[1:], half),
        scratch_shapes=[pltpu.SemaphoreType.DMA((2 * len(edges),))],
        compiler_params=pltpu.CompilerParams(vmem_limit_bytes=4 * MIB),
        name="pack",
    )(offsets, tile_re, tile_im)


def spot(places, at):
    row, col = places[2 * at], places[2 * at + 1]
    down, across = row % ROWS, col % LANES
    return down, across, pl.multiple_of(row - down, ROWS), pl.multiple_of(col - across, LANES)


def is_live(occupied, places, at):
    slots = places.shape[0] // 2 // occupied.shape[0]
    return at % slots < occupied[at // slots]


def gather_kernel(spots, edges, names, half, places, offsets, tile_re, tile_im, after, *rest):
    strips, (mine, other, padded, sems) = rest[:-4], rest[-4:]
    tile_rows, tile_cols = tile_re.shape[1:]
    size = mine.shape[-1]
    body = (pl.ds(half, tile_rows), pl.ds(half, tile_cols))
    copies = []

    def bring(source, target):
        copies.append(pltpu.make_async_copy(source, target, sems.at[len(copies)]))
        copies[-1].start()

    bring(tile_re.at[0], padded.at[(0,) + body])
    bring(tile_im.at[0], padded.at[(1,) + body])
    for (down, across), strip in zip(edges, strips):
        rows = span(down, offsets, names, half, body[0])
        cols = span(across, offsets, names, half, body[1])
        bring(strip, padded.at[:, rows, cols])
    for copy in copies:
        copy.wait()

    sections = 2
    lane = lax.broadcasted_iota(jnp.int32, (size, LANES), 1)
    top_lane = lax.broadcasted_iota(jnp.int32, (ROWS, LANES), 1)
    top_row = lax.broadcasted_iota(jnp.int32, (ROWS, size), 0)
    here = offsets[offsets.shape[0] - 1]

    def cut(at, target, place):
        down, across, top, left = spot(places, at)
        inner = size - LANES
        rest = pl.ds(pl.multiple_of(top + ROWS, ROWS), size - ROWS)

        def cols(start, width):
            return pl.ds(pl.multiple_of(left + start, LANES), width)

        for plane in range(2):
            target[place, plane, ROWS:, LANES:] = padded[plane, rest, cols(LANES, inner)]
            near = padded[plane, rest, cols(0, LANES)].astype(f32)
            far = padded[plane, rest, cols(size, LANES)].astype(f32)
            target[place, plane, ROWS:, :LANES] = jnp.where(
                lane[ROWS:] < across, far, near
            ).astype(bf16)
            rows = []
            for start in (0, size):
                block = padded[
                    plane, pl.ds(pl.multiple_of(top + start, ROWS), ROWS), cols(0, size + LANES)
                ].astype(f32)
                first = jnp.where(top_lane < across, block[:, size:], block[:, :LANES])
                rows.append(cols_of(first, block[:, LANES:size]))
            target[place, plane, :ROWS, :] = jnp.where(top_row < down, rows[1], rows[0]).astype(
                bf16
            )

    for place in range(spots // sections):
        cut(sections * place + 1 - here, other, place)
        cut(sections * place + here, mine, place)


def gather(places, offsets, tile_re, tile_im, after, edges, names, strips, size):
    half = size // 2
    spots = places.shape[0] // 2
    tile_rows, tile_cols = tile_re.shape[1:]
    shape = jax.ShapeDtypeStruct((spots // 2, 2, size, size), bf16)
    vmem = pl.BlockSpec(memory_space=pltpu.VMEM)
    return pl.pallas_call(
        functools.partial(gather_kernel, spots, edges, names, half),
        in_specs=[SMEM, SMEM, HBM, HBM] + [ANY] * (1 + len(strips)),
        out_specs=[vmem, vmem],
        out_shape=[shape, shape],
        scratch_shapes=[
            pltpu.VMEM((2, tile_rows + 2 * half, tile_cols + 2 * half), bf16),
            pltpu.SemaphoreType.DMA((2 + len(strips),)),
        ],
        compiler_params=pltpu.CompilerParams(vmem_limit_bytes=16 * MIB),
        name="gather",
    )(places, offsets, tile_re, tile_im, after, *strips)


def chain_kernel(
    group, places, occupied, offsets, tables, kern, mine, theirs, frames, waves,
    keep, send, pulled_keep, pulled_send, windows, middle, terms, pulled, sems,
):
    step = pl.program_id(0)
    steps = pl.num_programs(0)
    size = kern.shape[-1]
    half = size // 2
    me = offsets[offsets.shape[0] - 1]

    def fetch(at, which):
        source, slot = ((mine, me), (theirs, 1 - me))[which]
        rows = pl.ds(at * group, group)
        return pltpu.make_async_copy(
            source.at[rows], windows.at[at, slot], sems.at[2 * at + which]
        )

    @pl.when(step == 0)
    def _():
        for at in range(windows.shape[0]):
            fetch(at, 0).start()
            fetch(at, 1).start()
        pulled[...] = jnp.zeros_like(pulled)

    fetch(step, 0).wait()
    fetch(step, 1).wait()

    def table(which):
        return tables[which, 0], tables[which, 1]

    group_ids = range(group)

    def forward(waves, cut):
        halves = []
        for sign, which in ((1, 2), (-1, 3)):
            parts = []
            for pair in waves:
                if sign > 0:
                    parts.append(rows_of(*(x[:half] + x[half:] for x in pair)))
                else:
                    parts.append(rows_of(*(x[:half] - x[half:] for x in pair)))
            halves.append(dot(table(which), cut(cols_of(*parts))))
        outs = []
        for sign, which in ((1, 0), (-1, 1)):
            parts = []
            for at in group_ids:
                for out in halves:
                    x = out[:, at * size : (at + 1) * size]
                    if sign > 0:
                        x = x[:, :half] + x[:, half:]
                    else:
                        x = x[:, :half] - x[:, half:]
                    parts.append(cols_of(x[:half], x[half:]))
            outs.append(dot(cut(rows_of(*parts)), table(which)))
        return [[out[at * size : (at + 1) * size] for out in outs] for at in group_ids]

    def inverse(parts, cut):
        first = dot(cut(rows_of(*(part[0] for part in parts))), table(2))
        second = dot(cut(rows_of(*(part[1] for part in parts))), table(3))
        evens, odds = [], []
        for at in group_ids:
            rows = slice(at * size, (at + 1) * size)
            plus, minus = first[rows] + second[rows], first[rows] - second[rows]
            re = cols_of(plus[:, :half], minus[:, :half])
            im = cols_of(plus[:, half:], minus[:, half:])
            evens.append(rows_of(re[:half], im[:half]))
            odds.append(rows_of(re[half:], im[half:]))
        first = dot(table(0), cut(cols_of(*evens)))
        second = dot(table(1), cut(cols_of(*odds)))
        outs = []
        for at in group_ids:
            cols = slice(at * size, (at + 1) * size)
            plus, minus = first[:, cols] + second[:, cols], first[:, cols] - second[:, cols]
            outs.append((rows_of(plus[:half], minus[:half]), rows_of(plus[half:], minus[half:])))
        return outs

    def propagate(waves, sign, cut):
        kept = []
        for parts in forward(waves, cut):
            outs = []
            for k, part in enumerate(parts):
                cols = slice(k * half, (k + 1) * half)
                kre, kim = kern[0, :, cols], kern[1, :, cols] * sign
                re, im = part[:, :half], part[:, half:]
                outs.append(cols_of(re * kre - im * kim, re * kim + im * kre))
            kept.append(outs)
        return inverse(kept, cut)

    def product(left, right):
        return left[0] * right[0] - left[1] * right[1], left[0] * right[1] + left[1] * right[0]

    def conj_product(left, right):
        return left[0] * right[0] + left[1] * right[1], left[0] * right[1] - left[1] * right[0]

    def rounded(x):
        return x.astype(bf16).astype(f32)

    def window(slot, at):
        return windows[step, slot, at, 0].astype(f32), windows[step, slot, at, 1].astype(f32)

    def wave(at):
        return waves[at, 0], waves[at, 1]

    def passed(at):
        return middle[at, 0].astype(f32), middle[at, 1].astype(f32)

    outs = propagate([product(wave(at), window(0, at)) for at in group_ids], 1.0, split)
    for at in group_ids:
        middle[at, 0] = outs[at][0].astype(bf16)
        middle[at, 1] = outs[at][1].astype(bf16)

    far = forward([product(passed(at), window(1, at)) for at in group_ids], split)
    for at in group_ids:
        for k, part in enumerate(far[at]):
            re, im = part[:, :half], part[:, half:]
            misfit = re * re + im * im - frames[at, :, k * half : (k + 1) * half]
            far[at][k] = cols_of(re * misfit, im * misfit)
    pulls = []
    for at, chi in enumerate(inverse(far, split)):
        terms[1, at, 0], terms[1, at, 1] = conj_product(passed(at), chi)
        pulls.append(conj_product(window(1, at), chi))

    for at, chi in enumerate(propagate(pulls, -1.0, lambda x: (x.astype(bf16),))):
        chi = rounded(chi[0]), rounded(chi[1])
        terms[0, at, 0], terms[0, at, 1] = conj_product(wave(at), chi)
        spot_at = 2 * (step * group + at) + me
        up = (size - places[2 * spot_at] % ROWS) % size
        back_by = (size - places[2 * spot_at + 1] % LANES) % size
        weight = is_live(occupied, places, spot_at).astype(f32)
        for plane, value in enumerate(conj_product(window(0, at), chi)):
            value = pltpu.roll(pltpu.roll(value * weight, back_by, axis=1), up, axis=0)
            pulled[plane] += value

    keep[...] = terms[me].astype(bf16)
    send[...] = terms[1 - me].astype(bf16)

    @pl.when(step == steps - 1)
    def _():
        share = pulled_keep.shape[1]
        for plane in range(2):
            pulled_keep[plane] = pulled[plane, pl.ds(pl.multiple_of(me * share, share), share), :]
            pulled_send[plane] = pulled[
                plane, pl.ds(pl.multiple_of((1 - me) * share, share), share), :
            ]


def chain(places, occupied, offsets, kern, mine, theirs, frames, waves, group):
    count, size = waves.shape[0], waves.shape[-1]
    full = lambda *shape: pl.BlockSpec(shape, lambda i: (0,) * len(shape))
    block = pl.BlockSpec((group, 2, size, size), lambda i: (i, 0, 0, 0))
    return pl.pallas_call(
        functools.partial(chain_kernel, group),
        grid=(count // group,),
        in_specs=[
            SMEM,
            SMEM,
            SMEM,
            full(4, 2, size, size),
            full(2, size, size),
            ANY,
            ANY,
            pl.BlockSpec((group, size, size), lambda i: (i, 0, 0)),
            block,
        ],
        out_specs=[block, block, full(2, size // 2, size), full(2, size // 2, size)],
        out_shape=[
            jax.ShapeDtypeStruct((count, 2, size, size), bf16),
            jax.ShapeDtypeStruct((count, 2, size, size), bf16),
            jax.ShapeDtypeStruct((2, size // 2, size), f32),
            jax.ShapeDtypeStruct((2, size // 2, size), f32),
        ],
        scratch_shapes=[
            pltpu.VMEM((count // group, 2, group, 2, size, size), bf16),
            pltpu.VMEM((group, 2, size, size), bf16),
            pltpu.VMEM((2, group, 2, size, size), f32),
            pltpu.VMEM((2, size, size), f32),
            pltpu.SemaphoreType.DMA((2 * (count // group),)),
        ],
        compiler_params=pltpu.CompilerParams(vmem_limit_bytes=40 * MIB),
        name="chain",
    )(places, occupied, offsets, jnp.asarray(dft_tables(size)), kern, mine, theirs, frames, waves)


def scatter_kernel(edges, names, half, places, occupied, offsets, folds, kept, arrived, tile, *rest):
    strips, (total, sems) = rest[:-2], rest[-2:]
    count, size = kept.shape[0], kept.shape[-1]
    tile_rows, tile_cols = tile.shape[1:]
    sections = 2
    here = offsets[offsets.shape[0] - 1]

    total[...] = jnp.zeros_like(total)
    lane = lax.broadcasted_iota(jnp.int32, (size, LANES), 1)
    row = lax.broadcasted_iota(jnp.int32, (ROWS, size + LANES), 0)

    def add(at, source, place):
        down, across, top, left = spot(places, at)
        wide = pl.ds(left, size + LANES)

        @pl.when(is_live(occupied, places, at))
        def _():
            for plane in range(2):
                value = source[place, plane].astype(f32)
                first = value[:, :LANES]
                inside = lane >= across
                value = cols_of(
                    jnp.where(inside, first, 0.0), value[:, LANES:], jnp.where(inside, 0.0, first)
                )
                first = value[:ROWS]
                inside = row >= down
                value = rows_of(
                    jnp.where(inside, first, 0.0), value[ROWS:], jnp.where(inside, 0.0, first)
                )
                total[plane, pl.ds(top, size + ROWS), wide] += value

    for source, owner in ((kept, here), (arrived, 1 - here)):
        for place in range(count):
            add(sections * place + owner, source, place)
    body = (pl.ds(half, tile_rows), pl.ds(half, tile_cols))
    copy = pltpu.make_async_copy(total.at[(slice(None),) + body], tile, sems.at[0])
    copy.start()
    bands, strips = strips[: len(names)], strips[len(names) :]
    for (down, across), strip in zip(edges, strips):
        rows = span(down, offsets, names, half, body[0])
        cols = span(across, offsets, names, half, body[1])
        for plane in range(2):
            strip[plane] = total[plane, rows, cols].astype(bf16)
    for (rows, cols), band in zip(band_places(names, folds, half, bands, tile_cols), bands):
        rows = pl.ds(pl.multiple_of(rows.start + half, half), rows.size)
        cols = pl.ds(pl.multiple_of(cols.start + half, half), cols.size)
        band[...] = total[:, rows, cols]
    for (down, acrosses), strip in zip(corner_keys(names), strips[len(edges) :]):
        rows = span(down, offsets, names, half, None)
        for k, across in enumerate(acrosses):
            cols = span(across, offsets, names, half, None)
            for plane in range(2):
                strip[plane, k] = total[plane, rows, cols].astype(bf16)
    copy.wait()


def band_shapes(names, tile_rows, tile_cols, half):
    tall = tile_rows - half * sum(key[0] == "row" for key in names)
    return [(2, half, tile_cols) if key[0] == "row" else (2, tall, half) for key in names]


def band_places(names, folds, half, bands, tile_cols):
    result = []
    for k, (key, band) in enumerate(zip(names, bands)):
        own = pl.ds(pl.multiple_of(folds[k], half), half)
        if key[0] == "row":
            result.append((own, pl.ds(0, tile_cols)))
        else:
            first = pl.multiple_of(folds[len(names)], half)
            result.append((pl.ds(first, band.shape[1]), own))
    return result


def corner_keys(names):
    acrosses = [key for key in names if key[0] == "col"]
    return [(key, acrosses) for key in names if key[0] == "row" and acrosses]


def scatter(places, occupied, offsets, folds, kept, arrived, edges, names, tile_rows, tile_cols):
    count, _, size, _ = kept.shape
    half = size // 2
    corners = corner_keys(names)
    vmem = pl.BlockSpec(memory_space=pltpu.VMEM)
    return pl.pallas_call(
        functools.partial(scatter_kernel, edges, names, half),
        in_specs=[SMEM, SMEM, SMEM, SMEM, vmem, vmem],
        out_specs=[HBM] + [vmem] * (len(names) + len(edges) + len(corners)),
        out_shape=[jax.ShapeDtypeStruct((2, tile_rows, tile_cols), f32)]
        + [jax.ShapeDtypeStruct(x, f32) for x in band_shapes(names, tile_rows, tile_cols, half)]
        + strip_shapes(edges, tile_rows, tile_cols, half)
        + [jax.ShapeDtypeStruct((2, len(keys), half, half), bf16) for _, keys in corners],
        scratch_shapes=[
            pltpu.VMEM((2, tile_rows + 2 * half, tile_cols + 2 * half), f32),
            pltpu.SemaphoreType.DMA((1,)),
        ],
        compiler_params=pltpu.CompilerParams(vmem_limit_bytes=20 * MIB),
        cost_estimate=pl.CostEstimate(
            flops=0, bytes_accessed=16 * tile_rows * tile_cols, transcendentals=0
        ),
        name="scatter",
    )(places, occupied, offsets, folds, kept, arrived)


def corner_kernel(names, half, offsets, *refs):
    corners = corner_keys(names)
    arrived, refs = refs[: len(corners)], refs[len(corners) :]
    ins, outs = refs[: len(refs) // 2], refs[len(refs) // 2 :]
    for k, (before, strip) in enumerate(zip(ins, outs)):
        strip[...] = before[...]
        for (down, _), block in zip(corners, arrived):
            rows = span(down, offsets, names, half, None)
            for plane in range(2):
                strip[plane, rows, :] = (
                    strip[plane, rows, :].astype(f32) + block[plane, k].astype(f32)
                ).astype(bf16)


def add_corners(offsets, strips, arrived, names, half):
    vmem = pl.BlockSpec(memory_space=pltpu.VMEM)
    return pl.pallas_call(
        functools.partial(corner_kernel, names, half),
        in_specs=[SMEM] + [vmem] * (len(arrived) + len(strips)),
        out_specs=[vmem] * len(strips),
        out_shape=[jax.ShapeDtypeStruct(strip.shape, bf16) for strip in strips],
        compiler_params=pltpu.CompilerParams(vmem_limit_bytes=8 * MIB),
        name="corners",
    )(offsets, *arrived, *strips)


def border_kernel(edges, names, half, folds, tile_in, part, other, *rest):
    bands, rest = rest[: len(names)], rest[len(names) :]
    strips, rest = rest[: len(edges)], rest[len(edges) :]
    tile, probe_share, sems = rest[0], rest[1], rest[-1]
    sums = rest[2:-1]
    strips = dict(zip(edges, strips))
    tile_cols = tile.shape[2]
    regions = band_places(names, folds, half, bands, tile_cols)
    copies = []
    for k, (key, (rows, cols)) in enumerate(zip(names, regions)):
        for plane in range(2):
            block = sums[k]
            if key[0] == "row":
                block[plane] = bands[k][plane] + strips[(key, None)][plane].astype(f32)
                for j, across in enumerate(names):
                    if across[0] == "col":
                        wide = pl.ds(pl.multiple_of(folds[j], half), half)
                        block[plane, :, wide] += strips[(None, across)][plane, rows, :].astype(f32)
            else:
                block[plane] = bands[k][plane] + strips[(None, key)][plane, rows, :].astype(f32)
            copies.append(
                pltpu.make_async_copy(
                    block.at[plane], tile.at[plane, rows, cols], sems.at[len(copies)]
                )
            )
            copies[-1].start()
    probe_share[...] = part[...].astype(f32) + other[...].astype(f32)
    for copy in copies:
        copy.wait()


def add_borders(folds, tile, bands, probe_parts, edges, names, strips, half):
    vmem = pl.BlockSpec(memory_space=pltpu.VMEM)
    return pl.pallas_call(
        functools.partial(border_kernel, edges, names, half),
        in_specs=[SMEM, HBM] + [vmem] * (2 + len(bands) + len(strips)),
        out_specs=[HBM, vmem],
        out_shape=[
            jax.ShapeDtypeStruct(tile.shape, f32),
            jax.ShapeDtypeStruct(probe_parts[0].shape, f32),
        ],
        scratch_shapes=[
            *(pltpu.VMEM(band.shape, f32) for band in bands),
            pltpu.SemaphoreType.DMA((max(2 * len(bands), 1),)),
        ],
        input_output_aliases={1: 0},
        compiler_params=pltpu.CompilerParams(vmem_limit_bytes=12 * MIB),
        name="borders",
    )(folds, tile, *probe_parts, *bands, *strips)


def partner(index, kind):
    return index ^ 1 if kind == 0 else ((index + 1) ^ 1) - 1


def route(edge, rows, cols):
    down, across = edge
    pairs = []
    for r in range(rows):
        to_row = partner(r, down[1]) if down else r
        for c in range(cols):
            to_col = partner(c, across[1]) if across else c
            if 0 <= to_row < rows and 0 <= to_col < cols:
                pairs.append((r * cols + c, to_row * cols + to_col))
    return pairs


def shards(probe, object_re, object_im, phases, centres, occupied, measured):
    size = probe.shape[1]
    half = size // 2
    rows, cols = lax.axis_size("row"), lax.axis_size("col")
    sections = lax.axis_size("depth")
    assert sections == 2 and object_re.shape[0] == 1
    here = lax.axis_index("depth").astype(jnp.int32)
    row_at = lax.axis_index("row").astype(jnp.int32)
    tile_rows, tile_cols = object_re.shape[1:]
    batches, slots = centres.shape[2:4]
    spots = batches * slots
    count = spots // sections

    places = centres.reshape(2 * spots)
    live_counts = occupied.reshape(batches)
    frames = measured.reshape(count, sections, size, size)

    names, tile_at, padded_at = [], [], []
    for axis, extent, own, length in (
        ("row", rows, row_at, tile_rows),
        ("col", cols, lax.axis_index("col").astype(jnp.int32), tile_cols),
    ):
        for kind in range(min(2, extent - 1)):
            forward = own % 2 == kind
            names.append((axis, kind))
            tile_at.append(jnp.where(forward, length - half, 0))
            padded_at.append(jnp.where(forward, length + half, 0))
    downs = [key for key in names if key[0] == "row"]
    acrosses = [key for key in names if key[0] == "col"]
    edges = [(key, None) for key in downs] + [(None, key) for key in acrosses]
    outer, paths = edges, [route(edge, rows, cols) for edge in edges]
    edges = edges + [(down, across) for down in downs for across in acrosses]
    paths += [route(edge, rows, cols) for edge in edges[len(outer) :]]
    both = ("row", "col")

    def numbers(*values):
        return jnp.stack(values).astype(jnp.int32)

    padded_at = numbers(*padded_at, here)
    tile_at = numbers(*tile_at, here)
    if rows == 2:
        first_row = jnp.where(row_at == 0, 0, half)
    else:
        first_row = jnp.int32(half if downs else 0)
    fold_at = numbers(*(tile_at[k] for k in range(len(names))), first_row)
    own = pack(tile_at, object_re, object_im, edges, names, half)
    strips = [lax.ppermute(strip, both, path) for strip, path in zip(own, paths)]
    kern, sorted_frames, waves = prepare(places, padded_at, own[0], probe, phases, frames)
    mine, other = gather(
        places, padded_at, object_re, object_im, waves, edges, names, strips, size
    )
    across_depth = [(i, 1 - i) for i in range(sections)]
    theirs = lax.ppermute(other, "depth", across_depth)
    keep, send, pulled_keep, pulled_send = chain(
        places, live_counts, padded_at, kern, mine, theirs, sorted_frames, waves, count
    )
    arrived = lax.ppermute(send, "depth", across_depth)
    pulled = pulled_keep + lax.ppermute(pulled_send, "depth", across_depth)

    assert rows & (rows - 1) == 0 and cols & (cols - 1) == 0
    flips = [cols << k for k in range(rows.bit_length() - 1)]
    across = [1 << k for k in range(cols.bit_length() - 1)]
    flips += across[-1:] + across[:-1]
    corner_at = max(len(flips) - 3, 0)

    def exchange(block, flip):
        own = block.astype(bf16)
        return own, lax.ppermute(own, both, [(i, i ^ flip) for i in range(rows * cols)])

    def summed(pair):
        return pair[0].astype(f32) + pair[1].astype(f32)

    pair = pulled, jnp.zeros_like(pulled)
    for at in range(corner_at):
        pair = exchange(summed(pair), flips[at])

    tile, *own = scatter(
        places, live_counts, padded_at, fold_at, keep, arrived, outer, names, tile_rows, tile_cols
    )
    bands, own = own[: len(names)], own[len(names) :]
    own, corners = own[: len(outer)], own[len(outer) :]
    pair, own, corners = lax.optimization_barrier((pair, own, corners))
    if corners:
        corners = [lax.ppermute(x, both, path) for x, path in zip(corners, paths)]
    if corner_at < len(flips):
        pair = exchange(summed(pair), flips[corner_at])
    if corners:
        pair, corners = lax.optimization_barrier((pair, corners))
        own[len(downs) :] = add_corners(tile_at, own[len(downs) :], corners, names, half)
    added = [lax.ppermute(strip, both, path) for strip, path in zip(own, paths)]
    for flip in flips[corner_at + 1 :]:
        pair = exchange(summed(pair), flip)
    gradient, probe_share = add_borders(fold_at, tile, bands, pair, outer, names, added, half)
    return (gradient[:, None], probe_share)


def solution(mesh):
    in_specs = (
        P(),
        P("depth", "row", "col"),
        P("depth", "row", "col"),
        P(),
        P("row", "col", None, None, None),
        P("row", "col", None),
        P("row", "col", None, None, None, None),
    )
    out_specs = (P(None, "depth", "row", "col"), P(None, "depth", None))
    return jax.shard_map(shards, mesh=mesh, in_specs=in_specs, out_specs=out_specs, check_vma=False)
```

```python
import functools

import jax
import jax.numpy as jnp
import numpy as np
from jax import lax
from jax.experimental import pallas as pl
from jax.experimental.pallas import tpu as pltpu
from jax.sharding import PartitionSpec as P

f32 = jnp.float32
bf16 = jnp.bfloat16
ROWS = 16
LANES = 128
ANY = pl.BlockSpec(memory_space=pl.ANY)
HBM = pl.BlockSpec(memory_space=pltpu.HBM)
SMEM = pl.BlockSpec(memory_space=pltpu.SMEM)
MIB = 1024 * 1024


def dft_tables(size):
    half = size // 2
    rows = np.arange(half)[:, None]
    cols = np.arange(half)[None, :]

    def packed(turns):
        angle = -2.0 * np.pi * (turns % size) / size
        re, im = np.cos(angle) / np.sqrt(size), np.sin(angle) / np.sqrt(size)
        return np.block([[re, im], [-im, re]])

    even, odd = packed(rows * 2 * cols), packed(rows * (2 * cols + 1))
    full = np.stack([even, odd, even.T, odd.T]).astype(np.float32)
    high = full.astype(jnp.bfloat16)
    low = (full - high.astype(np.float32)).astype(jnp.bfloat16)
    return np.stack([high, low], axis=1)


def split(x):
    high = x.astype(bf16)
    return high, (x - high.astype(f32)).astype(bf16)


def dot3(left, right):
    lhs = jnp.concatenate([left[0], left[0], left[1]], axis=1)
    rhs = jnp.concatenate([right[0], right[1], right[0]], axis=0)
    return jnp.dot(lhs, rhs, preferred_element_type=f32)


def dot(left, right):
    if len(left) == 2 and len(right) == 2:
        return dot3(left, right)
    lhs = left if len(left) == 2 else left * 2
    rhs = right if len(right) == 2 else right * 2
    return jnp.dot(cols_of(*lhs), rows_of(*rhs), preferred_element_type=f32)


def rows_of(*parts):
    return jnp.concatenate(parts, axis=0)


def cols_of(*parts):
    return jnp.concatenate(parts, axis=1)


def prep_kernel(places, offsets, after, probe, *refs):
    step = pl.program_id(0)
    size = probe.shape[-1]
    half = size // 2
    blocks = size // LANES
    phases, frames = refs[:blocks], refs[blocks : 2 * blocks]
    kern, sorted_frames, waves, order = refs[2 * blocks :]

    def halved(parts, at):
        ids = [at + (pl.ds(start, half, stride=2), slice(None)) for start in range(2)]
        return rows_of(*(cols_of(*(part[i] for part in parts)) for i in ids))

    def in_order(rows):
        first, rest = split(rows)
        second, third = split(rows - first.astype(f32))
        table = order[...]
        return jnp.dot(
            cols_of(first, second, third), rows_of(table, table, table), preferred_element_type=f32
        )

    @pl.when(step == 0)
    def _():
        source = lax.broadcasted_iota(jnp.int32, (size, size), 0)
        target = lax.broadcasted_iota(jnp.int32, (size, size), 1)
        chosen = source == 2 * (target % half) + target // half
        order[...] = jnp.where(chosen, 1.0, 0.0).astype(bf16)
        angles = in_order(halved(phases, ()))
        kern[0] = jnp.cos(angles)
        kern[1] = jnp.sin(angles)

    sorted_frames[0] = in_order(halved(frames, (0, 0)))
    at = 2 * step + offsets[offsets.shape[0] - 1]
    down = places[2 * at] % ROWS
    across = places[2 * at + 1] % LANES
    for plane in range(2):
        moved = pltpu.roll(probe[plane], across, axis=1)
        waves[0, plane] = pltpu.roll(moved, down, axis=0)


def prepare(places, offsets, after, probe, phases, frames):
    count, sections, size = frames.shape[:3]
    blocks = size // LANES
    last = offsets.shape[0] - 1
    full = lambda *shape: pl.BlockSpec(shape, lambda i, p, o: (0,) * len(shape))
    return pl.pallas_call(
        prep_kernel,
        grid_spec=pltpu.PrefetchScalarGridSpec(
            num_scalar_prefetch=2,
            grid=(count,),
            in_specs=[
                ANY,
                full(2, size, size),
                *(
                    pl.BlockSpec((size, LANES), lambda i, p, o, b=b: (0, b))
                    for b in range(blocks)
                ),
                *(
                    pl.BlockSpec((1, 1, size, LANES), lambda i, p, o, b=b: (i, o[last], 0, b))
                    for b in range(blocks)
                ),
            ],
            out_specs=[
                full(2, size, size),
                pl.BlockSpec((1, size, size), lambda i, p, o: (i, 0, 0)),
                pl.BlockSpec((1, 2, size, size), lambda i, p, o: (i, 0, 0, 0)),
            ],
            scratch_shapes=[pltpu.VMEM((size, size), bf16)],
        ),
        out_shape=[
            jax.ShapeDtypeStruct((2, size, size), f32),
            jax.ShapeDtypeStruct((count, size, size), f32),
            jax.ShapeDtypeStruct((count, 2, size, size), f32),
        ],
        compiler_params=pltpu.CompilerParams(vmem_limit_bytes=16 * MIB),
        cost_estimate=pl.CostEstimate(flops=0, bytes_accessed=0, transcendentals=0),
        name="prepare",
    )(
        places,
        offsets,
        after,
        probe,
        *[phases] * blocks,
        *[frames] * blocks,
    )


def span(key, offsets, names, half, whole):
    if key is None:
        return whole
    return pl.ds(pl.multiple_of(offsets[names.index(key)], half), half)


def pack_kernel(edges, names, half, offsets, tile_re, tile_im, *rest):
    strips, sems = rest[:-1], rest[-1]
    tile_rows, tile_cols = tile_re.shape[1:]
    copies = []
    for (down, across), strip in zip(edges, strips):
        rows = span(down, offsets, names, half, pl.ds(0, tile_rows))
        cols = span(across, offsets, names, half, pl.ds(0, tile_cols))
        for plane, tile in enumerate((tile_re, tile_im)):
            copies.append(
                pltpu.make_async_copy(
                    tile.at[0, rows, cols], strip.at[plane], sems.at[len(copies)]
                )
            )
            copies[-1].start()
    for copy in copies:
        copy.wait()


def strip_shapes(edges, tile_rows, tile_cols, half):
    return [
        jax.ShapeDtypeStruct(
            (2, half if down else tile_rows, half if across else tile_cols), bf16
        )
        for down, across in edges
    ]


def pack(offsets, tile_re, tile_im, edges, names, half):
    return pl.pallas_call(
        functools.partial(pack_kernel, edges, names, half),
        in_specs=[SMEM, HBM, HBM],
        out_specs=[ANY] * len(edges),
        out_shape=strip_shapes(edges, *tile_re.shape[1:], half),
        scratch_shapes=[pltpu.SemaphoreType.DMA((2 * len(edges),))],
        compiler_params=pltpu.CompilerParams(vmem_limit_bytes=4 * MIB),
        name="pack",
    )(offsets, tile_re, tile_im)


def spot(places, at):
    row, col = places[2 * at], places[2 * at + 1]
    down, across = row % ROWS, col % LANES
    return down, across, pl.multiple_of(row - down, ROWS), pl.multiple_of(col - across, LANES)


def is_live(occupied, places, at):
    slots = places.shape[0] // 2 // occupied.shape[0]
    return at % slots < occupied[at // slots]


def gather_kernel(spots, edges, names, half, places, offsets, tile_re, tile_im, after, *rest):
    strips, (mine, other, padded, sems) = rest[:-4], rest[-4:]
    tile_rows, tile_cols = tile_re.shape[1:]
    size = mine.shape[-1]
    body = (pl.ds(half, tile_rows), pl.ds(half, tile_cols))
    copies = []

    def bring(source, target):
        copies.append(pltpu.make_async_copy(source, target, sems.at[len(copies)]))
        copies[-1].start()

    bring(tile_re.at[0], padded.at[(0,) + body])
    bring(tile_im.at[0], padded.at[(1,) + body])
    for (down, across), strip in zip(edges, strips):
        rows = span(down, offsets, names, half, body[0])
        cols = span(across, offsets, names, half, body[1])
        bring(strip, padded.at[:, rows, cols])
    for copy in copies:
        copy.wait()

    sections = 2
    lane = lax.broadcasted_iota(jnp.int32, (size, LANES), 1)
    top_lane = lax.broadcasted_iota(jnp.int32, (ROWS, LANES), 1)
    top_row = lax.broadcasted_iota(jnp.int32, (ROWS, size), 0)
    here = offsets[offsets.shape[0] - 1]

    def cut(at, target, place):
        down, across, top, left = spot(places, at)
        inner = size - LANES
        rest = pl.ds(pl.multiple_of(top + ROWS, ROWS), size - ROWS)

        def cols(start, width):
            return pl.ds(pl.multiple_of(left + start, LANES), width)

        for plane in range(2):
            target[place, plane, ROWS:, LANES:] = padded[plane, rest, cols(LANES, inner)]
            near = padded[plane, rest, cols(0, LANES)].astype(f32)
            far = padded[plane, rest, cols(size, LANES)].astype(f32)
            target[place, plane, ROWS:, :LANES] = jnp.where(
                lane[ROWS:] < across, far, near
            ).astype(bf16)
            rows = []
            for start in (0, size):
                block = padded[
                    plane, pl.ds(pl.multiple_of(top + start, ROWS), ROWS), cols(0, size + LANES)
                ].astype(f32)
                first = jnp.where(top_lane < across, block[:, size:], block[:, :LANES])
                rows.append(cols_of(first, block[:, LANES:size]))
            target[place, plane, :ROWS, :] = jnp.where(top_row < down, rows[1], rows[0]).astype(
                bf16
            )

    for place in range(spots // sections):
        cut(sections * place + 1 - here, other, place)
        cut(sections * place + here, mine, place)


def gather(places, offsets, tile_re, tile_im, after, edges, names, strips, size):
    half = size // 2
    spots = places.shape[0] // 2
    tile_rows, tile_cols = tile_re.shape[1:]
    shape = jax.ShapeDtypeStruct((spots // 2, 2, size, size), bf16)
    vmem = pl.BlockSpec(memory_space=pltpu.VMEM)
    return pl.pallas_call(
        functools.partial(gather_kernel, spots, edges, names, half),
        in_specs=[SMEM, SMEM, HBM, HBM] + [ANY] * (1 + len(strips)),
        out_specs=[vmem, vmem],
        out_shape=[shape, shape],
        scratch_shapes=[
            pltpu.VMEM((2, tile_rows + 2 * half, tile_cols + 2 * half), bf16),
            pltpu.SemaphoreType.DMA((2 + len(strips),)),
        ],
        compiler_params=pltpu.CompilerParams(vmem_limit_bytes=16 * MIB),
        name="gather",
    )(places, offsets, tile_re, tile_im, after, *strips)


def chain_kernel(
    group, places, occupied, offsets, tables, kern, mine, theirs, frames, waves,
    keep, send, pulled_keep, pulled_send, windows, middle, terms, pulled, sems,
):
    step = pl.program_id(0)
    steps = pl.num_programs(0)
    size = kern.shape[-1]
    half = size // 2
    me = offsets[offsets.shape[0] - 1]

    def fetch(at, which):
        source, slot = ((mine, me), (theirs, 1 - me))[which]
        rows = pl.ds(at * group, group)
        return pltpu.make_async_copy(
            source.at[rows], windows.at[at, slot], sems.at[2 * at + which]
        )

    @pl.when(step == 0)
    def _():
        for at in range(windows.shape[0]):
            fetch(at, 0).start()
            fetch(at, 1).start()
        pulled[...] = jnp.zeros_like(pulled)

    fetch(step, 0).wait()
    fetch(step, 1).wait()

    def table(which):
        return tables[which, 0], tables[which, 1]

    group_ids = range(group)

    def forward(waves, cut):
        halves = []
        for sign, which in ((1, 2), (-1, 3)):
            parts = []
            for pair in waves:
                if sign > 0:
                    parts.append(rows_of(*(x[:half] + x[half:] for x in pair)))
                else:
                    parts.append(rows_of(*(x[:half] - x[half:] for x in pair)))
            halves.append(dot(table(which), cut(cols_of(*parts))))
        outs = []
        for sign, which in ((1, 0), (-1, 1)):
            parts = []
            for at in group_ids:
                for out in halves:
                    x = out[:, at * size : (at + 1) * size]
                    if sign > 0:
                        x = x[:, :half] + x[:, half:]
                    else:
                        x = x[:, :half] - x[:, half:]
                    parts.append(cols_of(x[:half], x[half:]))
            outs.append(dot(cut(rows_of(*parts)), table(which)))
        return [[out[at * size : (at + 1) * size] for out in outs] for at in group_ids]

    def inverse(parts, cut):
        first = dot(cut(rows_of(*(part[0] for part in parts))), table(2))
        second = dot(cut(rows_of(*(part[1] for part in parts))), table(3))
        evens, odds = [], []
        for at in group_ids:
            rows = slice(at * size, (at + 1) * size)
            plus, minus = first[rows] + second[rows], first[rows] - second[rows]
            re = cols_of(plus[:, :half], minus[:, :half])
            im = cols_of(plus[:, half:], minus[:, half:])
            evens.append(rows_of(re[:half], im[:half]))
            odds.append(rows_of(re[half:], im[half:]))
        first = dot(table(0), cut(cols_of(*evens)))
        second = dot(table(1), cut(cols_of(*odds)))
        outs = []
        for at in group_ids:
            cols = slice(at * size, (at + 1) * size)
            plus, minus = first[:, cols] + second[:, cols], first[:, cols] - second[:, cols]
            outs.append((rows_of(plus[:half], minus[:half]), rows_of(plus[half:], minus[half:])))
        return outs

    def propagate(waves, sign, cut):
        kept = []
        for parts in forward(waves, cut):
            outs = []
            for k, part in enumerate(parts):
                cols = slice(k * half, (k + 1) * half)
                kre, kim = kern[0, :, cols], kern[1, :, cols] * sign
                re, im = part[:, :half], part[:, half:]
                outs.append(cols_of(re * kre - im * kim, re * kim + im * kre))
            kept.append(outs)
        return inverse(kept, cut)

    def product(left, right):
        return left[0] * right[0] - left[1] * right[1], left[0] * right[1] + left[1] * right[0]

    def conj_product(left, right):
        return left[0] * right[0] + left[1] * right[1], left[0] * right[1] - left[1] * right[0]

    def rounded(x):
        return x.astype(bf16).astype(f32)

    def window(slot, at):
        return windows[step, slot, at, 0].astype(f32), windows[step, slot, at, 1].astype(f32)

    def wave(at):
        return waves[at, 0], waves[at, 1]

    def passed(at):
        return middle[at, 0].astype(f32), middle[at, 1].astype(f32)

    outs = propagate([product(wave(at), window(0, at)) for at in group_ids], 1.0, split)
    for at in group_ids:
        middle[at, 0] = outs[at][0].astype(bf16)
        middle[at, 1] = outs[at][1].astype(bf16)

    far = forward([product(passed(at), window(1, at)) for at in group_ids], split)
    for at in group_ids:
        for k, part in enumerate(far[at]):
            re, im = part[:, :half], part[:, half:]
            misfit = re * re + im * im - frames[at, :, k * half : (k + 1) * half]
            far[at][k] = cols_of(re * misfit, im * misfit)
    pulls = []
    for at, chi in enumerate(inverse(far, split)):
        terms[1, at, 0], terms[1, at, 1] = conj_product(passed(at), chi)
        pulls.append(conj_product(window(1, at), chi))

    for at, chi in enumerate(propagate(pulls, -1.0, lambda x: (x.astype(bf16),))):
        chi = rounded(chi[0]), rounded(chi[1])
        terms[0, at, 0], terms[0, at, 1] = conj_product(wave(at), chi)
        spot_at = 2 * (step * group + at) + me
        up = (size - places[2 * spot_at] % ROWS) % size
        back_by = (size - places[2 * spot_at + 1] % LANES) % size
        weight = is_live(occupied, places, spot_at).astype(f32)
        for plane, value in enumerate(conj_product(window(0, at), chi)):
            value = pltpu.roll(pltpu.roll(value * weight, back_by, axis=1), up, axis=0)
            pulled[plane] += value

    keep[...] = terms[me].astype(bf16)
    send[...] = terms[1 - me].astype(bf16)

    @pl.when(step == steps - 1)
    def _():
        share = pulled_keep.shape[1]
        for out, owner in ((pulled_keep, me), (pulled_send, 1 - me)):
            rows = pl.ds(pl.multiple_of(owner * share, share), share)
            out[...] = pulled[:, rows, :].astype(bf16)


def chain(places, occupied, offsets, kern, mine, theirs, frames, waves, group):
    count, size = waves.shape[0], waves.shape[-1]
    full = lambda *shape: pl.BlockSpec(shape, lambda i: (0,) * len(shape))
    block = pl.BlockSpec((group, 2, size, size), lambda i: (i, 0, 0, 0))
    return pl.pallas_call(
        functools.partial(chain_kernel, group),
        grid=(count // group,),
        in_specs=[
            SMEM,
            SMEM,
            SMEM,
            full(4, 2, size, size),
            full(2, size, size),
            ANY,
            ANY,
            pl.BlockSpec((group, size, size), lambda i: (i, 0, 0)),
            block,
        ],
        out_specs=[block, block, full(2, size // 2, size), full(2, size // 2, size)],
        out_shape=[
            jax.ShapeDtypeStruct((count, 2, size, size), bf16),
            jax.ShapeDtypeStruct((count, 2, size, size), bf16),
            jax.ShapeDtypeStruct((2, size // 2, size), bf16),
            jax.ShapeDtypeStruct((2, size // 2, size), bf16),
        ],
        scratch_shapes=[
            pltpu.VMEM((count // group, 2, group, 2, size, size), bf16),
            pltpu.VMEM((group, 2, size, size), bf16),
            pltpu.VMEM((2, group, 2, size, size), f32),
            pltpu.VMEM((2, size, size), f32),
            pltpu.SemaphoreType.DMA((2 * (count // group),)),
        ],
        compiler_params=pltpu.CompilerParams(vmem_limit_bytes=40 * MIB),
        name="chain",
    )(places, occupied, offsets, jnp.asarray(dft_tables(size)), kern, mine, theirs, frames, waves)


def scatter_kernel(edges, names, half, places, occupied, offsets, folds, kept, arrived, tile, *rest):
    strips, (total, sems) = rest[:-2], rest[-2:]
    count, size = kept.shape[0], kept.shape[-1]
    tile_rows, tile_cols = tile.shape[1:]
    sections = 2
    here = offsets[offsets.shape[0] - 1]

    total[...] = jnp.zeros_like(total)
    lane = lax.broadcasted_iota(jnp.int32, (size, LANES), 1)
    row = lax.broadcasted_iota(jnp.int32, (ROWS, size + LANES), 0)

    def add(at, source, place):
        down, across, top, left = spot(places, at)
        wide = pl.ds(left, size + LANES)

        @pl.when(is_live(occupied, places, at))
        def _():
            for plane in range(2):
                value = source[place, plane].astype(f32)
                first = value[:, :LANES]
                inside = lane >= across
                value = cols_of(
                    jnp.where(inside, first, 0.0), value[:, LANES:], jnp.where(inside, 0.0, first)
                )
                first = value[:ROWS]
                inside = row >= down
                value = rows_of(
                    jnp.where(inside, first, 0.0), value[ROWS:], jnp.where(inside, 0.0, first)
                )
                total[plane, pl.ds(top, size + ROWS), wide] += value

    for source, owner in ((kept, here), (arrived, 1 - here)):
        for place in range(count):
            add(sections * place + owner, source, place)
    body = (pl.ds(half, tile_rows), pl.ds(half, tile_cols))
    copy = pltpu.make_async_copy(total.at[(slice(None),) + body], tile, sems.at[0])
    copy.start()
    bands, strips = strips[: len(names)], strips[len(names) :]
    for (down, across), strip in zip(edges, strips):
        rows = span(down, offsets, names, half, body[0])
        cols = span(across, offsets, names, half, body[1])
        for plane in range(2):
            strip[plane] = total[plane, rows, cols].astype(bf16)
    for (rows, cols), band in zip(band_places(names, folds, half, bands, tile_cols), bands):
        rows = pl.ds(pl.multiple_of(rows.start + half, half), rows.size)
        cols = pl.ds(pl.multiple_of(cols.start + half, half), cols.size)
        band[...] = total[:, rows, cols]
    for (down, acrosses), strip in zip(corner_keys(names), strips[len(edges) :]):
        rows = span(down, offsets, names, half, None)
        for k, across in enumerate(acrosses):
            cols = span(across, offsets, names, half, None)
            for plane in range(2):
                strip[plane, k] = total[plane, rows, cols].astype(bf16)
    copy.wait()


def band_shapes(names, tile_rows, tile_cols, half):
    tall = tile_rows - half * sum(key[0] == "row" for key in names)
    return [(2, half, tile_cols) if key[0] == "row" else (2, tall, half) for key in names]


def band_places(names, folds, half, bands, tile_cols):
    result = []
    for k, (key, band) in enumerate(zip(names, bands)):
        own = pl.ds(pl.multiple_of(folds[k], half), half)
        if key[0] == "row":
            result.append((own, pl.ds(0, tile_cols)))
        else:
            first = pl.multiple_of(folds[len(names)], half)
            result.append((pl.ds(first, band.shape[1]), own))
    return result


def corner_keys(names):
    acrosses = [key for key in names if key[0] == "col"]
    return [(key, acrosses) for key in names if key[0] == "row" and acrosses]


def scatter(places, occupied, offsets, folds, kept, arrived, edges, names, tile_rows, tile_cols):
    count, _, size, _ = kept.shape
    half = size // 2
    corners = corner_keys(names)
    vmem = pl.BlockSpec(memory_space=pltpu.VMEM)
    return pl.pallas_call(
        functools.partial(scatter_kernel, edges, names, half),
        in_specs=[SMEM, SMEM, SMEM, SMEM, vmem, vmem],
        out_specs=[HBM] + [vmem] * (len(names) + len(edges) + len(corners)),
        out_shape=[jax.ShapeDtypeStruct((2, tile_rows, tile_cols), f32)]
        + [jax.ShapeDtypeStruct(x, f32) for x in band_shapes(names, tile_rows, tile_cols, half)]
        + strip_shapes(edges, tile_rows, tile_cols, half)
        + [jax.ShapeDtypeStruct((2, len(keys), half, half), bf16) for _, keys in corners],
        scratch_shapes=[
            pltpu.VMEM((2, tile_rows + 2 * half, tile_cols + 2 * half), f32),
            pltpu.SemaphoreType.DMA((1,)),
        ],
        compiler_params=pltpu.CompilerParams(vmem_limit_bytes=20 * MIB),
        cost_estimate=pl.CostEstimate(
            flops=0, bytes_accessed=16 * tile_rows * tile_cols, transcendentals=0
        ),
        name="scatter",
    )(places, occupied, offsets, folds, kept, arrived)


def corner_kernel(names, half, offsets, *refs):
    corners = corner_keys(names)
    arrived, refs = refs[: len(corners)], refs[len(corners) :]
    ins, outs = refs[: len(refs) // 2], refs[len(refs) // 2 :]
    for k, (before, strip) in enumerate(zip(ins, outs)):
        strip[...] = before[...]
        for (down, _), block in zip(corners, arrived):
            rows = span(down, offsets, names, half, None)
            for plane in range(2):
                strip[plane, rows, :] = (
                    strip[plane, rows, :].astype(f32) + block[plane, k].astype(f32)
                ).astype(bf16)


def add_corners(offsets, strips, arrived, names, half):
    vmem = pl.BlockSpec(memory_space=pltpu.VMEM)
    return pl.pallas_call(
        functools.partial(corner_kernel, names, half),
        in_specs=[SMEM] + [vmem] * (len(arrived) + len(strips)),
        out_specs=[vmem] * len(strips),
        out_shape=[jax.ShapeDtypeStruct(strip.shape, bf16) for strip in strips],
        compiler_params=pltpu.CompilerParams(vmem_limit_bytes=8 * MIB),
        name="corners",
    )(offsets, *arrived, *strips)


def border_kernel(edges, names, half, folds, tile_in, part, other, *rest):
    bands, rest = rest[: len(names)], rest[len(names) :]
    strips, rest = rest[: len(edges)], rest[len(edges) :]
    tile, probe_share, sems = rest[0], rest[1], rest[-1]
    sums = rest[2:-1]
    strips = dict(zip(edges, strips))
    tile_cols = tile.shape[2]
    regions = band_places(names, folds, half, bands, tile_cols)
    copies = []
    for k, (key, (rows, cols)) in enumerate(zip(names, regions)):
        for plane in range(2):
            block = sums[k]
            if key[0] == "row":
                block[plane] = bands[k][plane] + strips[(key, None)][plane].astype(f32)
                for j, across in enumerate(names):
                    if across[0] == "col":
                        wide = pl.ds(pl.multiple_of(folds[j], half), half)
                        block[plane, :, wide] += strips[(None, across)][plane, rows, :].astype(f32)
            else:
                block[plane] = bands[k][plane] + strips[(None, key)][plane, rows, :].astype(f32)
            copies.append(
                pltpu.make_async_copy(
                    block.at[plane], tile.at[plane, rows, cols], sems.at[len(copies)]
                )
            )
            copies[-1].start()
    probe_share[...] = part[...].astype(f32) + other[...].astype(f32)
    for copy in copies:
        copy.wait()


def add_borders(folds, tile, bands, probe_parts, edges, names, strips, half):
    vmem = pl.BlockSpec(memory_space=pltpu.VMEM)
    return pl.pallas_call(
        functools.partial(border_kernel, edges, names, half),
        in_specs=[SMEM, HBM] + [vmem] * (2 + len(bands) + len(strips)),
        out_specs=[HBM, vmem],
        out_shape=[
            jax.ShapeDtypeStruct(tile.shape, f32),
            jax.ShapeDtypeStruct(probe_parts[0].shape, f32),
        ],
        scratch_shapes=[
            *(pltpu.VMEM(band.shape, f32) for band in bands),
            pltpu.SemaphoreType.DMA((max(2 * len(bands), 1),)),
        ],
        input_output_aliases={1: 0},
        compiler_params=pltpu.CompilerParams(vmem_limit_bytes=12 * MIB),
        name="borders",
    )(folds, tile, *probe_parts, *bands, *strips)


def partner(index, kind):
    return index ^ 1 if kind == 0 else ((index + 1) ^ 1) - 1


def route(edge, rows, cols):
    down, across = edge
    pairs = []
    for r in range(rows):
        to_row = partner(r, down[1]) if down else r
        for c in range(cols):
            to_col = partner(c, across[1]) if across else c
            if 0 <= to_row < rows and 0 <= to_col < cols:
                pairs.append((r * cols + c, to_row * cols + to_col))
    return pairs


def shards(probe, object_re, object_im, phases, centres, occupied, measured):
    size = probe.shape[1]
    half = size // 2
    rows, cols = lax.axis_size("row"), lax.axis_size("col")
    sections = lax.axis_size("depth")
    assert sections == 2 and object_re.shape[0] == 1
    here = lax.axis_index("depth").astype(jnp.int32)
    row_at = lax.axis_index("row").astype(jnp.int32)
    tile_rows, tile_cols = object_re.shape[1:]
    batches, slots = centres.shape[2:4]
    spots = batches * slots
    count = spots // sections

    places = centres.reshape(2 * spots)
    live_counts = occupied.reshape(batches)
    frames = measured.reshape(count, sections, size, size)

    names, tile_at, padded_at = [], [], []
    for axis, extent, own, length in (
        ("row", rows, row_at, tile_rows),
        ("col", cols, lax.axis_index("col").astype(jnp.int32), tile_cols),
    ):
        for kind in range(min(2, extent - 1)):
            forward = own % 2 == kind
            names.append((axis, kind))
            tile_at.append(jnp.where(forward, length - half, 0))
            padded_at.append(jnp.where(forward, length + half, 0))
    downs = [key for key in names if key[0] == "row"]
    acrosses = [key for key in names if key[0] == "col"]
    edges = [(key, None) for key in downs] + [(None, key) for key in acrosses]
    outer, paths = edges, [route(edge, rows, cols) for edge in edges]
    edges = edges + [(down, across) for down in downs for across in acrosses]
    paths += [route(edge, rows, cols) for edge in edges[len(outer) :]]
    both = ("row", "col")

    def numbers(*values):
        return jnp.stack(values).astype(jnp.int32)

    padded_at = numbers(*padded_at, here)
    tile_at = numbers(*tile_at, here)
    if rows == 2:
        first_row = jnp.where(row_at == 0, 0, half)
    else:
        first_row = jnp.int32(half if downs else 0)
    fold_at = numbers(*(tile_at[k] for k in range(len(names))), first_row)
    own = pack(tile_at, object_re, object_im, edges, names, half)
    strips = [lax.ppermute(strip, both, path) for strip, path in zip(own, paths)]
    kern, sorted_frames, waves = prepare(places, padded_at, own[0], probe, phases, frames)
    mine, other = gather(
        places, padded_at, object_re, object_im, waves, edges, names, strips, size
    )
    across_depth = [(i, 1 - i) for i in range(sections)]
    theirs = lax.ppermute(other, "depth", across_depth)
    keep, send, own_rows, other_rows = chain(
        places, live_counts, padded_at, kern, mine, theirs, sorted_frames, waves, count
    )
    arrived = lax.ppermute(send, "depth", across_depth)

    assert rows & (rows - 1) == 0 and cols & (cols - 1) == 0
    tiles = rows * cols
    flips = [1 << k for k in range(cols.bit_length() - 1)]
    flips = flips[-1:] + flips[:-1] + [cols << k for k in range(rows.bit_length() - 1)]

    def fetched(block, flip):
        pairs = [(i, i ^ flip) for i in range(sections * tiles)]
        return lax.ppermute(block, ("depth",) + both, pairs)

    def exchange(block, flip):
        own = block.astype(bf16)
        return own, fetched(own, flip)

    def summed(pair):
        return pair[0].astype(f32) + pair[1].astype(f32)

    parts = [own_rows, fetched(other_rows, tiles)]
    if flips:
        parts += [fetched(own_rows, flips[0]), fetched(other_rows, tiles ^ flips[0])]

    tile, *own = scatter(
        places, live_counts, padded_at, fold_at, keep, arrived, outer, names, tile_rows, tile_cols
    )
    bands, own = own[: len(names)], own[len(names) :]
    own, corners = own[: len(outer)], own[len(outer) :]
    parts, own, corners = lax.optimization_barrier((parts, own, corners))
    pair = parts[0].astype(f32), parts[1].astype(f32)
    if flips:
        pair = summed(parts[::2]), summed(parts[1::2])
    if corners:
        corners = [lax.ppermute(x, both, path) for x, path in zip(corners, paths)]
    if flips[1:]:
        pair = exchange(summed(pair), flips[1])
    if corners:
        pair, corners = lax.optimization_barrier((pair, corners))
        own[len(downs) :] = add_corners(tile_at, own[len(downs) :], corners, names, half)
    added = [lax.ppermute(strip, both, path) for strip, path in zip(own, paths)]
    for flip in flips[2:]:
        pair = exchange(summed(pair), flip)
    gradient, probe_share = add_borders(fold_at, tile, bands, pair, outer, names, added, half)
    return (gradient[:, None], probe_share)


def solution(mesh):
    in_specs = (
        P(),
        P("depth", "row", "col"),
        P("depth", "row", "col"),
        P(),
        P("row", "col", None, None, None),
        P("row", "col", None),
        P("row", "col", None, None, None, None),
    )
    out_specs = (P(None, "depth", "row", "col"), P(None, "depth", None))
    return jax.shard_map(shards, mesh=mesh, in_specs=in_specs, out_specs=out_specs, check_vma=False)
```

```python
import functools

import jax
import jax.numpy as jnp
import numpy as np
from jax import lax
from jax.experimental import pallas as pl
from jax.experimental.pallas import tpu as pltpu
from jax.sharding import PartitionSpec as P

f32 = jnp.float32
bf16 = jnp.bfloat16
ROWS = 16
LANES = 128
ANY = pl.BlockSpec(memory_space=pl.ANY)
HBM = pl.BlockSpec(memory_space=pltpu.HBM)
SMEM = pl.BlockSpec(memory_space=pltpu.SMEM)
MIB = 1024 * 1024


def dft_tables(size):
    half = size // 2
    rows = np.arange(half)[:, None]
    cols = np.arange(half)[None, :]

    def packed(turns):
        angle = -2.0 * np.pi * (turns % size) / size
        re, im = np.cos(angle) / np.sqrt(size), np.sin(angle) / np.sqrt(size)
        return np.block([[re, im], [-im, re]])

    even, odd = packed(rows * 2 * cols), packed(rows * (2 * cols + 1))
    full = np.stack([even, odd, even.T, odd.T]).astype(np.float32)
    high = full.astype(jnp.bfloat16)
    low = (full - high.astype(np.float32)).astype(jnp.bfloat16)
    return np.stack([high, low], axis=1)


def split(x):
    high = x.astype(bf16)
    return high, (x - high.astype(f32)).astype(bf16)


def dot3(left, right):
    lhs = jnp.concatenate([left[0], left[0], left[1]], axis=1)
    rhs = jnp.concatenate([right[0], right[1], right[0]], axis=0)
    return jnp.dot(lhs, rhs, preferred_element_type=f32)


def dot(left, right):
    if len(left) == 2 and len(right) == 2:
        return dot3(left, right)
    lhs = left if len(left) == 2 else left * 2
    rhs = right if len(right) == 2 else right * 2
    return jnp.dot(cols_of(*lhs), rows_of(*rhs), preferred_element_type=f32)


def rows_of(*parts):
    return jnp.concatenate(parts, axis=0)


def cols_of(*parts):
    return jnp.concatenate(parts, axis=1)


def prep_kernel(places, offsets, after, probe, *refs):
    step = pl.program_id(0)
    size = probe.shape[-1]
    half = size // 2
    blocks = size // LANES
    phases, frames = refs[:blocks], refs[blocks : 2 * blocks]
    kern, sorted_frames, waves, order = refs[2 * blocks :]

    def halved(parts, at):
        ids = [at + (pl.ds(start, half, stride=2), slice(None)) for start in range(2)]
        return rows_of(*(cols_of(*(part[i] for part in parts)) for i in ids))

    def in_order(rows):
        first, rest = split(rows)
        second, third = split(rows - first.astype(f32))
        table = order[...]
        return jnp.dot(
            cols_of(first, second, third), rows_of(table, table, table), preferred_element_type=f32
        )

    @pl.when(step == 0)
    def _():
        source = lax.broadcasted_iota(jnp.int32, (size, size), 0)
        target = lax.broadcasted_iota(jnp.int32, (size, size), 1)
        chosen = source == 2 * (target % half) + target // half
        order[...] = jnp.where(chosen, 1.0, 0.0).astype(bf16)
        angles = in_order(halved(phases, ()))
        kern[0] = jnp.cos(angles)
        kern[1] = jnp.sin(angles)

    sorted_frames[0] = in_order(halved(frames, (0, 0)))
    at = 2 * step + offsets[offsets.shape[0] - 1]
    down = places[2 * at] % ROWS
    across = places[2 * at + 1] % LANES
    for plane in range(2):
        moved = pltpu.roll(probe[plane], across, axis=1)
        waves[0, plane] = pltpu.roll(moved, down, axis=0)


def prepare(places, offsets, after, probe, phases, frames):
    count, sections, size = frames.shape[:3]
    blocks = size // LANES
    last = offsets.shape[0] - 1
    full = lambda *shape: pl.BlockSpec(shape, lambda i, p, o: (0,) * len(shape))
    return pl.pallas_call(
        prep_kernel,
        grid_spec=pltpu.PrefetchScalarGridSpec(
            num_scalar_prefetch=2,
            grid=(count,),
            in_specs=[
                ANY,
                full(2, size, size),
                *(
                    pl.BlockSpec((size, LANES), lambda i, p, o, b=b: (0, b))
                    for b in range(blocks)
                ),
                *(
                    pl.BlockSpec((1, 1, size, LANES), lambda i, p, o, b=b: (i, o[last], 0, b))
                    for b in range(blocks)
                ),
            ],
            out_specs=[
                full(2, size, size),
                pl.BlockSpec((1, size, size), lambda i, p, o: (i, 0, 0)),
                pl.BlockSpec((1, 2, size, size), lambda i, p, o: (i, 0, 0, 0)),
            ],
            scratch_shapes=[pltpu.VMEM((size, size), bf16)],
        ),
        out_shape=[
            jax.ShapeDtypeStruct((2, size, size), f32),
            jax.ShapeDtypeStruct((count, size, size), f32),
            jax.ShapeDtypeStruct((count, 2, size, size), f32),
        ],
        compiler_params=pltpu.CompilerParams(vmem_limit_bytes=16 * MIB),
        cost_estimate=pl.CostEstimate(flops=0, bytes_accessed=0, transcendentals=0),
        name="prepare",
    )(
        places,
        offsets,
        after,
        probe,
        *[phases] * blocks,
        *[frames] * blocks,
    )


def span(key, offsets, names, half, whole):
    if key is None:
        return whole
    return pl.ds(pl.multiple_of(offsets[names.index(key)], half), half)


def pack_kernel(edges, names, half, offsets, tile_re, tile_im, *rest):
    strips, sems = rest[:-1], rest[-1]
    tile_rows, tile_cols = tile_re.shape[1:]
    copies = []
    for (down, across), strip in zip(edges, strips):
        rows = span(down, offsets, names, half, pl.ds(0, tile_rows))
        cols = span(across, offsets, names, half, pl.ds(0, tile_cols))
        for plane, tile in enumerate((tile_re, tile_im)):
            copies.append(
                pltpu.make_async_copy(
                    tile.at[0, rows, cols], strip.at[plane], sems.at[len(copies)]
                )
            )
            copies[-1].start()
    for copy in copies:
        copy.wait()


def strip_shapes(edges, tile_rows, tile_cols, half):
    return [
        jax.ShapeDtypeStruct(
            (2, half if down else tile_rows, half if across else tile_cols), bf16
        )
        for down, across in edges
    ]


def pack(offsets, tile_re, tile_im, edges, names, half):
    return pl.pallas_call(
        functools.partial(pack_kernel, edges, names, half),
        in_specs=[SMEM, HBM, HBM],
        out_specs=[ANY] * len(edges),
        out_shape=strip_shapes(edges, *tile_re.shape[1:], half),
        scratch_shapes=[pltpu.SemaphoreType.DMA((2 * len(edges),))],
        compiler_params=pltpu.CompilerParams(vmem_limit_bytes=4 * MIB),
        name="pack",
    )(offsets, tile_re, tile_im)


def spot(places, at):
    row, col = places[2 * at], places[2 * at + 1]
    down, across = row % ROWS, col % LANES
    return down, across, pl.multiple_of(row - down, ROWS), pl.multiple_of(col - across, LANES)


def is_live(occupied, places, at):
    slots = places.shape[0] // 2 // occupied.shape[0]
    return at % slots < occupied[at // slots]


def gather_kernel(spots, edges, names, half, places, offsets, tile_re, tile_im, after, *rest):
    strips, (mine, other, padded, sems) = rest[:-4], rest[-4:]
    tile_rows, tile_cols = tile_re.shape[1:]
    size = mine.shape[-1]
    body = (pl.ds(half, tile_rows), pl.ds(half, tile_cols))
    copies = []

    def bring(source, target):
        copies.append(pltpu.make_async_copy(source, target, sems.at[len(copies)]))
        copies[-1].start()

    bring(tile_re.at[0], padded.at[(0,) + body])
    bring(tile_im.at[0], padded.at[(1,) + body])
    for (down, across), strip in zip(edges, strips):
        rows = span(down, offsets, names, half, body[0])
        cols = span(across, offsets, names, half, body[1])
        bring(strip, padded.at[:, rows, cols])
    for copy in copies:
        copy.wait()

    sections = 2
    lane = lax.broadcasted_iota(jnp.int32, (size, LANES), 1)
    top_lane = lax.broadcasted_iota(jnp.int32, (ROWS, LANES), 1)
    top_row = lax.broadcasted_iota(jnp.int32, (ROWS, size), 0)
    here = offsets[offsets.shape[0] - 1]

    def cut(at, target, place):
        down, across, top, left = spot(places, at)
        inner = size - LANES
        rest = pl.ds(pl.multiple_of(top + ROWS, ROWS), size - ROWS)

        def cols(start, width):
            return pl.ds(pl.multiple_of(left + start, LANES), width)

        for plane in range(2):
            target[place, plane, ROWS:, LANES:] = padded[plane, rest, cols(LANES, inner)]
            near = padded[plane, rest, cols(0, LANES)].astype(f32)
            far = padded[plane, rest, cols(size, LANES)].astype(f32)
            target[place, plane, ROWS:, :LANES] = jnp.where(
                lane[ROWS:] < across, far, near
            ).astype(bf16)
            rows = []
            for start in (0, size):
                block = padded[
                    plane, pl.ds(pl.multiple_of(top + start, ROWS), ROWS), cols(0, size + LANES)
                ].astype(f32)
                first = jnp.where(top_lane < across, block[:, size:], block[:, :LANES])
                rows.append(cols_of(first, block[:, LANES:size]))
            target[place, plane, :ROWS, :] = jnp.where(top_row < down, rows[1], rows[0]).astype(
                bf16
            )

    for place in range(spots // sections):
        cut(sections * place + 1 - here, other, place)
        cut(sections * place + here, mine, place)


def gather(places, offsets, tile_re, tile_im, after, edges, names, strips, size):
    half = size // 2
    spots = places.shape[0] // 2
    tile_rows, tile_cols = tile_re.shape[1:]
    shape = jax.ShapeDtypeStruct((spots // 2, 2, size, size), bf16)
    vmem = pl.BlockSpec(memory_space=pltpu.VMEM)
    return pl.pallas_call(
        functools.partial(gather_kernel, spots, edges, names, half),
        in_specs=[SMEM, SMEM, HBM, HBM] + [ANY] * (1 + len(strips)),
        out_specs=[vmem, vmem],
        out_shape=[shape, shape],
        scratch_shapes=[
            pltpu.VMEM((2, tile_rows + 2 * half, tile_cols + 2 * half), bf16),
            pltpu.SemaphoreType.DMA((2 + len(strips),)),
        ],
        compiler_params=pltpu.CompilerParams(vmem_limit_bytes=16 * MIB),
        name="gather",
    )(places, offsets, tile_re, tile_im, after, *strips)


def chain_kernel(
    group, places, occupied, offsets, tables, kern, mine, theirs, frames, waves,
    keep, send, pulled_keep, pulled_send, windows, middle, terms, pulled, sems,
):
    step = pl.program_id(0)
    steps = pl.num_programs(0)
    size = kern.shape[-1]
    half = size // 2
    me = offsets[offsets.shape[0] - 1]

    def fetch(at, which):
        source, slot = ((mine, me), (theirs, 1 - me))[which]
        rows = pl.ds(at * group, group)
        return pltpu.make_async_copy(
            source.at[rows], windows.at[at, slot], sems.at[2 * at + which]
        )

    @pl.when(step == 0)
    def _():
        for at in range(windows.shape[0]):
            fetch(at, 0).start()
            fetch(at, 1).start()
        pulled[...] = jnp.zeros_like(pulled)

    fetch(step, 0).wait()
    fetch(step, 1).wait()

    def table(which):
        return tables[which, 0], tables[which, 1]

    group_ids = range(group)

    def forward(waves, cut):
        halves = []
        for sign, which in ((1, 2), (-1, 3)):
            parts = []
            for pair in waves:
                if sign > 0:
                    parts.append(rows_of(*(x[:half] + x[half:] for x in pair)))
                else:
                    parts.append(rows_of(*(x[:half] - x[half:] for x in pair)))
            halves.append(dot(table(which), cut(cols_of(*parts))))
        outs = []
        for sign, which in ((1, 0), (-1, 1)):
            parts = []
            for at in group_ids:
                for out in halves:
                    x = out[:, at * size : (at + 1) * size]
                    if sign > 0:
                        x = x[:, :half] + x[:, half:]
                    else:
                        x = x[:, :half] - x[:, half:]
                    parts.append(cols_of(x[:half], x[half:]))
            outs.append(dot(cut(rows_of(*parts)), table(which)))
        return [[out[at * size : (at + 1) * size] for out in outs] for at in group_ids]

    def inverse(parts, cut):
        first = dot(cut(rows_of(*(part[0] for part in parts))), table(2))
        second = dot(cut(rows_of(*(part[1] for part in parts))), table(3))
        evens, odds = [], []
        for at in group_ids:
            rows = slice(at * size, (at + 1) * size)
            plus, minus = first[rows] + second[rows], first[rows] - second[rows]
            re = cols_of(plus[:, :half], minus[:, :half])
            im = cols_of(plus[:, half:], minus[:, half:])
            evens.append(rows_of(re[:half], im[:half]))
            odds.append(rows_of(re[half:], im[half:]))
        first = dot(table(0), cut(cols_of(*evens)))
        second = dot(table(1), cut(cols_of(*odds)))
        outs = []
        for at in group_ids:
            cols = slice(at * size, (at + 1) * size)
            plus, minus = first[:, cols] + second[:, cols], first[:, cols] - second[:, cols]
            outs.append((rows_of(plus[:half], minus[:half]), rows_of(plus[half:], minus[half:])))
        return outs

    def propagate(waves, sign, cut):
        kept = []
        for parts in forward(waves, cut):
            outs = []
            for k, part in enumerate(parts):
                cols = slice(k * half, (k + 1) * half)
                kre, kim = kern[0, :, cols], kern[1, :, cols] * sign
                re, im = part[:, :half], part[:, half:]
                outs.append(cols_of(re * kre - im * kim, re * kim + im * kre))
            kept.append(outs)
        return inverse(kept, cut)

    def product(left, right):
        return left[0] * right[0] - left[1] * right[1], left[0] * right[1] + left[1] * right[0]

    def conj_product(left, right):
        return left[0] * right[0] + left[1] * right[1], left[0] * right[1] - left[1] * right[0]

    def rounded(x):
        return x.astype(bf16).astype(f32)

    def window(slot, at):
        return windows[step, slot, at, 0].astype(f32), windows[step, slot, at, 1].astype(f32)

    def wave(at):
        return waves[at, 0], waves[at, 1]

    def passed(at):
        return middle[at, 0].astype(f32), middle[at, 1].astype(f32)

    outs = propagate([product(wave(at), window(0, at)) for at in group_ids], 1.0, split)
    for at in group_ids:
        middle[at, 0] = outs[at][0].astype(bf16)
        middle[at, 1] = outs[at][1].astype(bf16)

    far = forward([product(passed(at), window(1, at)) for at in group_ids], split)
    for at in group_ids:
        for k, part in enumerate(far[at]):
            re, im = part[:, :half], part[:, half:]
            misfit = re * re + im * im - frames[at, :, k * half : (k + 1) * half]
            far[at][k] = cols_of(re * misfit, im * misfit)
    pulls = []
    for at, chi in enumerate(inverse(far, split)):
        terms[1, at, 0], terms[1, at, 1] = conj_product(passed(at), chi)
        pulls.append(conj_product(window(1, at), chi))

    for at, chi in enumerate(propagate(pulls, -1.0, lambda x: (x.astype(bf16),))):
        chi = rounded(chi[0]), rounded(chi[1])
        terms[0, at, 0], terms[0, at, 1] = conj_product(wave(at), chi)
        spot_at = 2 * (step * group + at) + me
        up = (size - places[2 * spot_at] % ROWS) % size
        back_by = (size - places[2 * spot_at + 1] % LANES) % size
        weight = is_live(occupied, places, spot_at).astype(f32)
        for plane, value in enumerate(conj_product(window(0, at), chi)):
            value = pltpu.roll(pltpu.roll(value * weight, back_by, axis=1), up, axis=0)
            pulled[plane] += value

    keep[...] = terms[me].astype(bf16)
    send[...] = terms[1 - me].astype(bf16)

    @pl.when(step == steps - 1)
    def _():
        share = pulled_keep.shape[1]
        for out, owner in ((pulled_keep, me), (pulled_send, 1 - me)):
            rows = pl.ds(pl.multiple_of(owner * share, share), share)
            out[...] = pulled[:, rows, :].astype(bf16)


def chain(places, occupied, offsets, kern, mine, theirs, frames, waves, group):
    count, size = waves.shape[0], waves.shape[-1]
    full = lambda *shape: pl.BlockSpec(shape, lambda i: (0,) * len(shape))
    block = pl.BlockSpec((group, 2, size, size), lambda i: (i, 0, 0, 0))
    return pl.pallas_call(
        functools.partial(chain_kernel, group),
        grid=(count // group,),
        in_specs=[
            SMEM,
            SMEM,
            SMEM,
            full(4, 2, size, size),
            full(2, size, size),
            ANY,
            ANY,
            pl.BlockSpec((group, size, size), lambda i: (i, 0, 0)),
            block,
        ],
        out_specs=[block, block, full(2, size // 2, size), full(2, size // 2, size)],
        out_shape=[
            jax.ShapeDtypeStruct((count, 2, size, size), bf16),
            jax.ShapeDtypeStruct((count, 2, size, size), bf16),
            jax.ShapeDtypeStruct((2, size // 2, size), bf16),
            jax.ShapeDtypeStruct((2, size // 2, size), bf16),
        ],
        scratch_shapes=[
            pltpu.VMEM((count // group, 2, group, 2, size, size), bf16),
            pltpu.VMEM((group, 2, size, size), bf16),
            pltpu.VMEM((2, group, 2, size, size), f32),
            pltpu.VMEM((2, size, size), f32),
            pltpu.SemaphoreType.DMA((2 * (count // group),)),
        ],
        compiler_params=pltpu.CompilerParams(vmem_limit_bytes=40 * MIB),
        name="chain",
    )(places, occupied, offsets, jnp.asarray(dft_tables(size)), kern, mine, theirs, frames, waves)


def scatter_kernel(edges, names, half, places, occupied, offsets, folds, kept, arrived, tile, *rest):
    strips, (total, sems) = rest[:-2], rest[-2:]
    count, size = kept.shape[0], kept.shape[-1]
    tile_rows, tile_cols = tile.shape[1:]
    sections = 2
    here = offsets[offsets.shape[0] - 1]

    total[...] = jnp.zeros_like(total)
    lane = lax.broadcasted_iota(jnp.int32, (size, LANES), 1)
    row = lax.broadcasted_iota(jnp.int32, (ROWS, size + LANES), 0)

    def add(at, source, place):
        down, across, top, left = spot(places, at)
        wide = pl.ds(left, size + LANES)

        @pl.when(is_live(occupied, places, at))
        def _():
            for plane in range(2):
                value = source[place, plane].astype(f32)
                first = value[:, :LANES]
                inside = lane >= across
                value = cols_of(
                    jnp.where(inside, first, 0.0), value[:, LANES:], jnp.where(inside, 0.0, first)
                )
                first = value[:ROWS]
                inside = row >= down
                value = rows_of(
                    jnp.where(inside, first, 0.0), value[ROWS:], jnp.where(inside, 0.0, first)
                )
                total[plane, pl.ds(top, size + ROWS), wide] += value

    for source, owner in ((kept, here), (arrived, 1 - here)):
        for place in range(count):
            add(sections * place + owner, source, place)
    body = (pl.ds(half, tile_rows), pl.ds(half, tile_cols))
    copy = pltpu.make_async_copy(total.at[(slice(None),) + body], tile, sems.at[0])
    copy.start()
    bands, strips = strips[: len(names)], strips[len(names) :]
    for (down, across), strip in zip(edges, strips):
        rows = span(down, offsets, names, half, body[0])
        cols = span(across, offsets, names, half, body[1])
        for plane in range(2):
            strip[plane] = total[plane, rows, cols].astype(bf16)
    for (rows, cols), band in zip(band_places(names, folds, half, bands, tile_cols), bands):
        rows = pl.ds(pl.multiple_of(rows.start + half, half), rows.size)
        cols = pl.ds(pl.multiple_of(cols.start + half, half), cols.size)
        band[...] = total[:, rows, cols]
    for (down, acrosses), strip in zip(corner_keys(names), strips[len(edges) :]):
        rows = span(down, offsets, names, half, None)
        for k, across in enumerate(acrosses):
            cols = span(across, offsets, names, half, None)
            for plane in range(2):
                strip[plane, k] = total[plane, rows, cols].astype(bf16)
    copy.wait()


def band_shapes(names, tile_rows, tile_cols, half):
    tall = tile_rows - half * sum(key[0] == "row" for key in names)
    return [(2, half, tile_cols) if key[0] == "row" else (2, tall, half) for key in names]


def band_places(names, folds, half, bands, tile_cols):
    result = []
    for k, (key, band) in enumerate(zip(names, bands)):
        own = pl.ds(pl.multiple_of(folds[k], half), half)
        if key[0] == "row":
            result.append((own, pl.ds(0, tile_cols)))
        else:
            first = pl.multiple_of(folds[len(names)], half)
            result.append((pl.ds(first, band.shape[1]), own))
    return result


def corner_keys(names):
    acrosses = [key for key in names if key[0] == "col"]
    return [(key, acrosses) for key in names if key[0] == "row" and acrosses]


def scatter(places, occupied, offsets, folds, kept, arrived, edges, names, tile_rows, tile_cols):
    count, _, size, _ = kept.shape
    half = size // 2
    corners = corner_keys(names)
    vmem = pl.BlockSpec(memory_space=pltpu.VMEM)
    return pl.pallas_call(
        functools.partial(scatter_kernel, edges, names, half),
        in_specs=[SMEM, SMEM, SMEM, SMEM, vmem, vmem],
        out_specs=[HBM] + [vmem] * (len(names) + len(edges) + len(corners)),
        out_shape=[jax.ShapeDtypeStruct((2, tile_rows, tile_cols), f32)]
        + [jax.ShapeDtypeStruct(x, f32) for x in band_shapes(names, tile_rows, tile_cols, half)]
        + strip_shapes(edges, tile_rows, tile_cols, half)
        + [jax.ShapeDtypeStruct((2, len(keys), half, half), bf16) for _, keys in corners],
        scratch_shapes=[
            pltpu.VMEM((2, tile_rows + 2 * half, tile_cols + 2 * half), f32),
            pltpu.SemaphoreType.DMA((1,)),
        ],
        compiler_params=pltpu.CompilerParams(vmem_limit_bytes=20 * MIB),
        cost_estimate=pl.CostEstimate(
            flops=0, bytes_accessed=16 * tile_rows * tile_cols, transcendentals=0
        ),
        name="scatter",
    )(places, occupied, offsets, folds, kept, arrived)


def corner_kernel(names, half, offsets, *refs):
    corners = corner_keys(names)
    arrived, refs = refs[: len(corners)], refs[len(corners) :]
    ins, outs = refs[: len(refs) // 2], refs[len(refs) // 2 :]
    for k, (before, strip) in enumerate(zip(ins, outs)):
        strip[...] = before[...]
        for (down, _), block in zip(corners, arrived):
            rows = span(down, offsets, names, half, None)
            for plane in range(2):
                strip[plane, rows, :] = (
                    strip[plane, rows, :].astype(f32) + block[plane, k].astype(f32)
                ).astype(bf16)


def add_corners(offsets, strips, arrived, names, half):
    vmem = pl.BlockSpec(memory_space=pltpu.VMEM)
    return pl.pallas_call(
        functools.partial(corner_kernel, names, half),
        in_specs=[SMEM] + [vmem] * (len(arrived) + len(strips)),
        out_specs=[vmem] * len(strips),
        out_shape=[jax.ShapeDtypeStruct(strip.shape, bf16) for strip in strips],
        compiler_params=pltpu.CompilerParams(vmem_limit_bytes=8 * MIB),
        name="corners",
    )(offsets, *arrived, *strips)


def border_kernel(edges, names, half, folds, tile_in, part, other, *rest):
    bands, rest = rest[: len(names)], rest[len(names) :]
    strips, rest = rest[: len(edges)], rest[len(edges) :]
    tile, probe_share, sems = rest[0], rest[1], rest[-1]
    sums = rest[2:-1]
    strips = dict(zip(edges, strips))
    tile_cols = tile.shape[2]
    regions = band_places(names, folds, half, bands, tile_cols)
    copies = []
    for k, (key, (rows, cols)) in enumerate(zip(names, regions)):
        for plane in range(2):
            block = sums[k]
            if key[0] == "row":
                block[plane] = bands[k][plane] + strips[(key, None)][plane].astype(f32)
                for j, across in enumerate(names):
                    if across[0] == "col":
                        wide = pl.ds(pl.multiple_of(folds[j], half), half)
                        block[plane, :, wide] += strips[(None, across)][plane, rows, :].astype(f32)
            else:
                block[plane] = bands[k][plane] + strips[(None, key)][plane, rows, :].astype(f32)
            copies.append(
                pltpu.make_async_copy(
                    block.at[plane], tile.at[plane, rows, cols], sems.at[len(copies)]
                )
            )
            copies[-1].start()
    probe_share[...] = part[...].astype(f32) + other[...].astype(f32)
    for copy in copies:
        copy.wait()


def add_borders(folds, tile, bands, probe_parts, edges, names, strips, half):
    vmem = pl.BlockSpec(memory_space=pltpu.VMEM)
    return pl.pallas_call(
        functools.partial(border_kernel, edges, names, half),
        in_specs=[SMEM, HBM] + [vmem] * (2 + len(bands) + len(strips)),
        out_specs=[HBM, vmem],
        out_shape=[
            jax.ShapeDtypeStruct(tile.shape, f32),
            jax.ShapeDtypeStruct(probe_parts[0].shape, f32),
        ],
        scratch_shapes=[
            *(pltpu.VMEM(band.shape, f32) for band in bands),
            pltpu.SemaphoreType.DMA((max(2 * len(bands), 1),)),
        ],
        input_output_aliases={1: 0},
        compiler_params=pltpu.CompilerParams(vmem_limit_bytes=12 * MIB),
        name="borders",
    )(folds, tile, *probe_parts, *bands, *strips)


def partner(index, kind):
    return index ^ 1 if kind == 0 else ((index + 1) ^ 1) - 1


def route(edge, rows, cols):
    down, across = edge
    pairs = []
    for r in range(rows):
        to_row = partner(r, down[1]) if down else r
        for c in range(cols):
            to_col = partner(c, across[1]) if across else c
            if 0 <= to_row < rows and 0 <= to_col < cols:
                pairs.append((r * cols + c, to_row * cols + to_col))
    return pairs


def shards(probe, object_re, object_im, phases, centres, occupied, measured):
    size = probe.shape[1]
    half = size // 2
    rows, cols = lax.axis_size("row"), lax.axis_size("col")
    sections = lax.axis_size("depth")
    assert sections == 2 and object_re.shape[0] == 1
    here = lax.axis_index("depth").astype(jnp.int32)
    row_at = lax.axis_index("row").astype(jnp.int32)
    tile_rows, tile_cols = object_re.shape[1:]
    batches, slots = centres.shape[2:4]
    spots = batches * slots
    count = spots // sections

    places = centres.reshape(2 * spots)
    live_counts = occupied.reshape(batches)
    frames = measured.reshape(count, sections, size, size)

    names, tile_at, padded_at = [], [], []
    for axis, extent, own, length in (
        ("row", rows, row_at, tile_rows),
        ("col", cols, lax.axis_index("col").astype(jnp.int32), tile_cols),
    ):
        for kind in range(min(2, extent - 1)):
            forward = own % 2 == kind
            names.append((axis, kind))
            tile_at.append(jnp.where(forward, length - half, 0))
            padded_at.append(jnp.where(forward, length + half, 0))
    downs = [key for key in names if key[0] == "row"]
    acrosses = [key for key in names if key[0] == "col"]
    edges = [(key, None) for key in downs] + [(None, key) for key in acrosses]
    outer, paths = edges, [route(edge, rows, cols) for edge in edges]
    edges = edges + [(down, across) for down in downs for across in acrosses]
    paths += [route(edge, rows, cols) for edge in edges[len(outer) :]]
    both = ("row", "col")

    def numbers(*values):
        return jnp.stack(values).astype(jnp.int32)

    padded_at = numbers(*padded_at, here)
    tile_at = numbers(*tile_at, here)
    if rows == 2:
        first_row = jnp.where(row_at == 0, 0, half)
    else:
        first_row = jnp.int32(half if downs else 0)
    fold_at = numbers(*(tile_at[k] for k in range(len(names))), first_row)
    own = pack(tile_at, object_re, object_im, edges, names, half)
    strips = [lax.ppermute(strip, both, path) for strip, path in zip(own, paths)]
    kern, sorted_frames, waves = prepare(places, padded_at, own[0], probe, phases, frames)
    mine, other = gather(
        places, padded_at, object_re, object_im, waves, edges, names, strips, size
    )
    across_depth = [(i, 1 - i) for i in range(sections)]
    theirs = lax.ppermute(other, "depth", across_depth)
    keep, send, own_rows, other_rows = chain(
        places, live_counts, padded_at, kern, mine, theirs, sorted_frames, waves, count
    )
    arrived = lax.ppermute(send, "depth", across_depth)

    assert rows & (rows - 1) == 0 and cols & (cols - 1) == 0
    tiles = rows * cols
    flips = [1 << k for k in range(cols.bit_length() - 1)]
    flips = flips[:1] + flips[1:][-1:] + flips[1:-1]
    flips = [cols << k for k in range(rows.bit_length() - 1)] + flips

    def fetched(block, flip):
        pairs = [(i, i ^ flip) for i in range(sections * tiles)]
        return lax.ppermute(block, ("depth",) + both, pairs)

    def exchange(block, flip):
        own = block.astype(bf16)
        return own, fetched(own, flip)

    def summed(pair):
        return pair[0].astype(f32) + pair[1].astype(f32)

    parts = [own_rows, fetched(other_rows, tiles)]
    if flips:
        parts += [fetched(own_rows, flips[0]), fetched(other_rows, tiles ^ flips[0])]

    tile, *own = scatter(
        places, live_counts, padded_at, fold_at, keep, arrived, outer, names, tile_rows, tile_cols
    )
    bands, own = own[: len(names)], own[len(names) :]
    own, corners = own[: len(outer)], own[len(outer) :]
    parts, own, corners = lax.optimization_barrier((parts, own, corners))
    pair = parts[0].astype(f32), parts[1].astype(f32)
    if flips:
        pair = summed(parts[::2]), summed(parts[1::2])
    if corners:
        corners = [lax.ppermute(x, both, path) for x, path in zip(corners, paths)]
    if flips[1:]:
        pair = exchange(summed(pair), flips[1])
    if corners:
        pair, corners, own = lax.optimization_barrier((pair, corners, own))
        own[len(downs) :] = add_corners(tile_at, own[len(downs) :], corners, names, half)
    added = [lax.ppermute(strip, both, path) for strip, path in zip(own, paths)]
    for flip in flips[2:]:
        pair = exchange(summed(pair), flip)
    gradient, probe_share = add_borders(fold_at, tile, bands, pair, outer, names, added, half)
    return (gradient[:, None], probe_share)


def solution(mesh):
    in_specs = (
        P(),
        P("depth", "row", "col"),
        P("depth", "row", "col"),
        P(),
        P("row", "col", None, None, None),
        P("row", "col", None),
        P("row", "col", None, None, None, None),
    )
    out_specs = (P(None, "depth", "row", "col"), P(None, "depth", None))
    return jax.shard_map(shards, mesh=mesh, in_specs=in_specs, out_specs=out_specs, check_vma=False)
```

```python
import functools

import jax
import jax.numpy as jnp
import numpy as np
from jax import lax
from jax.experimental import pallas as pl
from jax.experimental.pallas import tpu as pltpu
from jax.sharding import PartitionSpec as P

f32 = jnp.float32
bf16 = jnp.bfloat16
ROWS = 16
LANES = 128
ANY = pl.BlockSpec(memory_space=pl.ANY)
HBM = pl.BlockSpec(memory_space=pltpu.HBM)
SMEM = pl.BlockSpec(memory_space=pltpu.SMEM)
MIB = 1024 * 1024


def dft_tables(size):
    half = size // 2
    rows = np.arange(half)[:, None]
    cols = np.arange(half)[None, :]

    def packed(turns):
        angle = -2.0 * np.pi * (turns % size) / size
        re, im = np.cos(angle) / np.sqrt(size), np.sin(angle) / np.sqrt(size)
        return np.block([[re, im], [-im, re]])

    even, odd = packed(rows * 2 * cols), packed(rows * (2 * cols + 1))
    full = np.stack([even, odd, even.T, odd.T]).astype(np.float32)
    high = full.astype(jnp.bfloat16)
    low = (full - high.astype(np.float32)).astype(jnp.bfloat16)
    return np.stack([high, low], axis=1)


def split(x):
    high = x.astype(bf16)
    return high, (x - high.astype(f32)).astype(bf16)


def dot3(left, right):
    lhs = jnp.concatenate([left[0], left[0], left[1]], axis=1)
    rhs = jnp.concatenate([right[0], right[1], right[0]], axis=0)
    return jnp.dot(lhs, rhs, preferred_element_type=f32)


def dot(left, right):
    if len(left) == 2 and len(right) == 2:
        return dot3(left, right)
    lhs = left if len(left) == 2 else left * 2
    rhs = right if len(right) == 2 else right * 2
    return jnp.dot(cols_of(*lhs), rows_of(*rhs), preferred_element_type=f32)


def rows_of(*parts):
    return jnp.concatenate(parts, axis=0)


def cols_of(*parts):
    return jnp.concatenate(parts, axis=1)


def set_order(order):
    size = order.shape[0]
    half = size // 2
    source = lax.broadcasted_iota(jnp.int32, (size, size), 0)
    target = lax.broadcasted_iota(jnp.int32, (size, size), 1)
    chosen = source == 2 * (target % half) + target // half
    order[...] = jnp.where(chosen, 1.0, 0.0).astype(bf16)


def in_order(parts, at, order):
    half = order.shape[0] // 2
    ids = [at + (pl.ds(start, half, stride=2), slice(None)) for start in range(2)]
    rows = rows_of(*(cols_of(*(part[i] for part in parts)) for i in ids))
    first, rest = split(rows)
    second, third = split(rows - first.astype(f32))
    table = order[...]
    return jnp.dot(
        cols_of(first, second, third), rows_of(table, table, table), preferred_element_type=f32
    )


def wave_kernel(places, offsets, after, probe, *refs):
    step = pl.program_id(0)
    phases, (kern, waves, order) = refs[:-3], refs[-3:]

    @pl.when(step == 0)
    def _():
        set_order(order)
        angles = in_order(phases, (), order)
        kern[0] = jnp.cos(angles)
        kern[1] = jnp.sin(angles)

    at = 2 * step + offsets[offsets.shape[0] - 1]
    down = places[2 * at] % ROWS
    across = places[2 * at + 1] % LANES
    for plane in range(2):
        moved = pltpu.roll(probe[plane], across, axis=1)
        waves[0, plane] = pltpu.roll(moved, down, axis=0)


def frame_kernel(offsets, after, *refs):
    frames, (sorted_frames, order) = refs[:-2], refs[-2:]

    @pl.when(pl.program_id(0) == 0)
    def _():
        set_order(order)

    sorted_frames[0] = in_order(frames, (0, 0), order)


def shifted_waves(places, offsets, after, probe, phases, count):
    size = phases.shape[-1]
    blocks = size // LANES
    full = lambda *shape: pl.BlockSpec(shape, lambda i, p, o: (0,) * len(shape))
    return pl.pallas_call(
        wave_kernel,
        grid_spec=pltpu.PrefetchScalarGridSpec(
            num_scalar_prefetch=2,
            grid=(count,),
            in_specs=[
                ANY,
                full(2, size, size),
                *(
                    pl.BlockSpec((size, LANES), lambda i, p, o, b=b: (0, b))
                    for b in range(blocks)
                ),
            ],
            out_specs=[
                full(2, size, size),
                pl.BlockSpec((1, 2, size, size), lambda i, p, o: (i, 0, 0, 0)),
            ],
            scratch_shapes=[pltpu.VMEM((size, size), bf16)],
        ),
        out_shape=[
            jax.ShapeDtypeStruct((2, size, size), f32),
            jax.ShapeDtypeStruct((count, 2, size, size), f32),
        ],
        compiler_params=pltpu.CompilerParams(vmem_limit_bytes=16 * MIB),
        cost_estimate=pl.CostEstimate(flops=0, bytes_accessed=0, transcendentals=0),
        name="waves",
    )(places, offsets, after, probe, *[phases] * blocks)


def sorted_intensities(offsets, after, frames):
    count, sections, size = frames.shape[:3]
    blocks = size // LANES
    last = offsets.shape[0] - 1
    return pl.pallas_call(
        frame_kernel,
        grid_spec=pltpu.PrefetchScalarGridSpec(
            num_scalar_prefetch=1,
            grid=(count,),
            in_specs=[
                ANY,
                *(
                    pl.BlockSpec((1, 1, size, LANES), lambda i, o, b=b: (i, o[last], 0, b))
                    for b in range(blocks)
                ),
            ],
            out_specs=pl.BlockSpec((1, size, size), lambda i, o: (i, 0, 0)),
            scratch_shapes=[pltpu.VMEM((size, size), bf16)],
        ),
        out_shape=jax.ShapeDtypeStruct((count, size, size), f32),
        compiler_params=pltpu.CompilerParams(vmem_limit_bytes=16 * MIB),
        cost_estimate=pl.CostEstimate(flops=0, bytes_accessed=0, transcendentals=0),
        name="frames",
    )(offsets, after, *[frames] * blocks)


def span(key, offsets, names, half, whole):
    if key is None:
        return whole
    return pl.ds(pl.multiple_of(offsets[names.index(key)], half), half)


def pack_kernel(edges, names, half, offsets, tile_re, tile_im, *rest):
    strips, sems = rest[:-1], rest[-1]
    tile_rows, tile_cols = tile_re.shape[1:]
    copies = []
    for (down, across), strip in zip(edges, strips):
        rows = span(down, offsets, names, half, pl.ds(0, tile_rows))
        cols = span(across, offsets, names, half, pl.ds(0, tile_cols))
        for plane, tile in enumerate((tile_re, tile_im)):
            copies.append(
                pltpu.make_async_copy(
                    tile.at[0, rows, cols], strip.at[plane], sems.at[len(copies)]
                )
            )
            copies[-1].start()
    for copy in copies:
        copy.wait()


def strip_shapes(edges, tile_rows, tile_cols, half):
    return [
        jax.ShapeDtypeStruct(
            (2, half if down else tile_rows, half if across else tile_cols), bf16
        )
        for down, across in edges
    ]


def pack(offsets, tile_re, tile_im, edges, names, half):
    return pl.pallas_call(
        functools.partial(pack_kernel, edges, names, half),
        in_specs=[SMEM, HBM, HBM],
        out_specs=[ANY] * len(edges),
        out_shape=strip_shapes(edges, *tile_re.shape[1:], half),
        scratch_shapes=[pltpu.SemaphoreType.DMA((2 * len(edges),))],
        compiler_params=pltpu.CompilerParams(vmem_limit_bytes=4 * MIB),
        name="pack",
    )(offsets, tile_re, tile_im)


def spot(places, at):
    row, col = places[2 * at], places[2 * at + 1]
    down, across = row % ROWS, col % LANES
    return down, across, pl.multiple_of(row - down, ROWS), pl.multiple_of(col - across, LANES)


def is_live(occupied, places, at):
    slots = places.shape[0] // 2 // occupied.shape[0]
    return at % slots < occupied[at // slots]


def gather_kernel(spots, edges, names, half, places, offsets, tile_re, tile_im, after, *rest):
    strips, (mine, other, padded, sems) = rest[:-4], rest[-4:]
    tile_rows, tile_cols = tile_re.shape[1:]
    size = mine.shape[-1]
    body = (pl.ds(half, tile_rows), pl.ds(half, tile_cols))
    copies = []

    def bring(source, target):
        copies.append(pltpu.make_async_copy(source, target, sems.at[len(copies)]))
        copies[-1].start()

    bring(tile_re.at[0], padded.at[(0,) + body])
    bring(tile_im.at[0], padded.at[(1,) + body])
    for (down, across), strip in zip(edges, strips):
        rows = span(down, offsets, names, half, body[0])
        cols = span(across, offsets, names, half, body[1])
        bring(strip, padded.at[:, rows, cols])
    for copy in copies:
        copy.wait()

    sections = 2
    lane = lax.broadcasted_iota(jnp.int32, (size, LANES), 1)
    top_lane = lax.broadcasted_iota(jnp.int32, (ROWS, LANES), 1)
    top_row = lax.broadcasted_iota(jnp.int32, (ROWS, size), 0)
    here = offsets[offsets.shape[0] - 1]

    def cut(at, target, place):
        down, across, top, left = spot(places, at)
        inner = size - LANES
        rest = pl.ds(pl.multiple_of(top + ROWS, ROWS), size - ROWS)

        def cols(start, width):
            return pl.ds(pl.multiple_of(left + start, LANES), width)

        for plane in range(2):
            target[place, plane, ROWS:, LANES:] = padded[plane, rest, cols(LANES, inner)]
            near = padded[plane, rest, cols(0, LANES)].astype(f32)
            far = padded[plane, rest, cols(size, LANES)].astype(f32)
            target[place, plane, ROWS:, :LANES] = jnp.where(
                lane[ROWS:] < across, far, near
            ).astype(bf16)
            rows = []
            for start in (0, size):
                block = padded[
                    plane, pl.ds(pl.multiple_of(top + start, ROWS), ROWS), cols(0, size + LANES)
                ].astype(f32)
                first = jnp.where(top_lane < across, block[:, size:], block[:, :LANES])
                rows.append(cols_of(first, block[:, LANES:size]))
            target[place, plane, :ROWS, :] = jnp.where(top_row < down, rows[1], rows[0]).astype(
                bf16
            )

    for place in range(spots // sections):
        cut(sections * place + 1 - here, other, place)
        cut(sections * place + here, mine, place)


def gather(places, offsets, tile_re, tile_im, after, edges, names, strips, size):
    half = size // 2
    spots = places.shape[0] // 2
    tile_rows, tile_cols = tile_re.shape[1:]
    shape = jax.ShapeDtypeStruct((spots // 2, 2, size, size), bf16)
    vmem = pl.BlockSpec(memory_space=pltpu.VMEM)
    return pl.pallas_call(
        functools.partial(gather_kernel, spots, edges, names, half),
        in_specs=[SMEM, SMEM, HBM, HBM] + [ANY] * (1 + len(strips)),
        out_specs=[vmem, vmem],
        out_shape=[shape, shape],
        scratch_shapes=[
            pltpu.VMEM((2, tile_rows + 2 * half, tile_cols + 2 * half), bf16),
            pltpu.SemaphoreType.DMA((2 + len(strips),)),
        ],
        compiler_params=pltpu.CompilerParams(vmem_limit_bytes=16 * MIB),
        name="gather",
    )(places, offsets, tile_re, tile_im, after, *strips)


def chain_kernel(
    group, places, occupied, offsets, tables, kern, mine, theirs, frames, waves,
    keep, send, pulled_keep, pulled_send, windows, middle, terms, pulled, sems,
):
    step = pl.program_id(0)
    steps = pl.num_programs(0)
    size = kern.shape[-1]
    half = size // 2
    me = offsets[offsets.shape[0] - 1]

    def fetch(at, which):
        source, slot = ((mine, me), (theirs, 1 - me))[which]
        rows = pl.ds(at * group, group)
        return pltpu.make_async_copy(
            source.at[rows], windows.at[at, slot], sems.at[2 * at + which]
        )

    @pl.when(step == 0)
    def _():
        for at in range(windows.shape[0]):
            fetch(at, 0).start()
            fetch(at, 1).start()
        pulled[...] = jnp.zeros_like(pulled)

    fetch(step, 0).wait()
    fetch(step, 1).wait()

    def table(which):
        return tables[which, 0], tables[which, 1]

    group_ids = range(group)

    def forward(waves, cut):
        halves = []
        for sign, which in ((1, 2), (-1, 3)):
            parts = []
            for pair in waves:
                if sign > 0:
                    parts.append(rows_of(*(x[:half] + x[half:] for x in pair)))
                else:
                    parts.append(rows_of(*(x[:half] - x[half:] for x in pair)))
            halves.append(dot(table(which), cut(cols_of(*parts))))
        outs = []
        for sign, which in ((1, 0), (-1, 1)):
            parts = []
            for at in group_ids:
                for out in halves:
                    x = out[:, at * size : (at + 1) * size]
                    if sign > 0:
                        x = x[:, :half] + x[:, half:]
                    else:
                        x = x[:, :half] - x[:, half:]
                    parts.append(cols_of(x[:half], x[half:]))
            outs.append(dot(cut(rows_of(*parts)), table(which)))
        return [[out[at * size : (at + 1) * size] for out in outs] for at in group_ids]

    def inverse(parts, cut):
        first = dot(cut(rows_of(*(part[0] for part in parts))), table(2))
        second = dot(cut(rows_of(*(part[1] for part in parts))), table(3))
        evens, odds = [], []
        for at in group_ids:
            rows = slice(at * size, (at + 1) * size)
            plus, minus = first[rows] + second[rows], first[rows] - second[rows]
            re = cols_of(plus[:, :half], minus[:, :half])
            im = cols_of(plus[:, half:], minus[:, half:])
            evens.append(rows_of(re[:half], im[:half]))
            odds.append(rows_of(re[half:], im[half:]))
        first = dot(table(0), cut(cols_of(*evens)))
        second = dot(table(1), cut(cols_of(*odds)))
        outs = []
        for at in group_ids:
            cols = slice(at * size, (at + 1) * size)
            plus, minus = first[:, cols] + second[:, cols], first[:, cols] - second[:, cols]
            outs.append((rows_of(plus[:half], minus[:half]), rows_of(plus[half:], minus[half:])))
        return outs

    def propagate(waves, sign, cut):
        kept = []
        for parts in forward(waves, cut):
            outs = []
            for k, part in enumerate(parts):
                cols = slice(k * half, (k + 1) * half)
                kre, kim = kern[0, :, cols], kern[1, :, cols] * sign
                re, im = part[:, :half], part[:, half:]
                outs.append(cols_of(re * kre - im * kim, re * kim + im * kre))
            kept.append(outs)
        return inverse(kept, cut)

    def product(left, right):
        return left[0] * right[0] - left[1] * right[1], left[0] * right[1] + left[1] * right[0]

    def conj_product(left, right):
        return left[0] * right[0] + left[1] * right[1], left[0] * right[1] - left[1] * right[0]

    def rounded(x):
        return x.astype(bf16).astype(f32)

    def window(slot, at):
        return windows[step, slot, at, 0].astype(f32), windows[step, slot, at, 1].astype(f32)

    def wave(at):
        return waves[at, 0], waves[at, 1]

    def passed(at):
        return middle[at, 0].astype(f32), middle[at, 1].astype(f32)

    outs = propagate([product(wave(at), window(0, at)) for at in group_ids], 1.0, split)
    for at in group_ids:
        middle[at, 0] = outs[at][0].astype(bf16)
        middle[at, 1] = outs[at][1].astype(bf16)

    far = forward([product(passed(at), window(1, at)) for at in group_ids], split)
    for at in group_ids:
        for k, part in enumerate(far[at]):
            re, im = part[:, :half], part[:, half:]
            misfit = re * re + im * im - frames[at, :, k * half : (k + 1) * half]
            far[at][k] = cols_of(re * misfit, im * misfit)
    pulls = []
    for at, chi in enumerate(inverse(far, split)):
        terms[1, at, 0], terms[1, at, 1] = conj_product(passed(at), chi)
        pulls.append(conj_product(window(1, at), chi))

    for at, chi in enumerate(propagate(pulls, -1.0, lambda x: (x.astype(bf16),))):
        chi = rounded(chi[0]), rounded(chi[1])
        terms[0, at, 0], terms[0, at, 1] = conj_product(wave(at), chi)
        spot_at = 2 * (step * group + at) + me
        up = (size - places[2 * spot_at] % ROWS) % size
        back_by = (size - places[2 * spot_at + 1] % LANES) % size
        weight = is_live(occupied, places, spot_at).astype(f32)
        for plane, value in enumerate(conj_product(window(0, at), chi)):
            value = pltpu.roll(pltpu.roll(value * weight, back_by, axis=1), up, axis=0)
            pulled[plane] += value

    keep[...] = terms[me].astype(bf16)
    send[...] = terms[1 - me].astype(bf16)

    @pl.when(step == steps - 1)
    def _():
        share = pulled_keep.shape[1]
        for out, owner in ((pulled_keep, me), (pulled_send, 1 - me)):
            rows = pl.ds(pl.multiple_of(owner * share, share), share)
            out[...] = pulled[:, rows, :].astype(bf16)


def chain(places, occupied, offsets, kern, mine, theirs, frames, waves, group):
    count, size = waves.shape[0], waves.shape[-1]
    full = lambda *shape: pl.BlockSpec(shape, lambda i: (0,) * len(shape))
    block = pl.BlockSpec((group, 2, size, size), lambda i: (i, 0, 0, 0))
    return pl.pallas_call(
        functools.partial(chain_kernel, group),
        grid=(count // group,),
        in_specs=[
            SMEM,
            SMEM,
            SMEM,
            full(4, 2, size, size),
            full(2, size, size),
            ANY,
            ANY,
            pl.BlockSpec((group, size, size), lambda i: (i, 0, 0)),
            block,
        ],
        out_specs=[block, block, full(2, size // 2, size), full(2, size // 2, size)],
        out_shape=[
            jax.ShapeDtypeStruct((count, 2, size, size), bf16),
            jax.ShapeDtypeStruct((count, 2, size, size), bf16),
            jax.ShapeDtypeStruct((2, size // 2, size), bf16),
            jax.ShapeDtypeStruct((2, size // 2, size), bf16),
        ],
        scratch_shapes=[
            pltpu.VMEM((count // group, 2, group, 2, size, size), bf16),
            pltpu.VMEM((group, 2, size, size), bf16),
            pltpu.VMEM((2, group, 2, size, size), f32),
            pltpu.VMEM((2, size, size), f32),
            pltpu.SemaphoreType.DMA((2 * (count // group),)),
        ],
        compiler_params=pltpu.CompilerParams(vmem_limit_bytes=40 * MIB),
        name="chain",
    )(places, occupied, offsets, jnp.asarray(dft_tables(size)), kern, mine, theirs, frames, waves)


def scatter_kernel(edges, names, half, places, occupied, offsets, folds, kept, arrived, tile, *rest):
    strips, (total, sems) = rest[:-2], rest[-2:]
    count, size = kept.shape[0], kept.shape[-1]
    tile_rows, tile_cols = tile.shape[1:]
    sections = 2
    here = offsets[offsets.shape[0] - 1]

    total[...] = jnp.zeros_like(total)
    lane = lax.broadcasted_iota(jnp.int32, (size, LANES), 1)
    row = lax.broadcasted_iota(jnp.int32, (ROWS, size + LANES), 0)

    def add(at, source, place):
        down, across, top, left = spot(places, at)
        wide = pl.ds(left, size + LANES)

        @pl.when(is_live(occupied, places, at))
        def _():
            for plane in range(2):
                value = source[place, plane].astype(f32)
                first = value[:, :LANES]
                inside = lane >= across
                value = cols_of(
                    jnp.where(inside, first, 0.0), value[:, LANES:], jnp.where(inside, 0.0, first)
                )
                first = value[:ROWS]
                inside = row >= down
                value = rows_of(
                    jnp.where(inside, first, 0.0), value[ROWS:], jnp.where(inside, 0.0, first)
                )
                total[plane, pl.ds(top, size + ROWS), wide] += value

    for source, owner in ((kept, here), (arrived, 1 - here)):
        for place in range(count):
            add(sections * place + owner, source, place)
    body = (pl.ds(half, tile_rows), pl.ds(half, tile_cols))
    copy = pltpu.make_async_copy(total.at[(slice(None),) + body], tile, sems.at[0])
    copy.start()
    bands, strips = strips[: len(names)], strips[len(names) :]
    for (down, across), strip in zip(edges, strips):
        rows = span(down, offsets, names, half, body[0])
        cols = span(across, offsets, names, half, body[1])
        for plane in range(2):
            strip[plane] = total[plane, rows, cols].astype(bf16)
    for (rows, cols), band in zip(band_places(names, folds, half, bands, tile_cols), bands):
        rows = pl.ds(pl.multiple_of(rows.start + half, half), rows.size)
        cols = pl.ds(pl.multiple_of(cols.start + half, half), cols.size)
        band[...] = total[:, rows, cols]
    for (down, acrosses), strip in zip(corner_keys(names), strips[len(edges) :]):
        rows = span(down, offsets, names, half, None)
        for k, across in enumerate(acrosses):
            cols = span(across, offsets, names, half, None)
            for plane in range(2):
                strip[plane, k] = total[plane, rows, cols].astype(bf16)
    copy.wait()


def band_shapes(names, tile_rows, tile_cols, half):
    tall = tile_rows - half * sum(key[0] == "row" for key in names)
    return [(2, half, tile_cols) if key[0] == "row" else (2, tall, half) for key in names]


def band_places(names, folds, half, bands, tile_cols):
    result = []
    for k, (key, band) in enumerate(zip(names, bands)):
        own = pl.ds(pl.multiple_of(folds[k], half), half)
        if key[0] == "row":
            result.append((own, pl.ds(0, tile_cols)))
        else:
            first = pl.multiple_of(folds[len(names)], half)
            result.append((pl.ds(first, band.shape[1]), own))
    return result


def corner_keys(names):
    acrosses = [key for key in names if key[0] == "col"]
    return [(key, acrosses) for key in names if key[0] == "row" and acrosses]


def scatter(places, occupied, offsets, folds, kept, arrived, edges, names, tile_rows, tile_cols):
    count, _, size, _ = kept.shape
    half = size // 2
    corners = corner_keys(names)
    vmem = pl.BlockSpec(memory_space=pltpu.VMEM)
    return pl.pallas_call(
        functools.partial(scatter_kernel, edges, names, half),
        in_specs=[SMEM, SMEM, SMEM, SMEM, vmem, vmem],
        out_specs=[HBM] + [vmem] * (len(names) + len(edges) + len(corners)),
        out_shape=[jax.ShapeDtypeStruct((2, tile_rows, tile_cols), f32)]
        + [jax.ShapeDtypeStruct(x, f32) for x in band_shapes(names, tile_rows, tile_cols, half)]
        + strip_shapes(edges, tile_rows, tile_cols, half)
        + [jax.ShapeDtypeStruct((2, len(keys), half, half), bf16) for _, keys in corners],
        scratch_shapes=[
            pltpu.VMEM((2, tile_rows + 2 * half, tile_cols + 2 * half), f32),
            pltpu.SemaphoreType.DMA((1,)),
        ],
        compiler_params=pltpu.CompilerParams(vmem_limit_bytes=20 * MIB),
        cost_estimate=pl.CostEstimate(
            flops=0, bytes_accessed=16 * tile_rows * tile_cols, transcendentals=0
        ),
        name="scatter",
    )(places, occupied, offsets, folds, kept, arrived)


def corner_kernel(names, half, offsets, *refs):
    corners = corner_keys(names)
    arrived, refs = refs[: len(corners)], refs[len(corners) :]
    ins, outs = refs[: len(refs) // 2], refs[len(refs) // 2 :]
    for k, (before, strip) in enumerate(zip(ins, outs)):
        strip[...] = before[...]
        for (down, _), block in zip(corners, arrived):
            rows = span(down, offsets, names, half, None)
            for plane in range(2):
                strip[plane, rows, :] = (
                    strip[plane, rows, :].astype(f32) + block[plane, k].astype(f32)
                ).astype(bf16)


def add_corners(offsets, strips, arrived, names, half):
    vmem = pl.BlockSpec(memory_space=pltpu.VMEM)
    return pl.pallas_call(
        functools.partial(corner_kernel, names, half),
        in_specs=[SMEM] + [vmem] * (len(arrived) + len(strips)),
        out_specs=[vmem] * len(strips),
        out_shape=[jax.ShapeDtypeStruct(strip.shape, bf16) for strip in strips],
        compiler_params=pltpu.CompilerParams(vmem_limit_bytes=8 * MIB),
        name="corners",
    )(offsets, *arrived, *strips)


def border_kernel(edges, names, half, folds, tile_in, part, other, *rest):
    bands, rest = rest[: len(names)], rest[len(names) :]
    strips, rest = rest[: len(edges)], rest[len(edges) :]
    tile, probe_share, sems = rest[0], rest[1], rest[-1]
    sums = rest[2:-1]
    strips = dict(zip(edges, strips))
    tile_cols = tile.shape[2]
    regions = band_places(names, folds, half, bands, tile_cols)
    copies = []
    for k, (key, (rows, cols)) in enumerate(zip(names, regions)):
        for plane in range(2):
            block = sums[k]
            if key[0] == "row":
                block[plane] = bands[k][plane] + strips[(key, None)][plane].astype(f32)
                for j, across in enumerate(names):
                    if across[0] == "col":
                        wide = pl.ds(pl.multiple_of(folds[j], half), half)
                        block[plane, :, wide] += strips[(None, across)][plane, rows, :].astype(f32)
            else:
                block[plane] = bands[k][plane] + strips[(None, key)][plane, rows, :].astype(f32)
            copies.append(
                pltpu.make_async_copy(
                    block.at[plane], tile.at[plane, rows, cols], sems.at[len(copies)]
                )
            )
            copies[-1].start()
    probe_share[...] = part[...].astype(f32) + other[...].astype(f32)
    for copy in copies:
        copy.wait()


def add_borders(folds, tile, bands, probe_parts, edges, names, strips, half):
    vmem = pl.BlockSpec(memory_space=pltpu.VMEM)
    return pl.pallas_call(
        functools.partial(border_kernel, edges, names, half),
        in_specs=[SMEM, HBM] + [vmem] * (2 + len(bands) + len(strips)),
        out_specs=[HBM, vmem],
        out_shape=[
            jax.ShapeDtypeStruct(tile.shape, f32),
            jax.ShapeDtypeStruct(probe_parts[0].shape, f32),
        ],
        scratch_shapes=[
            *(pltpu.VMEM(band.shape, f32) for band in bands),
            pltpu.SemaphoreType.DMA((max(2 * len(bands), 1),)),
        ],
        input_output_aliases={1: 0},
        compiler_params=pltpu.CompilerParams(vmem_limit_bytes=12 * MIB),
        name="borders",
    )(folds, tile, *probe_parts, *bands, *strips)


def partner(index, kind):
    return index ^ 1 if kind == 0 else ((index + 1) ^ 1) - 1


def route(edge, rows, cols):
    down, across = edge
    pairs = []
    for r in range(rows):
        to_row = partner(r, down[1]) if down else r
        for c in range(cols):
            to_col = partner(c, across[1]) if across else c
            if 0 <= to_row < rows and 0 <= to_col < cols:
                pairs.append((r * cols + c, to_row * cols + to_col))
    return pairs


def shards(probe, object_re, object_im, phases, centres, occupied, measured):
    size = probe.shape[1]
    half = size // 2
    rows, cols = lax.axis_size("row"), lax.axis_size("col")
    sections = lax.axis_size("depth")
    assert sections == 2 and object_re.shape[0] == 1
    here = lax.axis_index("depth").astype(jnp.int32)
    row_at = lax.axis_index("row").astype(jnp.int32)
    tile_rows, tile_cols = object_re.shape[1:]
    batches, slots = centres.shape[2:4]
    spots = batches * slots
    count = spots // sections

    places = centres.reshape(2 * spots)
    live_counts = occupied.reshape(batches)
    frames = measured.reshape(count, sections, size, size)

    names, tile_at, padded_at = [], [], []
    for axis, extent, own, length in (
        ("row", rows, row_at, tile_rows),
        ("col", cols, lax.axis_index("col").astype(jnp.int32), tile_cols),
    ):
        for kind in range(min(2, extent - 1)):
            forward = own % 2 == kind
            names.append((axis, kind))
            tile_at.append(jnp.where(forward, length - half, 0))
            padded_at.append(jnp.where(forward, length + half, 0))
    downs = [key for key in names if key[0] == "row"]
    acrosses = [key for key in names if key[0] == "col"]
    edges = [(key, None) for key in downs] + [(None, key) for key in acrosses]
    outer, paths = edges, [route(edge, rows, cols) for edge in edges]
    edges = edges + [(down, across) for down in downs for across in acrosses]
    paths += [route(edge, rows, cols) for edge in edges[len(outer) :]]
    both = ("row", "col")

    def numbers(*values):
        return jnp.stack(values).astype(jnp.int32)

    padded_at = numbers(*padded_at, here)
    tile_at = numbers(*tile_at, here)
    if rows == 2:
        first_row = jnp.where(row_at == 0, 0, half)
    else:
        first_row = jnp.int32(half if downs else 0)
    fold_at = numbers(*(tile_at[k] for k in range(len(names))), first_row)
    own = pack(tile_at, object_re, object_im, edges, names, half)
    strips = [lax.ppermute(strip, both, path) for strip, path in zip(own, paths)]
    kern, waves = shifted_waves(places, padded_at, own[0], probe, phases, count)
    mine, other = gather(
        places, padded_at, object_re, object_im, waves, edges, names, strips, size
    )
    across_depth = [(i, 1 - i) for i in range(sections)]
    theirs = lax.ppermute(other, "depth", across_depth)
    sorted_frames = sorted_intensities(padded_at, mine, frames)
    keep, send, own_rows, other_rows = chain(
        places, live_counts, padded_at, kern, mine, theirs, sorted_frames, waves, count
    )
    arrived = lax.ppermute(send, "depth", across_depth)

    assert rows & (rows - 1) == 0 and cols & (cols - 1) == 0
    tiles = rows * cols
    flips = [1 << k for k in range(cols.bit_length() - 1)]
    flips = flips[:1] + flips[1:][-1:] + flips[1:-1]
    flips = [cols << k for k in range(rows.bit_length() - 1)] + flips

    def fetched(block, flip):
        pairs = [(i, i ^ flip) for i in range(sections * tiles)]
        return lax.ppermute(block, ("depth",) + both, pairs)

    def exchange(block, flip):
        own = block.astype(bf16)
        return own, fetched(own, flip)

    def summed(pair):
        return pair[0].astype(f32) + pair[1].astype(f32)

    parts = [own_rows, fetched(other_rows, tiles)]
    if flips:
        parts += [fetched(own_rows, flips[0]), fetched(other_rows, tiles ^ flips[0])]

    tile, *own = scatter(
        places, live_counts, padded_at, fold_at, keep, arrived, outer, names, tile_rows, tile_cols
    )
    bands, own = own[: len(names)], own[len(names) :]
    own, corners = own[: len(outer)], own[len(outer) :]
    parts, own, corners = lax.optimization_barrier((parts, own, corners))
    pair = parts[0].astype(f32), parts[1].astype(f32)
    if flips:
        pair = summed(parts[::2]), summed(parts[1::2])
    if corners:
        corners = [lax.ppermute(x, both, path) for x, path in zip(corners, paths)]
    if flips[1:]:
        pair = exchange(summed(pair), flips[1])
    if corners:
        pair, corners, own = lax.optimization_barrier((pair, corners, own))
        own[len(downs) :] = add_corners(tile_at, own[len(downs) :], corners, names, half)
    added = [lax.ppermute(strip, both, path) for strip, path in zip(own, paths)]
    for flip in flips[2:]:
        pair = exchange(summed(pair), flip)
    gradient, probe_share = add_borders(fold_at, tile, bands, pair, outer, names, added, half)
    return (gradient[:, None], probe_share)


def solution(mesh):
    in_specs = (
        P(),
        P("depth", "row", "col"),
        P("depth", "row", "col"),
        P(),
        P("row", "col", None, None, None),
        P("row", "col", None),
        P("row", "col", None, None, None, None),
    )
    out_specs = (P(None, "depth", "row", "col"), P(None, "depth", None))
    return jax.shard_map(shards, mesh=mesh, in_specs=in_specs, out_specs=out_specs, check_vma=False)
```
